128 devices in a mesh: gauss: 64 (over z, x, y), view: 2 (over core).
Axes of the slice: x: 4, y: 4, z: 4, core: 2. Of those that a mesh axis runs over, the one named last changes fastest.
Arguments:
- gauss_rows: float32 [64, 2097152], P(None, 'gauss')
- vis_shard: int32 [4096, 512, 1], P(('gauss', 'view')), may hold values from 0 to 63; in each aligned block of 16384 rows (0 to 16383, 16384 to 32767, ..., all dimensions but the last counted through in order) at most 512 rows name the same one
- vis_row: int32 [4096, 512], P(('gauss', 'view')), may hold values from 0 to 32767
- tile_index: int32 [4096], P(('gauss', 'view')), may hold values from 0 to 65279
- cotangent: float32 [4096, 29, 256], P(('gauss', 'view')), may hold values from -120 to 120
Outputs:
- images: float32 [4096, 29, 256], P(('gauss', 'view'))
- gradient: float32 [64, 2097152], P(None, ('gauss', 'view'))
The draws below stay inside these ranges and needn't reach their ends.
Inputs may be any that keep to these rules, and one draw needn't show every extreme that they name: `vis_shard`: within the lists of one device (aligned blocks of 16384 entries, tiles in order) no shard is named more than 512 times, a bound that some block reaches.
All inputs are finite; a program needn't handle non-finite values.
Results may differ from the reference program's by a relative error of at most 0.0003.
Values sent between devices are 32-bit elements; how exact they have to be, the bound alone decides.
A program may use at most 128 MiB of HBM per device.

```python
import math
import jax
import jax.numpy as jnp
import numpy as np
from jax import lax

ROW = 64
CHANNELS = 29
TILE_SIDE = 16
PIXELS = 256
VIEWS = 8
SCREEN_TILES = 8160
G_DEV = 32768
TILES_DEV = 32
LIST = 512
CAP = 512
NG = 2097152
TILES = 4096
N_GAUSS = 64


def draw_gauss_rows(key, part):
    key = jax.random.fold_in(key, 11)
    keys = jax.random.split(key, 6)
    centre = jax.random.uniform(keys[0], (2, NG), jnp.float32, 0.0, 16.0)
    log_a = jax.random.uniform(keys[1], (1, NG), jnp.float32, -4.1, -1.4)
    skew_term = jax.random.uniform(keys[2], (1, NG), jnp.float32, -2.0, 2.0)
    log_c = jax.random.uniform(keys[3], (1, NG), jnp.float32, -4.1, -1.4)
    opacity = jax.random.uniform(keys[4], (1, NG), jnp.float32, -7.0, -3.0)
    features = 8.0 * jax.random.normal(keys[5], (ROW - 6, NG), jnp.float32)
    return jnp.concatenate([centre, log_a, skew_term, log_c, opacity, features], axis=0).astype(jnp.float32)


def with_ends(drawn, own_key, smallest, largest):
    spot = [jax.random.randint(jax.random.fold_in(own_key, axis), (), 0, length) for axis, length in enumerate(drawn.shape)]
    widest = drawn.shape.index(max(drawn.shape))
    beside = spot[:widest] + [(spot[widest] + 1) % drawn.shape[widest]] + spot[widest + 1:]
    return drawn.at[tuple(spot)].set(smallest).at[tuple(beside)].set(largest)


def steps_of(rng, shape, cuts, least, top_value):
    level, own = 1.0, jax.random.fold_in(rng, 6)
    for position, parts in cuts:
        draws = jnp.exp(jax.random.uniform(jax.random.fold_in(own, position), (parts,), jnp.float32, least / len(cuts), top_value / len(cuts)))
        level = level * jnp.repeat(draws, shape[position] // parts).reshape([-1 if axis == position else 1 for axis in range(len(shape))])
    return level


def deal_out(stream_key, own, number, rows, amount, top, most, slope):
    order = jax.random.permutation(stream_key, amount)
    crowded, usual = portions_of(amount, rows * top, most, slope, True), portions_of(amount, rows * top, most, slope, False)
    places = jnp.arange(amount)

    def named(lengths, offset_by):
        used = int((lengths > 0).sum())
        fixed = max(1, used // 4)
        passed = fixed + (places - fixed + offset_by * (used - fixed)) % max(1, amount - fixed)
        return jnp.zeros((amount,), jnp.int32).at[order[jnp.where(places < fixed, places, passed)]].set(jnp.asarray(lengths, jnp.int32))

    lengths = jnp.where(number % 4 == 0, named(crowded, number // 4), named(usual, number - number // 4 - 1))
    mixed = jax.random.permutation(jax.random.fold_in(own, 3), amount)
    giver, sink = mixed[0:amount // 2 * 2:2], mixed[1:amount // 2 * 2:2]
    margin = jnp.minimum(lengths[giver] - 1, most - lengths[sink]) // 2
    margin = jnp.where((giver == order[0]) | (sink == order[0]) | (lengths[sink] == 0), 0, jnp.maximum(margin, 0))
    passed = jax.random.randint(jax.random.fold_in(own, 4), (amount // 2,), 0, 1 << 20) % (margin + 1)
    lengths = lengths.at[giver].add(-passed).at[sink].add(passed)
    labels = jnp.searchsorted(jnp.cumsum(lengths), jnp.arange(rows * top), side="right").astype(jnp.int32)
    grid = labels.reshape(top, rows).T
    grid = grid[jax.random.permutation(jax.random.fold_in(own, 1), rows)]
    offset_by = jax.random.randint(jax.random.fold_in(own, 2), (rows, 1), 0, top)
    return jnp.take_along_axis(grid, (jnp.arange(top)[None, :] + offset_by) % top, axis=1)


def portions_of(amount, total, most, skew, full):
    loads = [(1 << 20) // math.isqrt(grade ** skew) + 1 for grade in range(1, amount + 1)]
    largest = most if full else min(most, max(-(-total // amount), total * loads[0] // sum(loads)))
    least = 1 if total - largest >= amount - 1 else 0
    holding, surplus = [largest] + [least] * (amount - 1), total - largest - least * (amount - 1)
    while surplus > 0:
        free = [i for i in range(1, amount) if holding[i] < largest] or [i for i in range(1, amount) if holding[i] < most]
        pool, remaining = sum([loads[i] for i in free]), surplus
        for i in free:
            extra = min(most - holding[i], max(1, remaining * loads[i] // pool), surplus)
            holding[i] = holding[i] + extra
            surplus = surplus - extra
    return np.array(holding)


def noise(rng, extent, scale, most, cuts=(), dtype=jnp.bfloat16):
    array = jax.random.normal(rng, extent, jnp.float32) * scale
    if len(cuts) > 0:
        array = steps_of(rng, extent, cuts, -0.22, 0.18) * array
    return jnp.clip(array, min=-most, max=most).astype(dtype)


def setup_inputs(seed: int = 0) -> dict:
    splits = jax.random.split(jax.random.key(seed), 6)
    gauss_rows = draw_gauss_rows(jax.random.fold_in(splits[5], 71), 0)
    vis_shard_keys = jax.random.split(jax.random.fold_in(splits[1], 1), TILES * LIST // (TILES_DEV * LIST))
    vis_shard_turns = jax.random.permutation(jax.random.fold_in(splits[1], 3), TILES * LIST // (TILES_DEV * LIST))
    vis_shard = jax.vmap(lambda own, number: deal_out(jax.random.fold_in(splits[1], 2), own, number, TILES_DEV * LIST, N_GAUSS, 1, CAP, 2))(vis_shard_keys, vis_shard_turns).reshape((TILES, LIST, 1))
    vis_row = with_ends(jax.random.randint(splits[2], (TILES, LIST), 0, G_DEV), jax.random.fold_in(splits[2], 1), 0, G_DEV - 1).astype(jnp.int32)
    tile_index = with_ends(jax.random.randint(splits[3], (TILES,), 0, VIEWS * SCREEN_TILES), jax.random.fold_in(splits[3], 1), 0, (VIEWS * SCREEN_TILES) - 1).astype(jnp.int32)
    cotangent = noise(splits[4], (TILES, CHANNELS, PIXELS), 20.0, 120.0, ((0, 128),), jnp.float32)
    return {"gauss_rows": gauss_rows, "vis_shard": vis_shard, "vis_row": vis_row, "tile_index": tile_index, "cotangent": cotangent}


TWO_PI = 6.283185307179586

def composite(rows, view_cos, cotangent):
    pixel = jnp.arange(PIXELS)
    across = (pixel % TILE_SIDE).astype(jnp.float32) + 0.5
    down = (pixel // TILE_SIDE).astype(jnp.float32) + 0.5

    def render(params):
        off_x = across[None, :] - params[0][:, None]
        off_y = down[None, :] - params[1][:, None]
        conic_a = jnp.exp(params[2])
        conic_c = jnp.exp(params[4])
        conic_b = 0.9 * jnp.tanh(params[3]) * jnp.sqrt(conic_a * conic_c)
        power = -0.5 * (conic_a[:, None] * off_x * off_x + 2.0 * conic_b[:, None] * off_x * off_y + conic_c[:, None] * off_y * off_y)
        alpha = 0.99 * jax.nn.sigmoid(params[5])[:, None] * jnp.exp(power)
        logs = jnp.log(1.0 - alpha)
        before = jnp.cumsum(logs, axis=0) - logs
        weight = jnp.exp(before) * alpha
        colour = params[6:6 + CHANNELS] + view_cos * params[6 + CHANNELS:6 + 2 * CHANNELS]
        return jnp.dot(colour, weight, precision=lax.Precision.HIGHEST)
    image, pull = jax.vjp(render, rows)
    grads = pull(cotangent)
    return (image, grads[0])

def reference(gauss_rows, vis_shard, vis_row, tile_index, cotangent):
    index = (vis_shard[:, :, 0] * G_DEV + vis_row).astype(jnp.int32)
    view_cos = jnp.cos(TWO_PI * (tile_index // SCREEN_TILES).astype(jnp.float32) / VIEWS)

    def one_tile(packed):
        columns, cosine, cot = packed
        rows = jnp.take(gauss_rows, columns, axis=1)
        return composite(rows, cosine, cot)
    images, grads = lax.map(one_tile, (index, view_cos, cotangent), batch_size=16)
    flat = jnp.transpose(grads, (1, 0, 2)).reshape(ROW, TILES * LIST)
    gradient = jnp.zeros_like(gauss_rows).at[:, index.reshape(-1)].add(flat)
    return (images, gradient)
```

```python
import functools

import jax
import jax.numpy as jnp
from jax import lax
from jax.experimental import pallas as pl
from jax.experimental.pallas import tpu as pltpu
from jax.sharding import PartitionSpec as P

CHANNELS = 29
TILE_SIDE = 16
PIXELS = 256
VIEWS = 8
SCREEN_TILES = 8160
GEOM = 6
WIRE = 40
TWO_PI = 6.283185307179586
LOG2E = 1.4426950408889634
VMEM = pltpu.VMEM
SMEM = pltpu.SMEM
F32 = jnp.float32
BF16 = jnp.bfloat16
I32 = jnp.int32
ROWS = 32
GROUP = 16


def params():
    return pltpu.CompilerParams(vmem_limit_bytes=60 * 2**20)


def whole(space):
    return pl.BlockSpec(memory_space=space)


def iota(shape, dim):
    return lax.broadcasted_iota(I32, shape, dim)


def dot(a, b, contract=((1,), (0,))):
    return lax.dot_general(a, b, (contract, ((), ())), preferred_element_type=F32)


def split(x):
    high = x.astype(BF16).astype(F32)
    return high, x - high


def route_kernel(shard_ref, row_ref, view_ref, ask_row_ref, ask_view_ref, valid_ref, slot_ref):
    shards, capacity = ask_row_ref.shape
    chunks, width = shard_ref.shape
    before = (iota((width, width), 0) < iota((width, width), 1)).astype(F32).astype(BF16)
    spare = iota((shards, capacity), 1)

    def step(i, state):
        carry, total = state
        shard = shard_ref[pl.ds(i, 1), :]
        row = row_ref[pl.ds(i, 1), :]
        view = view_ref[pl.ds(i, 1), :]
        named = iota((shards, width), 0) == shard
        hot = named.astype(F32)
        seen = dot(hot.astype(BF16), before) + carry
        place = jnp.sum(hot * seen, axis=0, keepdims=True).astype(I32)
        slot_ref[pl.ds(i, 1), :] = shard * capacity + place
        at = (iota((capacity, width), 0) == place).astype(F32).astype(BF16)
        low = (row & 255).astype(F32)
        high = (row >> 8).astype(F32)
        values = jnp.concatenate([hot * low, hot * high, hot * view.astype(F32), hot], axis=0)
        total = total + dot(values.astype(BF16), at, ((1,), (1,)))
        return carry + jnp.sum(hot, axis=1, keepdims=True), total

    def pair(i, state):
        for u in range(4):
            state = step(4 * i + u, state)
        return state

    start = (jnp.zeros((shards, 1), F32), jnp.zeros((4 * shards, capacity), F32))
    _, total = lax.fori_loop(0, chunks // 4, pair, start)
    low, high, view, valid = (total[shards * k : shards * (k + 1)].astype(I32) for k in range(4))
    ask_row_ref[...] = jnp.where(valid > 0, low + 256 * high, spare)
    ask_view_ref[...] = view
    valid_ref[...] = valid


def route(shard, row, view, shards, capacity):
    grid = jax.ShapeDtypeStruct((shards, capacity), I32)
    return pl.pallas_call(
        route_kernel,
        out_shape=(grid, grid, grid, jax.ShapeDtypeStruct(shard.shape, I32)),
        in_specs=[whole(VMEM)] * 3,
        out_specs=(whole(VMEM),) * 4,
        compiler_params=params(),
        name="route",
    )(shard, row, view)


def fetch_kernel(ask_ref, ask_vec_ref, cos_ref, rows_ref, out_ref, clash_ref, table, got):
    source = pl.program_id(0)
    width, columns = rows_ref.shape
    capacity = got.shape[0]

    @pl.when(source == 0)
    def _():
        def turn(i, _):
            at = pl.multiple_of(i * capacity, capacity)
            table[pl.ds(at, capacity), 0:width] = rows_ref[:, pl.ds(at, capacity)].T
            return 0

        lax.fori_loop(0, columns // capacity, turn, 0)
        asked = ask_vec_ref[...]
        lane = iota(asked.shape, 1) % GROUP
        same = jnp.zeros(asked.shape, F32)
        for d in range(1, GROUP):
            same = jnp.where((pltpu.roll(asked, d, 1) == asked) & (lane >= d), 1.0, same)
        pool = (iota((capacity, 128), 0) // GROUP == iota((capacity, 128), 1)).astype(F32)
        clash_ref[...] = dot(same.astype(BF16), pool.astype(BF16)).astype(I32)

    def pick(i, _):
        at = pl.multiple_of(i * ROWS, ROWS)
        for u in range(ROWS):
            got[pl.ds(at + u, 1), :] = table[pl.ds(ask_ref[source, at + u], 1), :]
        return 0

    lax.fori_loop(0, capacity // ROWS, pick, 0)
    turned = got[...].T
    second = jnp.concatenate(
        [
            jnp.zeros((GEOM, capacity), F32),
            turned[GEOM + CHANNELS : GEOM + 2 * CHANNELS],
            jnp.zeros((WIRE - GEOM - CHANNELS, capacity), F32),
        ],
        axis=0,
    )
    out_ref[0] = turned[0:WIRE] + cos_ref[0] * second


def fetch(asked, cos, gauss_rows):
    shards, capacity = asked.shape
    width, columns = gauss_rows.shape
    return pl.pallas_call(
        fetch_kernel,
        grid=(shards,),
        out_shape=(
            jax.ShapeDtypeStruct((shards, WIRE, capacity), F32),
            jax.ShapeDtypeStruct((shards, 128), I32),
        ),
        in_specs=[
            whole(SMEM),
            pl.BlockSpec((shards, capacity), lambda i: (0, 0)),
            pl.BlockSpec((1, 1, capacity), lambda i: (i, 0, 0)),
            pl.BlockSpec((width, columns), lambda i: (0, 0), pipeline_mode=pl.Buffered(1)),
        ],
        out_specs=(
            pl.BlockSpec((1, WIRE, capacity), lambda i: (i, 0, 0)),
            pl.BlockSpec((shards, 128), lambda i: (0, 0)),
        ),
        scratch_shapes=[VMEM((columns, 128), F32), VMEM((capacity, 128), F32)],
        compiler_params=params(),
        name="fetch",
    )(asked, asked, cos, gauss_rows)


def composite_kernel(
    slot_ref, wire_ref, valid_ref, cot_ref, images_ref, out_ref,
    table, rows, alpha, ratio, logs, before, weight, weight_hi, weight_lo, pull, parts, after, earlier, later,
):
    shards, _, capacity = wire_ref.shape
    tiles, length = slot_ref.shape
    half = length // 2
    side = TILE_SIDE

    def unpack(s, _):
        at = pl.multiple_of(s * capacity, capacity)
        table[pl.ds(at, capacity), 0:WIRE] = wire_ref[s].T
        return 0

    lax.fori_loop(0, shards, unpack, 0)
    above = iota((2 * half, half), 0) % half
    beside = iota((2 * half, half), 1)
    earlier[...] = (above < beside).astype(F32).astype(BF16)
    later[...] = (above > beside).astype(F32).astype(BF16)

    def put(ref, at, x):
        high, low = split(x)
        high, low = high.astype(BF16), low.astype(BF16)
        ref[pl.ds(at, side), 0:half] = high[:, 0:half]
        ref[pl.ds(at, side), half : 2 * half] = low[:, 0:half]
        ref[pl.ds(at, side), 2 * half : 3 * half] = high[:, half:]
        ref[pl.ds(at, side), 3 * half : 4 * half] = low[:, half:]

    def tile(t, _):
        def pick(i, _):
            at = pl.multiple_of(i * ROWS, ROWS)
            for u in range(ROWS):
                rows[pl.ds(at + u, 1), :] = table[pl.ds(slot_ref[t, at + u], 1), :]
            return 0

        lax.fori_loop(0, length // ROWS, pick, 0)
        turned = rows[...].T
        x0, y0, r2, r3, r4, r5 = (turned[k : k + 1] for k in range(GEOM))
        conic_a = jnp.exp(r2)
        conic_c = jnp.exp(r4)
        skew = jnp.tanh(r3)
        middle = jnp.sqrt(conic_a * conic_c)
        conic_b = 0.9 * skew * middle
        opaque = 1.0 / (1.0 + jnp.exp(-r5))
        spot = iota((side, length), 0).astype(F32) + 0.5
        dx = spot - x0
        dy = spot - y0
        scale = -0.5 * LOG2E
        part_x = (scale * conic_a) * dx * dx
        cross = (2.0 * scale * conic_b) * dx
        part_y = (scale * conic_c) * dy * dy + jnp.log2(0.99 * opaque)

        for py in range(side):
            at = py * side
            a = jnp.exp2(part_x + (cross * dy[py : py + 1] + part_y[py : py + 1]))
            log = jnp.log2(1.0 - a)
            alpha[pl.ds(at, side), :] = a
            ratio[pl.ds(at, side), :] = a * jnp.exp2(-log)
            put(logs, at, log)

        before[:, 0:half] = dot(logs[:, 0 : 2 * half], earlier[...])
        before[:, half:] = dot(logs[:, 2 * half :], earlier[...])

        for py in range(side):
            at = py * side
            b = before[pl.ds(at, side), :]
            last = (
                b[:, half - 1 : half]
                + logs[pl.ds(at, side), half - 1 : half].astype(F32)
                + logs[pl.ds(at, side), 2 * half - 1 : 2 * half].astype(F32)
            )
            b = jnp.concatenate([b[:, 0:half], b[:, half:] + last], axis=1)
            w = jnp.exp2(b) * alpha[pl.ds(at, side), :]
            high, low = split(w)
            weight[pl.ds(at, side), :] = w
            weight_hi[pl.ds(at, side), :] = high.astype(BF16)
            weight_lo[pl.ds(at, side), :] = low.astype(BF16)

        channel = iota((WIRE, length), 0)
        colour = jnp.where((channel >= GEOM) & (channel < GEOM + CHANNELS), turned[0:WIRE], 0.0)
        colour_hi, colour_lo = split(colour)
        cot = cot_ref[t]
        cot_hi, cot_lo = split(cot)
        fill = jnp.zeros((128 - 3 * WIRE, length), F32)
        fill_cot = jnp.zeros((128 - 3 * WIRE, PIXELS), F32)
        both = jnp.concatenate([colour_hi, colour_lo], axis=0).astype(BF16)
        image = dot(both, weight_hi[...], ((1,), (1,)))
        image_lo = dot(both, weight_lo[...], ((1,), (1,)))
        image = image[0:WIRE] + image[WIRE:] + image_lo[0:WIRE]
        images_ref[t] = image[GEOM : GEOM + CHANNELS]
        both = jnp.concatenate([cot_hi, cot_lo], axis=0).astype(BF16)
        grad = dot(both, weight_hi[...])
        grad_lo = dot(both, weight_lo[...])
        grad = grad[0:WIRE] + grad[WIRE:] + grad_lo[0:WIRE]
        three = jnp.concatenate([cot_hi, cot_lo, cot_hi, fill_cot], axis=0).T.astype(BF16)
        other = jnp.concatenate([colour_hi, colour_hi, colour_lo, fill], axis=0).astype(BF16)
        pull[...] = dot(three, other)

        for py in range(side):
            at = py * side
            q = pull[pl.ds(at, side), :] * weight[pl.ds(at, side), :]
            pull[pl.ds(at, side), :] = q
            put(parts, at, q)

        after[:, 0:half] = dot(parts[:, 0 : 2 * half], later[...])
        after[:, half:] = dot(parts[:, 2 * half :], later[...])

        m0 = jnp.zeros((side, length), F32)
        m1 = jnp.zeros((side, length), F32)
        m2 = jnp.zeros((side, length), F32)
        for py in range(side):
            at = py * side
            s = after[pl.ds(at, side), :]
            q = pull[pl.ds(at, side), :]
            first = s[:, half : half + 1] + q[:, half : half + 1]
            s = jnp.concatenate([s[:, 0:half] + first, s[:, half:]], axis=1)
            h = q - s * ratio[pl.ds(at, side), :]
            hy = h * dy[py : py + 1]
            m0 = m0 + h
            m1 = m1 + hy
            m2 = m2 + hy * dy[py : py + 1]

        def total(x):
            return jnp.sum(x, axis=0, keepdims=True)

        m0x = m0 * dx
        s0, sx, sy, sxx, sxy, syy = total(m0), total(m0x), total(m1), total(m0x * dx), total(m1 * dx), total(m2)
        shared = -0.5 * conic_b * sxy
        geometry = (
            conic_a * sx + conic_b * sy,
            conic_b * sx + conic_c * sy,
            shared - 0.5 * conic_a * sxx,
            -0.9 * (1.0 - skew * skew) * middle * sxy,
            shared - 0.5 * conic_c * syy,
            (1.0 - opaque) * s0,
        )
        for k, value in enumerate(geometry):
            grad = jnp.where(channel == k, value, grad)
        rows[:, 0:WIRE] = grad.T

        def give(i, _):
            at = pl.multiple_of(i * ROWS, ROWS)
            for u in range(ROWS):
                table[pl.ds(slot_ref[t, at + u], 1), :] = rows[pl.ds(at + u, 1), :]
            return 0

        lax.fori_loop(0, length // ROWS, give, 0)
        return 0

    lax.fori_loop(0, tiles, tile, 0)

    def pack(s, _):
        at = pl.multiple_of(s * capacity, capacity)
        turned = table[pl.ds(at, capacity), :].T
        out_ref[s] = jnp.where(valid_ref[s] > 0, turned[0:WIRE], 0.0)
        return 0

    lax.fori_loop(0, shards, pack, 0)


def composite(slot, wire, valid, cot):
    shards, _, capacity = wire.shape
    tiles, length = slot.shape
    full = (PIXELS, length)
    return pl.pallas_call(
        composite_kernel,
        out_shape=(
            jax.ShapeDtypeStruct((tiles, CHANNELS, PIXELS), F32),
            jax.ShapeDtypeStruct(wire.shape, F32),
        ),
        in_specs=[whole(SMEM), whole(VMEM), whole(VMEM), whole(VMEM)],
        out_specs=(whole(VMEM), whole(VMEM)),
        scratch_shapes=[
            VMEM((shards * capacity, 128), F32),
            VMEM((length, 128), F32),
            VMEM(full, F32),
            VMEM(full, F32),
            VMEM((PIXELS, 2 * length), BF16),
            VMEM(full, F32),
            VMEM(full, F32),
            VMEM(full, BF16),
            VMEM(full, BF16),
            VMEM(full, F32),
            VMEM((PIXELS, 2 * length), BF16),
            VMEM(full, F32),
            VMEM((length, length // 2), BF16),
            VMEM((length, length // 2), BF16),
        ],
        compiler_params=params(),
        name="composite",
    )(slot, wire, valid, cot)


def collect_kernel(half_ref, ask_ref, clash_ref, cos_ref, wire_ref, keep_ref, send_ref, table, rows):
    source = pl.program_id(0)
    width, half = keep_ref.shape
    capacity = rows.shape[0]

    @pl.when(source == 0)
    def _():
        table[...] = jnp.zeros_like(table)
        rows[...] = jnp.zeros_like(rows)

    back = wire_ref[0]
    scaled = cos_ref[0] * back
    turned = jnp.concatenate([back[0 : GEOM + CHANNELS], scaled[GEOM : GEOM + CHANNELS]], axis=0)
    rows[:, 0:width] = turned.T

    def add(i, _):
        at = pl.multiple_of(i * GROUP, GROUP)

        @pl.when(clash_ref[source, i] == 0)
        def _():
            places = [ask_ref[source, at + u] for u in range(GROUP)]
            sums = [table[pl.ds(r, 1), :] + rows[pl.ds(at + u, 1), :] for u, r in enumerate(places)]
            for r, value in zip(places, sums):
                table[pl.ds(r, 1), :] = value

        @pl.when(clash_ref[source, i] != 0)
        def _():
            for u in range(GROUP):
                table[pl.ds(ask_ref[source, at + u], 1), :] += rows[pl.ds(at + u, 1), :]

        return 0

    lax.fori_loop(0, capacity // GROUP, add, 0)

    @pl.when(source == pl.num_programs(0) - 1)
    def _():
        for ref, base in ((keep_ref, half_ref[0]), (send_ref, half - half_ref[0])):
            def turn(i, _):
                at = pl.multiple_of(i * capacity, capacity)
                there = pl.multiple_of(base + at, capacity)
                ref[:, pl.ds(at, capacity)] = table[pl.ds(there, capacity), :].T[0:width]
                return 0

            lax.fori_loop(0, half // capacity, turn, 0)


def collect(half, asked, clash, cos, wire, width, columns):
    shards, _, capacity = wire.shape
    part = jax.ShapeDtypeStruct((width, columns // 2), F32)
    part_spec = pl.BlockSpec((width, columns // 2), lambda i: (0, 0), pipeline_mode=pl.Buffered(1))
    return pl.pallas_call(
        collect_kernel,
        grid=(shards,),
        out_shape=(part, part),
        in_specs=[
            whole(SMEM),
            whole(SMEM),
            whole(SMEM),
            pl.BlockSpec((1, 1, capacity), lambda i: (i, 0, 0)),
            pl.BlockSpec((1, WIRE, capacity), lambda i: (i, 0, 0)),
        ],
        out_specs=(part_spec, part_spec),
        scratch_shapes=[VMEM((columns, 128), F32), VMEM((capacity, 128), F32)],
        compiler_params=params(),
        name="collect",
    )(half, asked, clash, cos, wire)


def per_device(gauss_rows, vis_shard, vis_row, tile_index, cotangent):
    shards = lax.axis_size("gauss")
    tiles, length = vis_row.shape
    entries = tiles * length
    capacity = 2 * entries // shards
    width, columns = gauss_rows.shape
    view = jnp.broadcast_to((tile_index // SCREEN_TILES)[:, None], (tiles, length))
    chunk = (entries // 256, 256)
    ask_row, ask_view, valid, slot = route(
        vis_shard.reshape(chunk), vis_row.reshape(chunk), view.reshape(chunk), shards, capacity
    )
    requests = jnp.stack([ask_row, ask_view], axis=1)
    asked = lax.all_to_all(requests, "gauss", split_axis=0, concat_axis=0, tiled=True)
    asked_row = asked[:, 0]
    cos = jnp.cos(TWO_PI * asked[:, 1:2].astype(F32) / VIEWS)
    fetched, clash = fetch(asked_row, cos, gauss_rows)
    sent = lax.all_to_all(fetched, "gauss", split_axis=0, concat_axis=0, tiled=True)
    cot = jnp.pad(cotangent, ((0, 0), (GEOM, WIRE - GEOM - CHANNELS), (0, 0)))
    images, outgoing = composite(
        slot.reshape(tiles, length), sent, valid.reshape(shards, 1, capacity), cot
    )
    returned = lax.all_to_all(outgoing, "gauss", split_axis=0, concat_axis=0, tiled=True)
    half = (lax.axis_index("view") * (columns // 2)).astype(I32).reshape(1)
    keep, send = collect(half, asked_row, clash, cos, returned, width, columns)
    other = lax.ppermute(send, "view", [(0, 1), (1, 0)])
    return (images, keep + other)


def solution(mesh):
    placed = (
        P(None, "gauss"),
        P(("gauss", "view"), None, None),
        P(("gauss", "view"), None),
        P(("gauss", "view")),
        P(("gauss", "view"), None, None),
    )
    return jax.shard_map(
        per_device,
        mesh=mesh,
        in_specs=placed,
        out_specs=(P(("gauss", "view"), None, None), P(None, ("gauss", "view"))),
        check_vma=False,
    )
```

```python
import functools

import jax
import jax.numpy as jnp
from jax import lax
from jax.experimental import pallas as pl
from jax.experimental.pallas import tpu as pltpu
from jax.sharding import PartitionSpec as P

CHANNELS = 29
TILE_SIDE = 16
PIXELS = 256
VIEWS = 8
SCREEN_TILES = 8160
GEOM = 6
WIRE = 40
TWO_PI = 6.283185307179586
LOG2E = 1.4426950408889634
VMEM = pltpu.VMEM
SMEM = pltpu.SMEM
F32 = jnp.float32
BF16 = jnp.bfloat16
I32 = jnp.int32
ROWS = 32
GROUP = 16
BLOCK = 128


def params(**more):
    return pltpu.CompilerParams(vmem_limit_bytes=60 * 2**20, **more)


def whole(space):
    return pl.BlockSpec(memory_space=space)


def iota(shape, dim):
    return lax.broadcasted_iota(I32, shape, dim)


def dot(a, b, contract=((1,), (0,))):
    return lax.dot_general(a, b, (contract, ((), ())), preferred_element_type=F32)


def split(x):
    high = x.astype(BF16).astype(F32)
    return high, x - high


def route_kernel(shard_ref, row_ref, view_ref, ask_ref, valid_ref, entry_ref, slot_ref):
    shards, _, capacity = ask_ref.shape
    chunks, width = shard_ref.shape
    step = 4
    before = (iota((width, width), 0) < iota((width, width), 1)).astype(F32).astype(BF16)
    spare = iota((shards, capacity), 1)
    lane = iota((1, width), 1).astype(F32)

    def some(i, state):
        carry, total = state
        shard = [shard_ref[pl.ds(step * i + u, 1), :] for u in range(step)]
        hot = [(iota((shards, width), 0) == shard[u]).astype(F32) for u in range(step)]
        seen = dot(jnp.concatenate(hot, axis=0).astype(BF16), before)
        at, values = [], []
        for u in range(step):
            here = step * i + u
            place = jnp.sum(hot[u] * (seen[shards * u : shards * (u + 1)] + carry), axis=0, keepdims=True)
            carry = carry + jnp.sum(hot[u], axis=1, keepdims=True)
            place = place.astype(I32)
            slot_ref[pl.ds(here, 1), :] = shard[u] * capacity + place
            at.append((iota((capacity, width), 0) == place).astype(F32).astype(BF16))
            row = row_ref[pl.ds(here, 1), :]
            parts = (
                (row & 255).astype(F32),
                (row >> 8).astype(F32),
                (view_ref[pl.ds(here, 1), :] + 1).astype(F32),
                lane,
                jnp.full((1, width), here, I32).astype(F32),
            )
            values.append(jnp.concatenate([hot[u] * part for part in parts], axis=0).astype(BF16))
        at = jnp.concatenate(at, axis=1)
        values = jnp.concatenate(values, axis=1)
        return carry, total + dot(values, at, ((1,), (1,)))

    start = (jnp.zeros((shards, 1), F32), jnp.zeros((5 * shards, capacity), F32))
    _, total = lax.fori_loop(0, chunks // step, some, start)
    low, high, view, lane, chunk = (total[shards * k : shards * (k + 1)].astype(I32) for k in range(5))
    valid = view > 0
    ask_ref[:, 0, :] = jnp.where(valid, low + 256 * high, spare)
    ask_ref[:, 1, :] = jnp.where(valid, view - 1, 0)
    valid_ref[...] = valid.astype(I32)
    entry_ref[...] = lane + width * chunk


def route(shard, row, view, shards, capacity):
    grid = jax.ShapeDtypeStruct((shards, capacity), I32)
    return pl.pallas_call(
        route_kernel,
        out_shape=(
            jax.ShapeDtypeStruct((shards, 2, capacity), I32),
            grid,
            grid,
            jax.ShapeDtypeStruct(shard.shape, I32),
        ),
        in_specs=[whole(VMEM)] * 3,
        out_specs=(whole(VMEM),) * 4,
        compiler_params=params(),
        name="route",
    )(shard, row, view)


def exchange(pick, finish, table, even, odd, send, out_ref, send_sem, recv_sem, own_sem, ready):
    shards, _, capacity = send.shape
    blocks = capacity // BLOCK
    me = lax.axis_index("gauss")

    def other(k):
        return lax.rem(me + k + shards, shards)

    def copy(to, by):
        return pltpu.make_async_remote_copy(
            src_ref=send.at[to],
            dst_ref=out_ref.at[by],
            send_sem=send_sem.at[to],
            recv_sem=recv_sem.at[by],
            device_id={"gauss": to},
            device_id_type=pl.DeviceIdType.MESH,
        )

    own = pltpu.make_async_copy(send.at[me], out_ref.at[me], own_sem)
    ready()

    def one(k, _):
        to, last = other(k), other(k - 1)
        for c in range(blocks):
            now, past = (even, odd) if c % 2 == 0 else (odd, even)
            where, part = (to, c - 1) if c else (last, blocks - 1)
            finish(past, where, part)
            for u in range(BLOCK):
                now[u : u + 1, :] = table[pl.ds(pick(to, c * BLOCK + u), 1), :]
            if c == 0:

                @pl.when(k == 1)
                def _():
                    own.start()

                @pl.when(k > 1)
                def _():
                    copy(last, me).start()

        return 0

    lax.fori_loop(0, shards, one, 0)
    last = other(-1)
    finish(odd, last, blocks - 1)
    copy(last, me).start()
    own.wait()

    def end(k, _):
        copy(other(k), me).wait_send()
        copy(me, other(-k)).wait_recv()
        return 0

    lax.fori_loop(1, shards, end, 0)


def greet():
    shards = lax.axis_size("gauss")
    me = lax.axis_index("gauss")
    barrier = pltpu.get_barrier_semaphore()

    def hail(k, _):
        pl.semaphore_signal(
            barrier, inc=1, device_id={"gauss": lax.rem(me + k, shards)}, device_id_type=pl.DeviceIdType.MESH
        )
        return 0

    lax.fori_loop(1, shards, hail, 0)

    def wait():
        pl.semaphore_wait(barrier, shards - 1)

    return wait


def exchange_scratch(shards, capacity):
    return [
        VMEM((BLOCK, 128), F32),
        VMEM((BLOCK, 128), F32),
        VMEM((shards, WIRE, capacity), F32),
        pltpu.SemaphoreType.DMA((shards,)),
        pltpu.SemaphoreType.DMA((shards,)),
        pltpu.SemaphoreType.DMA,
    ]


def fetch_kernel(
    ask_ref, ask_vec_ref, cos_ref, rows_ref, out_ref, clash_ref, table, even, odd, send, send_sem, recv_sem, own_sem
):
    width, columns = rows_ref.shape
    shards, _, capacity = send.shape
    wait = greet()

    def turn(i, _):
        at = pl.multiple_of(i * 512, 512)
        table[pl.ds(at, 512), 0:width] = rows_ref[:, pl.ds(at, 512)].T
        return 0

    lax.fori_loop(0, columns // 512, turn, 0)
    asked = ask_vec_ref[...]
    lane = iota(asked.shape, 1) % GROUP
    same = jnp.zeros(asked.shape, F32)
    for d in range(1, GROUP):
        same = jnp.where((pltpu.roll(asked, d, 1) == asked) & (lane >= d), 1.0, same)
    pool = (iota((capacity, 128), 0) // BLOCK == iota((capacity, 128), 1)).astype(F32)
    clash_ref[...] = dot(same.astype(BF16), pool.astype(BF16)).astype(I32)

    def pick(to, slot):
        return ask_ref[to * capacity + slot]

    def finish(rows, to, part):
        turned = rows[...].T
        second = jnp.concatenate(
            [
                jnp.zeros((GEOM, BLOCK), F32),
                turned[GEOM + CHANNELS : GEOM + 2 * CHANNELS],
                jnp.zeros((WIRE - GEOM - CHANNELS, BLOCK), F32),
            ],
            axis=0,
        )
        lanes = slice(part * BLOCK, (part + 1) * BLOCK)
        send[to, :, lanes] = turned[0:WIRE] + cos_ref[to, :, lanes] * second

    exchange(pick, finish, table, even, odd, send, out_ref, send_sem, recv_sem, own_sem, wait)


def fetch(asked, cos, gauss_rows):
    shards, capacity = asked.shape
    width, columns = gauss_rows.shape
    return pl.pallas_call(
        fetch_kernel,
        out_shape=(
            jax.ShapeDtypeStruct((shards, WIRE, capacity), F32),
            jax.ShapeDtypeStruct((shards, 128), I32),
        ),
        in_specs=[whole(SMEM), whole(VMEM), whole(VMEM), whole(VMEM)],
        out_specs=(whole(pl.ANY), whole(VMEM)),
        scratch_shapes=[VMEM((columns, 128), F32)] + exchange_scratch(shards, capacity),
        compiler_params=params(collective_id=0, has_side_effects=True),
        name="fetch",
    )(asked.reshape(-1), asked, cos, gauss_rows)


def send_back_kernel(
    entry_ref, valid_ref, grads_ref, out_ref, even, odd, send, send_sem, recv_sem, own_sem
):
    capacity = send.shape[2]
    wait = greet()

    def pick(to, slot):
        return entry_ref[to * capacity + slot]

    def finish(rows, to, part):
        lanes = slice(part * BLOCK, (part + 1) * BLOCK)
        send[to, :, lanes] = jnp.where(valid_ref[to, :, lanes] > 0, rows[...].T[0:WIRE], 0.0)

    exchange(pick, finish, grads_ref, even, odd, send, out_ref, send_sem, recv_sem, own_sem, wait)


def send_back(entry, valid, grads):
    shards, _, capacity = valid.shape
    return pl.pallas_call(
        send_back_kernel,
        out_shape=jax.ShapeDtypeStruct((shards, WIRE, capacity), F32),
        in_specs=[whole(SMEM), whole(VMEM), whole(VMEM)],
        out_specs=whole(pl.ANY),
        scratch_shapes=exchange_scratch(shards, capacity),
        compiler_params=params(collective_id=1, has_side_effects=True),
        name="send_back",
    )(entry, valid, grads)


def composite_kernel(
    slot_ref, wire_ref, cot_ref, images_ref, out_ref,
    table, rows, alpha, ratio, logs, before, weight, weight_hi, weight_lo, pull, parts, after, earlier, later,
):
    t = pl.program_id(0)
    shards, _, capacity = wire_ref.shape
    length = rows.shape[0]
    half = length // 2
    side = TILE_SIDE

    @pl.when(t == 0)
    def _():
        def unpack(s, _):
            at = pl.multiple_of(s * capacity, capacity)
            table[pl.ds(at, capacity), 0:WIRE] = wire_ref[s].T
            return 0

        lax.fori_loop(0, shards, unpack, 0)
        above = iota((2 * half, half), 0) % half
        beside = iota((2 * half, half), 1)
        earlier[...] = (above < beside).astype(F32).astype(BF16)
        later[...] = (above > beside).astype(F32).astype(BF16)

    def put(ref, at, x):
        high, low = split(x)
        high, low = high.astype(BF16), low.astype(BF16)
        ref[pl.ds(at, side), 0:half] = high[:, 0:half]
        ref[pl.ds(at, side), half : 2 * half] = low[:, 0:half]
        ref[pl.ds(at, side), 2 * half : 3 * half] = high[:, half:]
        ref[pl.ds(at, side), 3 * half : 4 * half] = low[:, half:]

    def pick(i, _):
        at = pl.multiple_of(i * ROWS, ROWS)
        for u in range(ROWS):
            rows[pl.ds(at + u, 1), :] = table[pl.ds(slot_ref[t * length + at + u], 1), :]
        return 0

    lax.fori_loop(0, length // ROWS, pick, 0)
    turned = rows[...].T
    x0, y0, r2, r3, r4, r5 = (turned[k : k + 1] for k in range(GEOM))
    conic_a = jnp.exp(r2)
    conic_c = jnp.exp(r4)
    skew = jnp.tanh(r3)
    middle = jnp.sqrt(conic_a * conic_c)
    conic_b = 0.9 * skew * middle
    opaque = 1.0 / (1.0 + jnp.exp(-r5))
    spot = iota((side, length), 0).astype(F32) + 0.5
    dx = spot - x0
    dy = spot - y0
    scale = -0.5 * LOG2E
    part_x = (scale * conic_a) * dx * dx
    cross = (2.0 * scale * conic_b) * dx
    part_y = (scale * conic_c) * dy * dy + jnp.log2(0.99 * opaque)

    for py in range(side):
        at = py * side
        a = jnp.exp2(part_x + (cross * dy[py : py + 1] + part_y[py : py + 1]))
        log = jnp.log2(1.0 - a)
        alpha[pl.ds(at, side), :] = a
        ratio[pl.ds(at, side), :] = a * jnp.exp2(-log)
        put(logs, at, log)

    before[:, 0:half] = dot(logs[:, 0 : 2 * half], earlier[...])
    before[:, half:] = dot(logs[:, 2 * half :], earlier[...])

    for py in range(side):
        at = py * side
        b = before[pl.ds(at, side), :]
        last = (
            b[:, half - 1 : half]
            + logs[pl.ds(at, side), half - 1 : half].astype(F32)
            + logs[pl.ds(at, side), 2 * half - 1 : 2 * half].astype(F32)
        )
        b = jnp.concatenate([b[:, 0:half], b[:, half:] + last], axis=1)
        w = jnp.exp2(b) * alpha[pl.ds(at, side), :]
        high, low = split(w)
        weight[pl.ds(at, side), :] = w
        weight_hi[pl.ds(at, side), :] = high.astype(BF16)
        weight_lo[pl.ds(at, side), :] = low.astype(BF16)

    channel = iota((WIRE, length), 0)
    colour = jnp.where((channel >= GEOM) & (channel < GEOM + CHANNELS), turned[0:WIRE], 0.0)
    colour_hi, colour_lo = split(colour)
    cot = cot_ref[0]
    cot_hi, cot_lo = split(cot)
    fill = jnp.zeros((128 - 3 * WIRE, length), F32)
    fill_cot = jnp.zeros((128 - 3 * WIRE, PIXELS), F32)
    both = jnp.concatenate([colour_hi, colour_lo], axis=0).astype(BF16)
    image = dot(both, weight_hi[...], ((1,), (1,)))
    image_lo = dot(both, weight_lo[...], ((1,), (1,)))
    image = image[0:WIRE] + image[WIRE:] + image_lo[0:WIRE]
    images_ref[0] = image[GEOM : GEOM + CHANNELS]
    both = jnp.concatenate([cot_hi, cot_lo], axis=0).astype(BF16)
    grad = dot(both, weight_hi[...])
    grad_lo = dot(both, weight_lo[...])
    grad = grad[0:WIRE] + grad[WIRE:] + grad_lo[0:WIRE]
    three = jnp.concatenate([cot_hi, cot_lo, cot_hi, fill_cot], axis=0).T.astype(BF16)
    other = jnp.concatenate([colour_hi, colour_hi, colour_lo, fill], axis=0).astype(BF16)
    pull[...] = dot(three, other)

    for py in range(side):
        at = py * side
        q = pull[pl.ds(at, side), :] * weight[pl.ds(at, side), :]
        pull[pl.ds(at, side), :] = q
        put(parts, at, q)

    after[:, 0:half] = dot(parts[:, 0 : 2 * half], later[...])
    after[:, half:] = dot(parts[:, 2 * half :], later[...])

    m0 = jnp.zeros((side, length), F32)
    m1 = jnp.zeros((side, length), F32)
    m2 = jnp.zeros((side, length), F32)
    for py in range(side):
        at = py * side
        s = after[pl.ds(at, side), :]
        q = pull[pl.ds(at, side), :]
        first = s[:, half : half + 1] + q[:, half : half + 1]
        s = jnp.concatenate([s[:, 0:half] + first, s[:, half:]], axis=1)
        h = q - s * ratio[pl.ds(at, side), :]
        hy = h * dy[py : py + 1]
        m0 = m0 + h
        m1 = m1 + hy
        m2 = m2 + hy * dy[py : py + 1]

    def total(x):
        return jnp.sum(x, axis=0, keepdims=True)

    m0x = m0 * dx
    s0, sx, sy, sxx, sxy, syy = total(m0), total(m0x), total(m1), total(m0x * dx), total(m1 * dx), total(m2)
    shared = -0.5 * conic_b * sxy
    geometry = (
        conic_a * sx + conic_b * sy,
        conic_b * sx + conic_c * sy,
        shared - 0.5 * conic_a * sxx,
        -0.9 * (1.0 - skew * skew) * middle * sxy,
        shared - 0.5 * conic_c * syy,
        (1.0 - opaque) * s0,
    )
    for k, value in enumerate(geometry):
        grad = jnp.where(channel == k, value, grad)
    out_ref[:, 0:WIRE] = grad.T


def composite(slot, wire, cot):
    shards, _, capacity = wire.shape
    tiles = cot.shape[0]
    length = slot.shape[0] // tiles
    full = (PIXELS, length)
    return pl.pallas_call(
        composite_kernel,
        grid=(tiles,),
        out_shape=(
            jax.ShapeDtypeStruct((tiles, CHANNELS, PIXELS), F32),
            jax.ShapeDtypeStruct((tiles * length, 128), F32),
        ),
        in_specs=[
            whole(SMEM),
            pl.BlockSpec(wire.shape, lambda i: (0, 0, 0), pipeline_mode=pl.Buffered(1)),
            pl.BlockSpec((1, WIRE, PIXELS), lambda i: (i, 0, 0)),
        ],
        out_specs=(
            pl.BlockSpec((1, CHANNELS, PIXELS), lambda i: (i, 0, 0)),
            pl.BlockSpec((length, 128), lambda i: (i, 0)),
        ),
        scratch_shapes=[
            VMEM((shards * capacity, 128), F32),
            VMEM((length, 128), F32),
            VMEM(full, F32),
            VMEM(full, F32),
            VMEM((PIXELS, 2 * length), BF16),
            VMEM(full, F32),
            VMEM(full, F32),
            VMEM(full, BF16),
            VMEM(full, BF16),
            VMEM(full, F32),
            VMEM((PIXELS, 2 * length), BF16),
            VMEM(full, F32),
            VMEM((length, length // 2), BF16),
            VMEM((length, length // 2), BF16),
        ],
        compiler_params=params(),
        name="composite",
    )(slot, wire, cot)


def collect_kernel(half_ref, ask_ref, clash_ref, cos_ref, wire_ref, keep_ref, send_ref, table, even, odd):
    source = pl.program_id(0)
    width, half = keep_ref.shape
    capacity = wire_ref.shape[2]
    blocks = capacity // BLOCK

    @pl.when(source == 0)
    def _():
        table[...] = jnp.zeros_like(table)
        even[...] = jnp.zeros_like(even)
        odd[...] = jnp.zeros_like(odd)

    def turn(c, rows):
        lanes = slice(c * BLOCK, (c + 1) * BLOCK)
        back = wire_ref[0, :, lanes]
        scaled = cos_ref[0, :, lanes] * back
        turned = jnp.concatenate([back[0 : GEOM + CHANNELS], scaled[GEOM : GEOM + CHANNELS]], axis=0)
        rows[:, 0:width] = turned.T

    def add(c, rows):
        base = source * capacity + c * BLOCK
        for first in range(0, BLOCK, GROUP):
            places = [ask_ref[jnp.maximum(base, 0) + first + u] for u in range(GROUP)]
            sums = [table[pl.ds(r, 1), :] + rows[first + u : first + u + 1, :] for u, r in enumerate(places)]
            for r, value in zip(places, sums):
                table[pl.ds(r, 1), :] = value

    def add_slowly(c, rows):
        base = source * capacity + c * BLOCK

        def one(u, _):
            table[pl.ds(ask_ref[jnp.maximum(base, 0) + u], 1), :] += rows[pl.ds(u, 1), :]
            return 0

        lax.fori_loop(0, BLOCK, one, 0)

    def finish(c, rows, more):
        clear = clash_ref[jnp.maximum((source + c // blocks) * 128 + c % blocks, 0)] == 0

        @pl.when(clear)
        def _():
            more()
            add(c, rows)

        @pl.when(jnp.logical_not(clear))
        def _():
            more()
            add_slowly(c, rows)

    for c in range(blocks):
        now, past = (even, odd) if c % 2 == 0 else (odd, even)
        finish(c - 1, past, functools.partial(turn, c, now))

    @pl.when(source == pl.num_programs(0) - 1)
    def _():
        finish(blocks - 1, odd, lambda: None)
        for ref, base in ((keep_ref, half_ref[0]), (send_ref, half - half_ref[0])):

            def back(i, _):
                at = pl.multiple_of(i * capacity, capacity)
                there = pl.multiple_of(base + at, capacity)
                ref[:, pl.ds(at, capacity)] = table[pl.ds(there, capacity), :].T[0:width]
                return 0

            lax.fori_loop(0, half // capacity, back, 0)


def collect(half, asked, clash, cos, wire, width, columns):
    shards, _, capacity = wire.shape
    part = jax.ShapeDtypeStruct((width, columns // 2), F32)
    part_spec = pl.BlockSpec((width, columns // 2), lambda i: (0, 0), pipeline_mode=pl.Buffered(1))
    return pl.pallas_call(
        collect_kernel,
        grid=(shards,),
        out_shape=(part, part),
        in_specs=[
            whole(SMEM),
            whole(SMEM),
            whole(SMEM),
            pl.BlockSpec((1, 1, capacity), lambda i: (i, 0, 0)),
            pl.BlockSpec((1, WIRE, capacity), lambda i: (i, 0, 0)),
        ],
        out_specs=(part_spec, part_spec),
        scratch_shapes=[VMEM((columns, 128), F32), VMEM((BLOCK, 128), F32), VMEM((BLOCK, 128), F32)],
        compiler_params=params(),
        name="collect",
    )(half, asked.reshape(-1), clash.reshape(-1), cos, wire)


def per_device(gauss_rows, vis_shard, vis_row, tile_index, cotangent):
    shards = lax.axis_size("gauss")
    tiles, length = vis_row.shape
    entries = tiles * length
    capacity = 2 * entries // shards
    width, columns = gauss_rows.shape
    view = jnp.broadcast_to((tile_index // SCREEN_TILES)[:, None], (tiles, length))
    chunk = (entries // 256, 256)
    requests, valid, entry, slot = route(
        vis_shard.reshape(chunk), vis_row.reshape(chunk), view.reshape(chunk), shards, capacity
    )
    asked = lax.all_to_all(requests, "gauss", split_axis=0, concat_axis=0, tiled=True)
    asked_row = asked[:, 0]
    cos = jnp.cos(TWO_PI * asked[:, 1:2].astype(F32) / VIEWS)
    fetched, clash = fetch(asked_row, cos, gauss_rows)
    cot = jnp.pad(cotangent, ((0, 0), (GEOM, WIRE - GEOM - CHANNELS), (0, 0)))
    images, grads = composite(slot.reshape(-1), fetched, cot)
    returned = send_back(entry.reshape(-1), valid.reshape(shards, 1, capacity), grads)
    half = (lax.axis_index("view") * (columns // 2)).astype(I32).reshape(1)
    keep, send = collect(half, asked_row, clash, cos, returned, width, columns)
    other = lax.ppermute(send, "view", [(0, 1), (1, 0)])
    return (images, keep + other)


def solution(mesh):
    placed = (
        P(None, "gauss"),
        P(("gauss", "view"), None, None),
        P(("gauss", "view"), None),
        P(("gauss", "view")),
        P(("gauss", "view"), None, None),
    )
    return jax.shard_map(
        per_device,
        mesh=mesh,
        in_specs=placed,
        out_specs=(P(("gauss", "view"), None, None), P(None, ("gauss", "view"))),
        check_vma=False,
    )
```

```python
import functools

import jax
import jax.numpy as jnp
from jax import lax
from jax.experimental import pallas as pl
from jax.experimental.pallas import tpu as pltpu
from jax.sharding import PartitionSpec as P

CHANNELS = 29
TILE_SIDE = 16
PIXELS = 256
VIEWS = 8
SCREEN_TILES = 8160
GEOM = 6
SENT = 35
WIRE = 40
PITCH = 36
TWO_PI = 6.283185307179586
LOG2E = 1.4426950408889634
VMEM = pltpu.VMEM
SMEM = pltpu.SMEM
F32 = jnp.float32
BF16 = jnp.bfloat16
I32 = jnp.int32
GROUP = 8
BLOCK = 128


def params(**more):
    return pltpu.CompilerParams(vmem_limit_bytes=60 * 2**20, **more)


def whole(space):
    return pl.BlockSpec(memory_space=space)


def iota(shape, dim):
    return lax.broadcasted_iota(I32, shape, dim)


def dot(a, b, contract=((1,), (0,))):
    return lax.dot_general(a, b, (contract, ((), ())), preferred_element_type=F32)


def split(x):
    high = x.astype(BF16).astype(F32)
    return high, x - high


def route_kernel(view_ref, shard_ref, row_ref, ask_ref, meta_ref, slot_ref):
    shards = ask_ref.shape[0]
    tiles, length = shard_ref.shape
    width = 256
    parts = length // width
    capacity = 2 * tiles * length // shards
    blocks = capacity // BLOCK
    before = (iota((width, width), 0) < iota((width, width), 1)).astype(F32).astype(BF16)
    lane = iota((1, width), 1).astype(F32)

    def some(i, state):
        carry, total = state
        spots = [(2 * i + u // parts, u % parts) for u in range(2 * parts)]
        shard = [shard_ref[pl.ds(t, 1), h * width : (h + 1) * width] for t, h in spots]
        hot = [(iota((shards, width), 0) == one).astype(F32) for one in shard]
        seen = dot(jnp.concatenate(hot, axis=0).astype(BF16), before)
        at, values = [], []
        for u, (t, h) in enumerate(spots):
            place = jnp.sum(hot[u] * (seen[shards * u : shards * (u + 1)] + carry), axis=0, keepdims=True)
            carry = carry + jnp.sum(hot[u], axis=1, keepdims=True)
            place = place.astype(I32)
            slot = shard[u] * capacity + place
            for b in range(width // BLOCK):
                slot_ref[pl.ds(t * (length // BLOCK) + h * (width // BLOCK) + b, 1), :] = slot[
                    :, b * BLOCK : (b + 1) * BLOCK
                ]
            at.append((iota((capacity, width), 0) == place).astype(F32).astype(BF16))
            row = row_ref[pl.ds(t, 1), h * width : (h + 1) * width]
            parts_of = (
                (row & 255).astype(F32),
                (row >> 8).astype(F32),
                jnp.full((1, width), view_ref[t] + 1, I32).astype(F32),
                lane,
                jnp.full((1, width), t * parts + h, I32).astype(F32),
            )
            values.append(jnp.concatenate([hot[u] * part for part in parts_of], axis=0).astype(BF16))
        at = jnp.concatenate(at, axis=1)
        values = jnp.concatenate(values, axis=1)
        return carry, total + dot(values, at, ((1,), (1,)))

    start = (jnp.zeros((shards, 1), F32), jnp.zeros((5 * shards, capacity), F32))
    _, total = lax.fori_loop(0, tiles // 2, some, start)
    low, high, view, lane, chunk = (total[shards * k : shards * (k + 1)].astype(I32) for k in range(5))
    used = view > 0
    row = jnp.where(used, low + 256 * high, iota((shards, capacity), 1))
    view = jnp.where(used, view - 1, 0)
    entry = lane + width * chunk
    used = used.astype(I32)
    for c in range(blocks):
        lanes = slice(c * BLOCK, (c + 1) * BLOCK)
        ask_ref[:, c, :] = row[:, lanes]
        ask_ref[:, blocks + c, :] = view[:, lanes]
        meta_ref[:, c, :] = entry[:, lanes]
        meta_ref[:, blocks + c, :] = used[:, lanes]


def route(view, shard, row, shards):
    tiles, length = shard.shape
    lists = jax.ShapeDtypeStruct((shards, 8, BLOCK), I32)
    return pl.pallas_call(
        route_kernel,
        out_shape=(lists, lists, jax.ShapeDtypeStruct((tiles * length // BLOCK, BLOCK), I32)),
        in_specs=[whole(SMEM), whole(VMEM), whole(VMEM)],
        out_specs=(whole(VMEM),) * 3,
        compiler_params=params(),
        name="route",
    )(view, shard, row)


def shifted(k, back=False):
    shards = lax.axis_size("gauss")
    side = round(shards ** (1 / 3))
    me = lax.axis_index("gauss")
    step = lax.rem(37 * k, shards)
    sign = 1 - 2 * lax.axis_index("view")
    if back:
        sign = -sign

    def part(x, by):
        return lax.rem(x // by, side)

    def moved(by):
        return lax.rem(part(me, by) + sign * part(step, by) + side, side) * by

    return moved(side * side) + moved(side) + moved(1)


def remote(src, dst, send_sem, recv_sem, to):
    return pltpu.make_async_remote_copy(
        src_ref=src,
        dst_ref=dst,
        send_sem=send_sem,
        recv_sem=recv_sem,
        device_id={"gauss": to},
        device_id_type=pl.DeviceIdType.MESH,
    )


def exchange(ask_ref, finish, table, even, odd, send, out_ref, send_sem, recv_sem, own_sem, ready):
    shards = send.shape[0]
    blocks = send.shape[1] // PITCH
    me = lax.axis_index("gauss")

    def copy(to, by):
        return remote(send.at[to], out_ref.at[by], send_sem.at[to], recv_sem.at[by], to)

    own = pltpu.make_async_copy(send.at[me], out_ref.at[me], own_sem)
    ready()

    def one(k, _):
        to, last = shifted(k), shifted(k + shards - 1)
        for c in range(blocks):
            now, past = (even, odd) if c % 2 == 0 else (odd, even)
            finish(past, *((to, c - 1) if c else (last, blocks - 1)))
            for u in range(BLOCK):
                now[u : u + 1, :] = table[pl.ds(ask_ref[to, c, u], 1), :]
            if c == 0:

                @pl.when(k == 1)
                def _():
                    own.start()

                @pl.when(k > 1)
                def _():
                    copy(last, me).start()

        return 0

    lax.fori_loop(0, shards, one, 0)
    last = shifted(shards - 1)
    finish(odd, last, blocks - 1)
    copy(last, me).start()
    own.wait()

    def end(k, _):
        copy(shifted(k), me).wait_send()
        copy(me, shifted(k, True)).wait_recv()
        return 0

    lax.fori_loop(1, shards, end, 0)


def greet():
    shards = lax.axis_size("gauss")
    me = lax.axis_index("gauss")
    barrier = pltpu.get_barrier_semaphore()

    def hail(k, _):
        pl.semaphore_signal(
            barrier, inc=1, device_id={"gauss": lax.rem(me + k, shards)}, device_id_type=pl.DeviceIdType.MESH
        )
        return 0

    lax.fori_loop(1, shards, hail, 0)

    def wait():
        pl.semaphore_wait(barrier, shards - 1)

    return wait


def exchange_scratch(shards, blocks):
    return [
        VMEM((BLOCK, 128), F32),
        VMEM((BLOCK, 128), F32),
        VMEM((shards, blocks * PITCH, BLOCK), F32),
        pltpu.SemaphoreType.DMA((shards,)),
        pltpu.SemaphoreType.DMA((shards,)),
        pltpu.SemaphoreType.DMA,
    ]


def fetch_kernel(
    cosines_ref, ask_ref, rows_ref, out_ref, asked_ref, cos_ref, clash_ref,
    table, asked, ask_send, ask_recv, ask_own, even, odd, send, send_sem, recv_sem, own_sem,
):
    width, columns = rows_ref.shape
    shards = send.shape[0]
    blocks = send.shape[1] // PITCH
    me = lax.axis_index("gauss")
    greet()()

    def copy(to, by):
        return remote(ask_ref.at[to], asked_ref.at[by], ask_send.at[to], ask_recv.at[by], to)

    def ask(k, _):
        copy(shifted(k), me).start()
        return 0

    lax.fori_loop(1, shards, ask, 0)

    def turn(i, _):
        at = pl.multiple_of(i * 512, 512)
        table[pl.ds(at, 512), 0:width] = rows_ref[:, pl.ds(at, 512)].T
        return 0

    lax.fori_loop(0, columns // 512, turn, 0)
    asked_ref[me] = ask_ref[me]

    def end(k, _):
        copy(shifted(k), me).wait_send()
        copy(me, shifted(k, True)).wait_recv()
        return 0

    lax.fori_loop(1, shards, end, 0)
    down = pltpu.make_async_copy(asked_ref, asked, ask_own)
    down.start()
    for c in range(blocks):
        row = asked_ref[:, c, :]
        view = asked_ref[:, blocks + c, :]
        cos = jnp.full(view.shape, cosines_ref[0], F32)
        for v in range(1, VIEWS):
            cos = jnp.where(view == v, cosines_ref[v], cos)
        cos_ref[:, c, :] = cos
        lane = iota(row.shape, 1) % GROUP
        same = jnp.zeros(row.shape, F32)
        for d in range(1, GROUP):
            same = jnp.where((pltpu.roll(row, d, 1) == row) & (lane >= d), 1.0, same)
        clash_ref[:, c : c + 1] = jnp.max(same, axis=1, keepdims=True).astype(I32)
    down.wait()

    def finish(rows, to, c):
        turned = rows[...].T
        second = jnp.concatenate(
            [jnp.zeros((GEOM, BLOCK), F32), turned[SENT : SENT + CHANNELS]],
            axis=0,
        )
        send[to, c * PITCH : c * PITCH + SENT, :] = turned[0:SENT] + cos_ref[to, c : c + 1, :] * second

    exchange(asked, finish, table, even, odd, send, out_ref, send_sem, recv_sem, own_sem, lambda: None)


def fetch(cosines, ask, gauss_rows):
    shards = ask.shape[0]
    blocks = ask.shape[1] // 2
    width, columns = gauss_rows.shape
    return pl.pallas_call(
        fetch_kernel,
        out_shape=(
            jax.ShapeDtypeStruct((shards, blocks * PITCH, BLOCK), F32),
            jax.ShapeDtypeStruct(ask.shape, I32),
            jax.ShapeDtypeStruct(ask.shape, F32),
            jax.ShapeDtypeStruct((shards, 128), I32),
        ),
        in_specs=[whole(SMEM), whole(VMEM), whole(VMEM)],
        out_specs=(whole(pl.ANY), whole(VMEM), whole(VMEM), whole(VMEM)),
        scratch_shapes=[
            VMEM((columns, 128), F32),
            SMEM(ask.shape, I32),
            pltpu.SemaphoreType.DMA((shards,)),
            pltpu.SemaphoreType.DMA((shards,)),
            pltpu.SemaphoreType.DMA,
        ]
        + exchange_scratch(shards, blocks),
        compiler_params=params(collective_id=0, has_side_effects=True),
        name="fetch",
    )(cosines, ask, gauss_rows)


def send_back_kernel(entry_ref, meta_ref, grads_ref, out_ref, even, odd, send, send_sem, recv_sem, own_sem):
    blocks = send.shape[1] // PITCH
    wait = greet()

    def finish(rows, to, c):
        used = meta_ref[to, blocks + c : blocks + c + 1, :] > 0
        send[to, c * PITCH : c * PITCH + SENT, :] = jnp.where(used, rows[...].T[0:SENT], 0.0)

    exchange(entry_ref, finish, grads_ref, even, odd, send, out_ref, send_sem, recv_sem, own_sem, wait)


def send_back(meta, grads):
    shards = meta.shape[0]
    blocks = meta.shape[1] // 2
    return pl.pallas_call(
        send_back_kernel,
        out_shape=jax.ShapeDtypeStruct((shards, blocks * PITCH, BLOCK), F32),
        in_specs=[whole(SMEM), whole(VMEM), whole(VMEM)],
        out_specs=whole(pl.ANY),
        scratch_shapes=exchange_scratch(shards, blocks),
        compiler_params=params(collective_id=1, has_side_effects=True),
        name="send_back",
    )(meta, meta, grads)


def composite_kernel(
    slot_ref, wire_ref, cot_ref, images_ref, out_ref,
    table, rows, alpha, ratio, logs, before, weight, weight_hi, weight_lo, pull, parts, after, earlier, later,
):
    t = pl.program_id(0)
    shards = wire_ref.shape[0]
    blocks = wire_ref.shape[1] // PITCH
    length = rows.shape[0]
    half = length // 2
    side = TILE_SIDE

    @pl.when(t == 0)
    def _():
        def unpack(s, _):
            for c in range(blocks):
                at = pl.multiple_of((s * blocks + c) * BLOCK, BLOCK)
                table[pl.ds(at, BLOCK), 0:SENT] = wire_ref[s, c * PITCH : c * PITCH + SENT, :].T
            return 0

        lax.fori_loop(0, shards, unpack, 0)
        above = iota((2 * half, half), 0) % half
        beside = iota((2 * half, half), 1)
        earlier[...] = (above < beside).astype(F32).astype(BF16)
        later[...] = (above > beside).astype(F32).astype(BF16)

    def put(ref, at, x):
        high, low = split(x)
        high, low = high.astype(BF16), low.astype(BF16)
        ref[pl.ds(at, side), 0:half] = high[:, 0:half]
        ref[pl.ds(at, side), half : 2 * half] = low[:, 0:half]
        ref[pl.ds(at, side), 2 * half : 3 * half] = high[:, half:]
        ref[pl.ds(at, side), 3 * half : 4 * half] = low[:, half:]

    def pick(i, _):
        at = pl.multiple_of(i * BLOCK, BLOCK)
        for u in range(BLOCK):
            rows[pl.ds(at + u, 1), :] = table[pl.ds(slot_ref[t * (length // BLOCK) + i, u], 1), :]
        return 0

    lax.fori_loop(0, length // BLOCK, pick, 0)
    turned = rows[...].T
    x0, y0, r2, r3, r4, r5 = (turned[k : k + 1] for k in range(GEOM))
    conic_a = jnp.exp(r2)
    conic_c = jnp.exp(r4)
    skew = jnp.tanh(r3)
    middle = jnp.sqrt(conic_a * conic_c)
    conic_b = 0.9 * skew * middle
    opaque = 1.0 / (1.0 + jnp.exp(-r5))
    spot = iota((side, length), 0).astype(F32) + 0.5
    dx = spot - x0
    dy = spot - y0
    scale = -0.5 * LOG2E
    part_x = (scale * conic_a) * dx * dx
    cross = (2.0 * scale * conic_b) * dx
    part_y = (scale * conic_c) * dy * dy + jnp.log2(0.99 * opaque)

    for py in range(side):
        at = py * side
        a = jnp.exp2(part_x + (cross * dy[py : py + 1] + part_y[py : py + 1]))
        log = jnp.log2(1.0 - a)
        alpha[pl.ds(at, side), :] = a
        ratio[pl.ds(at, side), :] = a * jnp.exp2(-log)
        put(logs, at, log)

    before[:, 0:half] = dot(logs[:, 0 : 2 * half], earlier[...])
    before[:, half:] = dot(logs[:, 2 * half :], earlier[...])

    for py in range(side):
        at = py * side
        b = before[pl.ds(at, side), :]
        last = (
            b[:, half - 1 : half]
            + logs[pl.ds(at, side), half - 1 : half].astype(F32)
            + logs[pl.ds(at, side), 2 * half - 1 : 2 * half].astype(F32)
        )
        b = jnp.concatenate([b[:, 0:half], b[:, half:] + last], axis=1)
        w = jnp.exp2(b) * alpha[pl.ds(at, side), :]
        high, low = split(w)
        weight[pl.ds(at, side), :] = w
        weight_hi[pl.ds(at, side), :] = high.astype(BF16)
        weight_lo[pl.ds(at, side), :] = low.astype(BF16)

    channel = iota((WIRE, length), 0)
    colour = jnp.where((channel >= GEOM) & (channel < GEOM + CHANNELS), turned[0:WIRE], 0.0)
    colour_hi, colour_lo = split(colour)
    cot = cot_ref[0]
    cot_hi, cot_lo = split(cot)
    fill = jnp.zeros((128 - 3 * WIRE, length), F32)
    fill_cot = jnp.zeros((128 - 3 * WIRE, PIXELS), F32)
    both = jnp.concatenate([colour_hi, colour_lo], axis=0).astype(BF16)
    image = dot(both, weight_hi[...], ((1,), (1,)))
    image_lo = dot(both, weight_lo[...], ((1,), (1,)))
    image = image[0:WIRE] + image[WIRE:] + image_lo[0:WIRE]
    images_ref[0] = image[GEOM : GEOM + CHANNELS]
    both = jnp.concatenate([cot_hi, cot_lo], axis=0).astype(BF16)
    grad = dot(both, weight_hi[...])
    grad_lo = dot(both, weight_lo[...])
    grad = grad[0:WIRE] + grad[WIRE:] + grad_lo[0:WIRE]
    three = jnp.concatenate([cot_hi, cot_lo, cot_hi, fill_cot], axis=0).T.astype(BF16)
    other = jnp.concatenate([colour_hi, colour_hi, colour_lo, fill], axis=0).astype(BF16)
    pull[...] = dot(three, other)

    for py in range(side):
        at = py * side
        q = pull[pl.ds(at, side), :] * weight[pl.ds(at, side), :]
        pull[pl.ds(at, side), :] = q
        put(parts, at, q)

    after[:, 0:half] = dot(parts[:, 0 : 2 * half], later[...])
    after[:, half:] = dot(parts[:, 2 * half :], later[...])

    m0 = jnp.zeros((side, length), F32)
    m1 = jnp.zeros((side, length), F32)
    m2 = jnp.zeros((side, length), F32)
    for py in range(side):
        at = py * side
        s = after[pl.ds(at, side), :]
        q = pull[pl.ds(at, side), :]
        first = s[:, half : half + 1] + q[:, half : half + 1]
        s = jnp.concatenate([s[:, 0:half] + first, s[:, half:]], axis=1)
        h = q - s * ratio[pl.ds(at, side), :]
        hy = h * dy[py : py + 1]
        m0 = m0 + h
        m1 = m1 + hy
        m2 = m2 + hy * dy[py : py + 1]

    def total(x):
        return jnp.sum(x, axis=0, keepdims=True)

    m0x = m0 * dx
    s0, sx, sy, sxx, sxy, syy = total(m0), total(m0x), total(m1), total(m0x * dx), total(m1 * dx), total(m2)
    shared = -0.5 * conic_b * sxy
    geometry = (
        conic_a * sx + conic_b * sy,
        conic_b * sx + conic_c * sy,
        shared - 0.5 * conic_a * sxx,
        -0.9 * (1.0 - skew * skew) * middle * sxy,
        shared - 0.5 * conic_c * syy,
        (1.0 - opaque) * s0,
    )
    for k, value in enumerate(geometry):
        grad = jnp.where(channel == k, value, grad)
    out_ref[:, 0:WIRE] = grad.T


def composite(slot, wire, cot):
    shards = wire.shape[0]
    slots = wire.shape[1] // PITCH * BLOCK
    tiles = cot.shape[0]
    length = slot.size // tiles
    full = (PIXELS, length)
    return pl.pallas_call(
        composite_kernel,
        grid=(tiles,),
        out_shape=(
            jax.ShapeDtypeStruct((tiles, CHANNELS, PIXELS), F32),
            jax.ShapeDtypeStruct((tiles * length, 128), F32),
        ),
        in_specs=[
            whole(SMEM),
            pl.BlockSpec(wire.shape, lambda i: (0, 0, 0), pipeline_mode=pl.Buffered(1)),
            pl.BlockSpec((1, WIRE, PIXELS), lambda i: (i, 0, 0)),
        ],
        out_specs=(
            pl.BlockSpec((1, CHANNELS, PIXELS), lambda i: (i, 0, 0)),
            pl.BlockSpec((length, 128), lambda i: (i, 0)),
        ),
        scratch_shapes=[
            VMEM((shards * slots, 128), F32),
            VMEM((length, 128), F32),
            VMEM(full, F32),
            VMEM(full, F32),
            VMEM((PIXELS, 2 * length), BF16),
            VMEM(full, F32),
            VMEM(full, F32),
            VMEM(full, BF16),
            VMEM(full, BF16),
            VMEM(full, F32),
            VMEM((PIXELS, 2 * length), BF16),
            VMEM(full, F32),
            VMEM((length, length // 2), BF16),
            VMEM((length, length // 2), BF16),
        ],
        compiler_params=params(),
        name="composite",
    )(slot, wire, cot)


def collect_kernel(half_ref, ask_ref, clash_ref, cos_ref, wire_ref, keep_ref, send_ref, table, table2, even, odd):
    source = pl.program_id(0)
    width, half = keep_ref.shape
    blocks = wire_ref.shape[1] // PITCH
    step = 512

    @pl.when(source == 0)
    def _():
        table[...] = jnp.zeros_like(table)
        table2[...] = jnp.zeros_like(table2)
        even[...] = jnp.zeros_like(even)
        odd[...] = jnp.zeros_like(odd)

    def turn(c, rows):
        back = wire_ref[0, c * PITCH : c * PITCH + SENT, :]
        scaled = cos_ref[0, c : c + 1, :] * back
        rows[:, 0:width] = jnp.concatenate([back, scaled[GEOM:SENT]], axis=0).T

    def add(at, c, rows):
        for g in range(BLOCK // GROUP):
            into = (table, table2)[g % 2]
            places = [ask_ref[at, c, g * GROUP + u] for u in range(GROUP)]
            sums = [into[pl.ds(r, 1), :] + rows[g * GROUP + u : g * GROUP + u + 1, :] for u, r in enumerate(places)]
            for r, value in zip(places, sums):
                into[pl.ds(r, 1), :] = value

    def add_slowly(at, c, rows):
        def one(u, _):
            table[pl.ds(ask_ref[at, c, u], 1), :] += rows[pl.ds(u, 1), :]
            return 0

        lax.fori_loop(0, BLOCK, one, 0)

    def finish(at, c, rows, more):
        clear = clash_ref[at, c] == 0

        @pl.when(clear)
        def _():
            more()
            add(at, c, rows)

        @pl.when(jnp.logical_not(clear))
        def _():
            more()
            add_slowly(at, c, rows)

    for c in range(blocks):
        now, past = (even, odd) if c % 2 == 0 else (odd, even)
        at = source if c else jnp.maximum(source - 1, 0)
        finish(at, (c - 1) % blocks, past, functools.partial(turn, c, now))

    @pl.when(source == pl.num_programs(0) - 1)
    def _():
        finish(source, blocks - 1, odd, lambda: None)
        for ref, base in ((keep_ref, half_ref[0]), (send_ref, half - half_ref[0])):

            def back(i, _):
                at = pl.multiple_of(i * step, step)
                there = pl.multiple_of(base + at, step)
                both = table[pl.ds(there, step), :] + table2[pl.ds(there, step), :]
                ref[:, pl.ds(at, step)] = both.T[0:width]
                return 0

            lax.fori_loop(0, half // step, back, 0)


def collect(half, asked, clash, cos, wire, width, columns):
    shards, sent, _ = wire.shape
    part = jax.ShapeDtypeStruct((width, columns // 2), F32)
    part_spec = pl.BlockSpec((width, columns // 2), lambda i: (0, 0), pipeline_mode=pl.Buffered(1))
    return pl.pallas_call(
        collect_kernel,
        grid=(shards,),
        out_shape=(part, part),
        in_specs=[
            whole(SMEM),
            whole(SMEM),
            whole(SMEM),
            pl.BlockSpec((1,) + cos.shape[1:], lambda i: (i, 0, 0)),
            pl.BlockSpec((1, sent, BLOCK), lambda i: (i, 0, 0)),
        ],
        out_specs=(part_spec, part_spec),
        scratch_shapes=[
            VMEM((columns, 128), F32),
            VMEM((columns, 128), F32),
            VMEM((BLOCK, 128), F32),
            VMEM((BLOCK, 128), F32),
        ],
        compiler_params=params(),
        name="collect",
    )(half, asked, clash, cos, wire)


def per_device(gauss_rows, vis_shard, vis_row, tile_index, cotangent):
    shards = lax.axis_size("gauss")
    width, columns = gauss_rows.shape
    ask, meta, slot = route(tile_index // SCREEN_TILES, vis_shard.reshape(vis_row.shape), vis_row, shards)
    cosines = jnp.cos(TWO_PI * jnp.arange(VIEWS, dtype=I32).astype(F32) / VIEWS)
    fetched, asked, cos, clash = fetch(cosines, ask, gauss_rows)
    cot = jnp.pad(cotangent, ((0, 0), (GEOM, WIRE - GEOM - CHANNELS), (0, 0)))
    images, grads = composite(slot, fetched, cot)
    returned = send_back(meta, grads)
    half = (lax.axis_index("view") * (columns // 2)).astype(I32).reshape(1)
    keep, send = collect(half, asked, clash, cos, returned, width, columns)
    other = lax.ppermute(send, "view", [(0, 1), (1, 0)])
    return (images, keep + other)


def solution(mesh):
    placed = (
        P(None, "gauss"),
        P(("gauss", "view"), None, None),
        P(("gauss", "view"), None),
        P(("gauss", "view")),
        P(("gauss", "view"), None, None),
    )
    return jax.shard_map(
        per_device,
        mesh=mesh,
        in_specs=placed,
        out_specs=(P(("gauss", "view"), None, None), P(None, ("gauss", "view"))),
        check_vma=False,
    )
```

```python
import functools
import math

import jax
import jax.numpy as jnp
from jax import lax
from jax.experimental import pallas as pl
from jax.experimental.pallas import tpu as pltpu
from jax.sharding import PartitionSpec as P

CHANNELS = 29
TILE_SIDE = 16
PIXELS = 256
VIEWS = 8
SCREEN_TILES = 8160
GEOM = 6
SENT = 35
WIRE = 40
PITCH = 36
TWO_PI = 6.283185307179586
LOG2E = 1.4426950408889634
VMEM = pltpu.VMEM
SMEM = pltpu.SMEM
F32 = jnp.float32
BF16 = jnp.bfloat16
I32 = jnp.int32
GROUP = 8
BLOCK = 128
SOURCES = 8
PICKS = 8


def params(**more):
    return pltpu.CompilerParams(vmem_limit_bytes=60 * 2**20, **more)


def whole(space):
    return pl.BlockSpec(memory_space=space)


def iota(shape, dim):
    return lax.broadcasted_iota(I32, shape, dim)


def dot(a, b, contract=((1,), (0,))):
    return lax.dot_general(a, b, (contract, ((), ())), preferred_element_type=F32)


def view_cosines():
    return [math.cos(TWO_PI * v / VIEWS) for v in range(VIEWS)]


def split(x):
    high = x.astype(BF16).astype(F32)
    return high, x - high


def route_kernel(tile_ref, shard_ref, row_ref, ask_ref, meta_ref, slot_ref):
    shards = ask_ref.shape[0]
    tiles, length = row_ref.shape
    tile_blocks = length // BLOCK
    width = 256
    parts = length // width
    capacity = 2 * tiles * length // shards
    blocks = capacity // BLOCK
    before = (iota((width, width), 0) < iota((width, width), 1)).astype(F32).astype(BF16)
    lane = iota((1, width), 1).astype(F32)

    def some(i, state):
        carry, total = state
        spots = [(2 * i + u // parts, u % parts) for u in range(2 * parts)]
        shard = [
            jnp.concatenate(
                [shard_ref[pl.ds(t * tile_blocks + h * (width // BLOCK) + b, 1), :] for b in range(width // BLOCK)],
                axis=1,
            )
            for t, h in spots
        ]
        hot = [(iota((shards, width), 0) == one).astype(F32) for one in shard]
        seen = dot(jnp.concatenate(hot, axis=0).astype(BF16), before)
        at, values = [], []
        for u, (t, h) in enumerate(spots):
            place = jnp.sum(hot[u] * (seen[shards * u : shards * (u + 1)] + carry), axis=0, keepdims=True)
            carry = carry + jnp.sum(hot[u], axis=1, keepdims=True)
            place = place.astype(I32)
            slot = shard[u] * capacity + place
            for b in range(width // BLOCK):
                slot_ref[pl.ds(t * tile_blocks + h * (width // BLOCK) + b, 1), :] = slot[
                    :, b * BLOCK : (b + 1) * BLOCK
                ]
            at.append((iota((capacity, width), 0) == place).astype(F32).astype(BF16))
            row = row_ref[pl.ds(t, 1), h * width : (h + 1) * width]
            parts_of = (
                (row & 255).astype(F32),
                (row >> 8).astype(F32),
                sum(
                    (jnp.full((1, width), tile_ref[t], I32) >= SCREEN_TILES * v).astype(F32) for v in range(VIEWS)
                ),
                lane,
                jnp.full((1, width), t * parts + h, I32).astype(F32),
            )
            values.append(jnp.concatenate([hot[u] * part for part in parts_of], axis=0).astype(BF16))
        at = jnp.concatenate(at, axis=1)
        values = jnp.concatenate(values, axis=1)
        return carry, total + dot(values, at, ((1,), (1,)))

    start = (jnp.zeros((shards, 1), F32), jnp.zeros((5 * shards, capacity), F32))
    _, total = lax.fori_loop(0, tiles // 2, some, start)
    low, high, view, lane, chunk = (total[shards * k : shards * (k + 1)].astype(I32) for k in range(5))
    used = view > 0
    row = jnp.where(used, low + 256 * high, iota((shards, capacity), 1))
    view = jnp.where(used, view - 1, 0)
    entry = lane + width * chunk
    used = used.astype(I32)
    for c in range(blocks):
        lanes = slice(c * BLOCK, (c + 1) * BLOCK)
        ask_ref[:, c, :] = row[:, lanes]
        ask_ref[:, blocks + c, :] = view[:, lanes]
        meta_ref[:, c, :] = entry[:, lanes]
        meta_ref[:, blocks + c, :] = used[:, lanes]


def route(tile, shard, row, shards):
    tiles, length = row.shape
    lists = jax.ShapeDtypeStruct((shards, 8, BLOCK), I32)
    return pl.pallas_call(
        route_kernel,
        out_shape=(lists, lists, jax.ShapeDtypeStruct((tiles * length // BLOCK, BLOCK), I32)),
        in_specs=[whole(SMEM), whole(VMEM), whole(VMEM)],
        out_specs=(whole(VMEM),) * 3,
        compiler_params=params(),
        name="route",
    )(tile, shard, row)


def shifted(k, back=False):
    shards = lax.axis_size("gauss")
    side = round(shards ** (1 / 3))
    me = lax.axis_index("gauss")
    step = lax.rem(37 * k, shards)
    sign = 1 - 2 * lax.axis_index("view")
    if back:
        sign = -sign

    def part(x, by):
        return lax.rem(x // by, side)

    def moved(by):
        return lax.rem(part(me, by) + sign * part(step, by) + side, side) * by

    return moved(side * side) + moved(side) + moved(1)


def remote(src, dst, send_sem, recv_sem, to):
    return pltpu.make_async_remote_copy(
        src_ref=src,
        dst_ref=dst,
        send_sem=send_sem,
        recv_sem=recv_sem,
        device_id={"gauss": to},
        device_id_type=pl.DeviceIdType.MESH,
    )


def exchange(ask_ref, finish, table, even, odd, send, to_ref, send_sem, recv_sem, arrived, own):
    shards = send.shape[0]
    blocks = send.shape[1] // PITCH
    me = lax.axis_index("gauss")

    def copy(to, by):
        return remote(send.at[to], to_ref.at[by], send_sem.at[to], recv_sem.at[by], to)

    def one(k, _):
        to, last = shifted(k), shifted(k + shards - 1)
        for c in range(blocks):
            now, past = (even, odd) if c % 2 == 0 else (odd, even)
            finish(past, *((to, c - 1) if c else (last, blocks - 1)))
            for u in range(BLOCK):
                now[u : u + 1, :] = table[pl.ds(ask_ref[to, c, u], 1), :]
            if c == 0:

                @pl.when(k == 1)
                def _():
                    own()

                @pl.when(k > 1)
                def _():
                    copy(last, me).start()

        return 0

    lax.fori_loop(0, shards, one, 0)
    last = shifted(shards - 1)
    finish(odd, last, blocks - 1)
    copy(last, me).start()

    def end(k, _):
        by = shifted(k, True)
        copy(me, by).wait_recv()
        arrived(by)
        copy(shifted(k), me).wait_send()
        return 0

    lax.fori_loop(1, shards, end, 0)


def greet():
    shards = lax.axis_size("gauss")
    me = lax.axis_index("gauss")
    barrier = pltpu.get_barrier_semaphore()

    def hail(k, _):
        pl.semaphore_signal(
            barrier, inc=1, device_id={"gauss": lax.rem(me + k, shards)}, device_id_type=pl.DeviceIdType.MESH
        )
        return 0

    lax.fori_loop(1, shards, hail, 0)

    def wait():
        pl.semaphore_wait(barrier, shards - 1)

    return wait


class Tile:
    def __init__(self, t, cot_ref, images_ref, grads, rows, earlier, later, scratch):
        self.t, self.cot_ref, self.images_ref, self.grads, self.rows = t, cot_ref, images_ref, grads, rows
        self.earlier, self.later = earlier, later
        self.turned, self.alpha, self.ratio, self.parts, self.sums, self.weight, self.high, self.low, self.pull = scratch
        self.length = rows.shape[0]
        self.half = self.length // 2

    def put(self, at, x):
        half = self.half
        high, low = split(x)
        high, low = high.astype(BF16), low.astype(BF16)
        self.parts[pl.ds(at, TILE_SIDE), 0:half] = high[:, 0:half]
        self.parts[pl.ds(at, TILE_SIDE), half : 2 * half] = low[:, 0:half]
        self.parts[pl.ds(at, TILE_SIDE), 2 * half : 3 * half] = high[:, half:]
        self.parts[pl.ds(at, TILE_SIDE), 3 * half : 4 * half] = low[:, half:]

    def turn(self):
        self.turned[...] = self.rows[...].T[0:WIRE]

    def shape(self):
        turned = self.turned
        self.x0, self.y0, r2, r3, r4, r5 = (turned[k : k + 1, :] for k in range(GEOM))
        self.conic_a = jnp.exp(r2)
        self.conic_c = jnp.exp(r4)
        self.skew = jnp.tanh(r3)
        self.middle = jnp.sqrt(self.conic_a * self.conic_c)
        self.conic_b = 0.9 * self.skew * self.middle
        self.opaque = 1.0 / (1.0 + jnp.exp(-r5))
        spot = iota((TILE_SIDE, self.length), 0).astype(F32) + 0.5
        self.dx = spot - self.x0
        self.dy = spot - self.y0
        scale = -0.5 * LOG2E
        self.part_x = (scale * self.conic_a) * self.dx * self.dx
        self.cross = (2.0 * scale * self.conic_b) * self.dx
        self.part_y = (scale * self.conic_c) * self.dy * self.dy + jnp.log2(0.99 * self.opaque)

    def alphas(self, py):
        at = py * TILE_SIDE
        a = jnp.exp2(self.part_x + (self.cross * self.dy[py : py + 1] + self.part_y[py : py + 1]))
        log = jnp.log2(1.0 - a)
        self.alpha[pl.ds(at, TILE_SIDE), :] = a
        self.ratio[pl.ds(at, TILE_SIDE), :] = a * jnp.exp2(-log)
        self.put(at, log)

    def prefix(self):
        half = self.half
        self.sums[:, 0:half] = dot(self.parts[:, 0 : 2 * half], self.earlier[...])
        self.sums[:, half:] = dot(self.parts[:, 2 * half :], self.earlier[...])

    def weights(self, py):
        at, half = py * TILE_SIDE, self.half
        b = self.sums[pl.ds(at, TILE_SIDE), :]
        last = (
            b[:, half - 1 : half]
            + self.parts[pl.ds(at, TILE_SIDE), half - 1 : half].astype(F32)
            + self.parts[pl.ds(at, TILE_SIDE), 2 * half - 1 : 2 * half].astype(F32)
        )
        b = jnp.concatenate([b[:, 0:half], b[:, half:] + last], axis=1)
        w = jnp.exp2(b) * self.alpha[pl.ds(at, TILE_SIDE), :]
        high, low = split(w)
        self.weight[pl.ds(at, TILE_SIDE), :] = w
        self.high[pl.ds(at, TILE_SIDE), :] = high.astype(BF16)
        self.low[pl.ds(at, TILE_SIDE), :] = low.astype(BF16)

    def products(self):
        channel = iota((WIRE, self.length), 0)
        colour = jnp.where((channel >= GEOM) & (channel < SENT), self.turned[...], 0.0)
        colour_hi, colour_lo = split(colour)
        cot = jnp.concatenate(
            [jnp.zeros((GEOM, PIXELS), F32), self.cot_ref[self.t], jnp.zeros((WIRE - SENT, PIXELS), F32)], axis=0
        )
        cot_hi, cot_lo = split(cot)
        fill = jnp.zeros((128 - 3 * WIRE, self.length), F32)
        fill_cot = jnp.zeros((128 - 3 * WIRE, PIXELS), F32)
        three = jnp.concatenate([cot_hi, cot_lo, cot_hi, fill_cot], axis=0).T.astype(BF16)
        other = jnp.concatenate([colour_hi, colour_hi, colour_lo, fill], axis=0).astype(BF16)
        self.pull[...] = dot(three, other)
        both = jnp.concatenate([colour_hi, colour_lo], axis=0).astype(BF16)
        image = dot(both, self.high[...], ((1,), (1,)))
        image_lo = dot(both[0:48], self.low[...], ((1,), (1,)))
        image = image[0:WIRE] + image[WIRE:] + image_lo[0:WIRE]
        self.images_ref[self.t] = image[GEOM:SENT]
        both = jnp.concatenate([cot_hi, cot_lo], axis=0).astype(BF16)
        grad = dot(both, self.high[...])
        grad_lo = dot(both[0:48], self.low[...])
        self.turned[...] = grad[0:WIRE] + grad[WIRE:] + grad_lo[0:WIRE]

    def terms(self, py):
        at = py * TILE_SIDE
        q = self.pull[pl.ds(at, TILE_SIDE), :] * self.weight[pl.ds(at, TILE_SIDE), :]
        self.pull[pl.ds(at, TILE_SIDE), :] = q
        self.put(at, q)

    def suffix(self):
        half = self.half
        self.sums[:, 0:half] = dot(self.parts[:, 0 : 2 * half], self.later[...])
        self.sums[:, half:] = dot(self.parts[:, 2 * half :], self.later[...])

    def moments(self, py):
        at, half = py * TILE_SIDE, self.half
        s = self.sums[pl.ds(at, TILE_SIDE), :]
        q = self.pull[pl.ds(at, TILE_SIDE), :]
        first = s[:, half : half + 1] + q[:, half : half + 1]
        s = jnp.concatenate([s[:, 0:half] + first, s[:, half:]], axis=1)
        h = q - s * self.ratio[pl.ds(at, TILE_SIDE), :]
        hy = h * self.dy[py : py + 1]
        hyy = hy * self.dy[py : py + 1]
        if py == 0:
            self.m0, self.m1, self.m2 = h, hy, hyy
        else:
            self.m0, self.m1, self.m2 = self.m0 + h, self.m1 + hy, self.m2 + hyy

    def close(self):
        def total(x):
            return jnp.sum(x, axis=0, keepdims=True)

        m0x = self.m0 * self.dx
        s0, sx, sy = total(self.m0), total(m0x), total(self.m1)
        sxx, sxy, syy = total(m0x * self.dx), total(self.m1 * self.dx), total(self.m2)
        shared = -0.5 * self.conic_b * sxy
        geometry = (
            self.conic_a * sx + self.conic_b * sy,
            self.conic_b * sx + self.conic_c * sy,
            shared - 0.5 * self.conic_a * sxx,
            -0.9 * (1.0 - self.skew * self.skew) * self.middle * sxy,
            shared - 0.5 * self.conic_c * syy,
            (1.0 - self.opaque) * s0,
        )
        grad = self.turned[...]
        channel = iota(grad.shape, 0)
        for k, value in enumerate(geometry):
            grad = jnp.where(channel == k, value, grad)
        at = pl.multiple_of(self.t * self.length, self.length)
        self.grads[pl.ds(at, self.length), 0:WIRE] = grad.T


def paint(slot_ref, cot_ref, images_ref, table, grads, rows, earlier, later, scratch):
    tiles = cot_ref.shape[0]
    length = rows[0].shape[0]
    blocks = length // BLOCK
    half = length // 2
    above = iota((2 * half, half), 0) % half
    beside = iota((2 * half, half), 1)
    earlier[...] = (above < beside).astype(F32).astype(BF16)
    later[...] = (above > beside).astype(F32).astype(BF16)

    def pick(into, t, start, count):
        for u in range(start, start + count):
            into[u : u + 1, :] = table[pl.ds(slot_ref[t * blocks + u // BLOCK, u % BLOCK], 1), :]

    pick(rows[0], 0, 0, length)
    pick(rows[1], 1, 0, length)

    def two(i, _):
        a, b = (
            Tile(2 * i + k, cot_ref, images_ref, grads, rows[k], earlier, later, scratch[k]) for k in range(2)
        )
        following = [jnp.minimum(2 * i + 2 + k, tiles - 1) for k in range(2)]
        todo = [(k, start) for start in range(0, length, PICKS) for k in range(2)]

        def more():
            if todo:
                k, start = todo.pop(0)
                pick(rows[k], following[k], start, PICKS)

        def sweep(step):
            for py in range(TILE_SIDE):
                step(py)
                more()

        a.turn()
        b.turn()
        a.shape()
        sweep(a.alphas)
        a.prefix()
        b.shape()
        sweep(b.alphas)
        b.prefix()
        sweep(a.weights)
        a.products()
        sweep(b.weights)
        b.products()
        sweep(a.terms)
        a.suffix()
        sweep(b.terms)
        b.suffix()
        sweep(a.moments)
        a.close()
        sweep(b.moments)
        b.close()
        while todo:
            more()
        return 0

    lax.fori_loop(0, tiles // 2, two, 0)


def paint_scratch(length):
    full = (PIXELS, length)
    one = [
        VMEM((WIRE, length), F32),
        VMEM(full, F32),
        VMEM(full, F32),
        VMEM((PIXELS, 2 * length), BF16),
        VMEM(full, F32),
        VMEM(full, F32),
        VMEM(full, BF16),
        VMEM(full, BF16),
        VMEM(full, F32),
    ]
    return [VMEM((length, 128), F32)] * 2 + [VMEM((length, length // 2), BF16)] * 2 + one + one


def render_kernel(
    slot_ref, entry_ref, ask_ref, meta_ref, rows_ref, cot_ref,
    images_ref, back_ref, asked_ref, cos_ref, clash_ref,
    held, table, asked, ask_send, ask_recv, own_sem, even, odd, send, got,
    send_sem, recv_sem, back_send, back_recv, grads, *scratch,
):
    width, columns = held.shape
    shards = send.shape[0]
    blocks = send.shape[1] // PITCH
    me = lax.axis_index("gauss")
    load = pltpu.make_async_copy(rows_ref, held, own_sem)
    load.start()
    greet()()

    def copy(to, by):
        return remote(ask_ref.at[to], asked_ref.at[by], ask_send.at[to], ask_recv.at[by], to)

    def ask(k, _):
        copy(shifted(k), me).start()
        return 0

    lax.fori_loop(1, shards, ask, 0)
    load.wait()

    def turn(i, _):
        at = pl.multiple_of(i * 512, 512)
        table[pl.ds(at, 512), 0:width] = held[:, pl.ds(at, 512)].T
        return 0

    lax.fori_loop(0, columns // 512, turn, 0)
    asked_ref[me] = ask_ref[me]

    def end(k, _):
        copy(shifted(k), me).wait_send()
        copy(me, shifted(k, True)).wait_recv()
        return 0

    lax.fori_loop(1, shards, end, 0)
    down = pltpu.make_async_copy(asked_ref, asked, own_sem)
    down.start()
    for c in range(blocks):
        row = asked_ref[:, c, :]
        view = asked_ref[:, blocks + c, :]
        cos = jnp.zeros(view.shape, F32)
        for v, value in enumerate(view_cosines()):
            cos = jnp.where(view == v, value, cos)
        cos_ref[:, c, :] = cos
        lane = iota(row.shape, 1) % GROUP
        same = jnp.zeros(row.shape, F32)
        for d in range(1, GROUP):
            same = jnp.where((pltpu.roll(row, d, 1) == row) & (lane >= d), 1.0, same)
        clash_ref[:, c : c + 1] = jnp.max(same, axis=1, keepdims=True).astype(I32)
    down.wait()

    def blend(rows, to, c):
        turned = rows[...].T
        second = jnp.concatenate([jnp.zeros((GEOM, BLOCK), F32), turned[SENT : SENT + CHANNELS]], axis=0)
        send[to, c * PITCH : c * PITCH + SENT, :] = turned[0:SENT] + cos_ref[to, c : c + 1, :] * second

    def unpack(source, by):
        for c in range(blocks):
            at = pl.multiple_of((by * blocks + c) * BLOCK, BLOCK)
            table[pl.ds(at, BLOCK), 0:SENT] = source[by, c * PITCH : c * PITCH + SENT, :].T

    def arrived(by):
        unpack(got, by)

    exchange(asked, blend, table, even, odd, send, got, send_sem, recv_sem, arrived, lambda: None)
    unpack(send, me)

    paint(
        slot_ref, cot_ref, images_ref, table, grads, scratch[0:2], scratch[2], scratch[3], (scratch[4:13], scratch[13:22])
    )

    def mask(rows, to, c):
        used = meta_ref[to, blocks + c : blocks + c + 1, :] > 0
        send[to, c * PITCH : c * PITCH + SENT, :] = jnp.where(used, rows[...].T[0:SENT], 0.0)

    own = pltpu.make_async_copy(send.at[me], back_ref.at[me], own_sem)
    exchange(entry_ref, mask, grads, even, odd, send, back_ref, back_send, back_recv, lambda by: None, own.start)
    own.wait()


def render(slot, meta, ask, gauss_rows, cot):
    shards = ask.shape[0]
    blocks = ask.shape[1] // 2
    width, columns = gauss_rows.shape
    tiles = cot.shape[0]
    length = slot.size // tiles
    wire = (shards, blocks * PITCH, BLOCK)
    sems = pltpu.SemaphoreType.DMA((shards,))
    return pl.pallas_call(
        render_kernel,
        out_shape=(
            jax.ShapeDtypeStruct((tiles, CHANNELS, PIXELS), F32),
            jax.ShapeDtypeStruct(wire, F32),
            jax.ShapeDtypeStruct(ask.shape, I32),
            jax.ShapeDtypeStruct(ask.shape, F32),
            jax.ShapeDtypeStruct((shards, 128), I32),
        ),
        in_specs=[whole(SMEM), whole(SMEM), whole(VMEM), whole(VMEM), whole(pl.ANY), whole(VMEM)],
        out_specs=(whole(VMEM), whole(pl.ANY), whole(VMEM), whole(VMEM), whole(VMEM)),
        scratch_shapes=[
            VMEM((width, columns), F32),
            VMEM((columns, 128), F32),
            SMEM(ask.shape, I32),
            sems,
            sems,
            pltpu.SemaphoreType.DMA,
            VMEM((BLOCK, 128), F32),
            VMEM((BLOCK, 128), F32),
            VMEM(wire, F32),
            VMEM(wire, F32),
            sems,
            sems,
            sems,
            sems,
            VMEM((tiles * length, 128), F32),
        ]
        + paint_scratch(length),
        compiler_params=params(collective_id=0, has_side_effects=True),
        name="render",
    )(slot, meta, ask, meta, gauss_rows, cot)


def collect_kernel(half_ref, ask_ref, clash_ref, cos_ref, wire_ref, keep_ref, send_ref, table, table2, even, odd):
    step_id = pl.program_id(0)
    sources = wire_ref.shape[0]
    width, half = keep_ref.shape
    blocks = wire_ref.shape[1] // PITCH
    step = 512

    @pl.when(step_id == 0)
    def _():
        table[...] = jnp.zeros_like(table)
        table2[...] = jnp.zeros_like(table2)
        even[...] = jnp.zeros_like(even)
        odd[...] = jnp.zeros_like(odd)

    def turn(s, c, rows):
        back = wire_ref[s, c * PITCH : c * PITCH + SENT, :]
        scaled = cos_ref[s, c : c + 1, :] * back
        rows[:, 0:width] = jnp.concatenate([back, scaled[GEOM:SENT]], axis=0).T

    def add(at, c, rows):
        for g in range(BLOCK // GROUP):
            into = (table, table2)[g % 2]
            places = [ask_ref[at, c, g * GROUP + u] for u in range(GROUP)]
            sums = [into[pl.ds(r, 1), :] + rows[g * GROUP + u : g * GROUP + u + 1, :] for u, r in enumerate(places)]
            for r, value in zip(places, sums):
                into[pl.ds(r, 1), :] = value

    def add_slowly(at, c, rows):
        def one(u, _):
            table[pl.ds(ask_ref[at, c, u], 1), :] += rows[pl.ds(u, 1), :]
            return 0

        lax.fori_loop(0, BLOCK, one, 0)

    def finish(at, c, rows, more):
        clear = clash_ref[at, c] == 0

        @pl.when(clear)
        def _():
            more()
            add(at, c, rows)

        @pl.when(jnp.logical_not(clear))
        def _():
            more()
            add_slowly(at, c, rows)

    def one(s, _):
        source = step_id * sources + s
        for c in range(blocks):
            now, past = (even, odd) if c % 2 == 0 else (odd, even)
            at = source if c else jnp.maximum(source - 1, 0)
            finish(at, (c - 1) % blocks, past, functools.partial(turn, s, c, now))
        return 0

    lax.fori_loop(0, sources, one, 0)

    @pl.when(step_id == pl.num_programs(0) - 1)
    def _():
        finish(pl.num_programs(0) * sources - 1, blocks - 1, odd, lambda: None)
        for ref, base in ((keep_ref, half_ref[0]), (send_ref, half - half_ref[0])):

            def back(i, _):
                at = pl.multiple_of(i * step, step)
                there = pl.multiple_of(base + at, step)
                both = table[pl.ds(there, step), :] + table2[pl.ds(there, step), :]
                ref[:, pl.ds(at, step)] = both.T[0:width]
                return 0

            lax.fori_loop(0, half // step, back, 0)


def collect(half, asked, clash, cos, wire, width, columns):
    shards, sent, _ = wire.shape
    part = jax.ShapeDtypeStruct((width, columns // 2), F32)
    part_spec = pl.BlockSpec((width, columns // 2), lambda i: (0, 0), pipeline_mode=pl.Buffered(1))
    return pl.pallas_call(
        collect_kernel,
        grid=(shards // SOURCES,),
        out_shape=(part, part),
        in_specs=[
            whole(SMEM),
            whole(SMEM),
            whole(SMEM),
            pl.BlockSpec((SOURCES,) + cos.shape[1:], lambda i: (i, 0, 0)),
            pl.BlockSpec((SOURCES, sent, BLOCK), lambda i: (i, 0, 0)),
        ],
        out_specs=(part_spec, part_spec),
        scratch_shapes=[
            VMEM((columns, 128), F32),
            VMEM((columns, 128), F32),
            VMEM((BLOCK, 128), F32),
            VMEM((BLOCK, 128), F32),
        ],
        compiler_params=params(),
        name="collect",
    )(half, asked, clash, cos, wire)


def per_device(gauss_rows, vis_shard, vis_row, tile_index, cotangent):
    shards = lax.axis_size("gauss")
    width, columns = gauss_rows.shape
    ask, meta, slot = route(tile_index, vis_shard.reshape(-1, BLOCK), vis_row, shards)
    images, returned, asked, cos, clash = render(slot, meta, ask, gauss_rows, cotangent)
    half = (lax.axis_index("view") * (columns // 2)).astype(I32).reshape(1)
    keep, send = collect(half, asked, clash, cos, returned, width, columns)
    other = lax.ppermute(send, "view", [(0, 1), (1, 0)])
    return (images, keep + other)


def solution(mesh):
    placed = (
        P(None, "gauss"),
        P(("gauss", "view"), None, None),
        P(("gauss", "view"), None),
        P(("gauss", "view")),
        P(("gauss", "view"), None, None),
    )
    return jax.shard_map(
        per_device,
        mesh=mesh,
        in_specs=placed,
        out_specs=(P(("gauss", "view"), None, None), P(None, ("gauss", "view"))),
        check_vma=False,
    )
```

```python
import functools
import math

import jax
import jax.numpy as jnp
from jax import lax
from jax.experimental import pallas as pl
from jax.experimental.pallas import tpu as pltpu
from jax.sharding import PartitionSpec as P

CHANNELS = 29
TILE_SIDE = 16
PIXELS = 256
VIEWS = 8
SCREEN_TILES = 8160
GEOM = 6
SENT = 35
WIRE = 40
PITCH = 36
TWO_PI = 6.283185307179586
LOG2E = 1.4426950408889634
VMEM = pltpu.VMEM
SMEM = pltpu.SMEM
F32 = jnp.float32
BF16 = jnp.bfloat16
I32 = jnp.int32
GROUP = 8
BLOCK = 128
REGIONS = 2
FIRST = 3 / 8
SECOND = 5 / 8
SOURCES = 8
COPIES = 4
PICKS = 8


def params(**more):
    return pltpu.CompilerParams(vmem_limit_bytes=60 * 2**20, **more)


def whole(space):
    return pl.BlockSpec(memory_space=space)


def iota(shape, dim):
    return lax.broadcasted_iota(I32, shape, dim)


def dot(a, b, contract=((1,), (0,))):
    return lax.dot_general(a, b, (contract, ((), ())), preferred_element_type=F32)


def view_cosines():
    return [math.cos(TWO_PI * v / VIEWS) for v in range(VIEWS)]


def split(x):
    high = x.astype(BF16).astype(F32)
    return high, x - high


def route_kernel(tile_ref, shard_ref, row_ref, ask_ref, entry_ref, used_ref, slot_ref, carry_ref, early_ref):
    shards = ask_ref.shape[0]
    tiles, length = row_ref.shape
    tile_blocks = length // BLOCK
    width = 256
    parts = length // width
    capacity = 2 * tiles * length // shards
    blocks = capacity // BLOCK
    part = float(capacity // REGIONS)
    first, second = int(tiles * FIRST) // 2, int(tiles * SECOND) // 2
    before = (iota((width, width), 0) < iota((width, width), 1)).astype(F32).astype(BF16)
    lane = iota((1, width), 1).astype(F32)

    def some(i, state):
        total = state
        carry = carry_ref[...]
        early_ref[...] = jnp.maximum(early_ref[...], carry * jnp.where(i == first, 1.0, 0.0))
        carry = jnp.maximum(carry, jnp.where(i == second, part, 0.0))
        spots = [(2 * i + u // parts, u % parts) for u in range(2 * parts)]
        shard = [
            jnp.concatenate(
                [shard_ref[pl.ds(t * tile_blocks + h * (width // BLOCK) + b, 1), :] for b in range(width // BLOCK)],
                axis=1,
            )
            for t, h in spots
        ]
        hot = [(iota((shards, width), 0) == one).astype(F32) for one in shard]
        seen = dot(jnp.concatenate(hot, axis=0).astype(BF16), before)
        at, values = [], []
        for u, (t, h) in enumerate(spots):
            place = jnp.sum(hot[u] * (seen[shards * u : shards * (u + 1)] + carry), axis=0, keepdims=True)
            carry = carry + jnp.broadcast_to(jnp.sum(hot[u], axis=1, keepdims=True), hot[u].shape)
            place = place.astype(I32)
            slot = shard[u] * capacity + jnp.minimum(place, capacity - 1)
            for b in range(width // BLOCK):
                slot_ref[pl.ds(t * tile_blocks + h * (width // BLOCK) + b, 1), :] = slot[
                    :, b * BLOCK : (b + 1) * BLOCK
                ]
            at.append((iota((capacity, width), 0) == place).astype(F32).astype(BF16))
            row = row_ref[pl.ds(t, 1), h * width : (h + 1) * width]
            parts_of = (
                (row & 255).astype(F32),
                (row >> 8).astype(F32),
                sum(
                    (jnp.full((1, width), tile_ref[t], I32) >= SCREEN_TILES * v).astype(F32) for v in range(VIEWS)
                ),
                lane,
                jnp.full((1, width), t * parts + h, I32).astype(F32),
            )
            values.append(jnp.concatenate([hot[u] * part for part in parts_of], axis=0).astype(BF16))
        at = jnp.concatenate(at, axis=1)
        values = jnp.concatenate(values, axis=1)
        carry_ref[...] = carry
        return total + dot(values, at, ((1,), (1,)))

    carry_ref[...] = jnp.zeros_like(carry_ref)
    early_ref[...] = jnp.zeros_like(early_ref)
    total = lax.fori_loop(0, tiles // 2, some, jnp.zeros((5 * shards, capacity), F32))
    over = (early_ref[...] > part) | (carry_ref[...] > float(capacity))
    over = jnp.max(over.astype(F32), axis=(0, 1), keepdims=True)
    low, high, view, lane, chunk = (total[shards * k : shards * (k + 1)].astype(I32) for k in range(5))
    used = view > 0
    row = jnp.where(used, low + 256 * high, iota((shards, capacity), 1))
    view = jnp.where(over > 0.0, VIEWS, jnp.where(used, view - 1, 0))
    entry = lane + width * chunk
    used = used.astype(I32)
    for c in range(blocks):
        lanes = slice(c * BLOCK, (c + 1) * BLOCK)
        ask_ref[:, c, :] = row[:, lanes]
        ask_ref[:, blocks + c, :] = view[:, lanes]
        entry_ref[:, c, :] = entry[:, lanes]
        used_ref[:, c, :] = used[:, lanes]


def route(tile, shard, row, shards):
    tiles, length = row.shape
    blocks = 2 * tiles * length // shards // BLOCK
    lists = jax.ShapeDtypeStruct((shards, blocks, BLOCK), I32)
    return pl.pallas_call(
        route_kernel,
        out_shape=(
            jax.ShapeDtypeStruct((shards, 2 * blocks, BLOCK), I32),
            lists,
            lists,
            jax.ShapeDtypeStruct((tiles * length // BLOCK, BLOCK), I32),
        ),
        in_specs=[whole(SMEM), whole(VMEM), whole(VMEM)],
        out_specs=(whole(VMEM),) * 4,
        scratch_shapes=[VMEM((shards, 256), F32)] * 2,
        compiler_params=params(),
        name="route",
    )(tile, shard, row)


def shifted(k, back=False):
    shards = lax.axis_size("gauss")
    side = round(shards ** (1 / 3))
    me = lax.axis_index("gauss")
    step = lax.rem(37 * k, shards)
    sign = 1 - 2 * lax.axis_index("view")
    if back:
        sign = -sign

    def part(x, by):
        return lax.rem(x // by, side)

    def moved(by):
        return lax.rem(part(me, by) + sign * part(step, by) + side, side) * by

    return moved(side * side) + moved(side) + moved(1)


def remote(src, dst, send_sem, recv_sem, to):
    return pltpu.make_async_remote_copy(
        src_ref=src,
        dst_ref=dst,
        send_sem=send_sem,
        recv_sem=recv_sem,
        device_id={"gauss": to},
        device_id_type=pl.DeviceIdType.MESH,
    )


class Exchange:
    def __init__(self, ask_ref, finish, table, even, odd, send, to_ref, send_sem, recv_sem, own=None):
        self.ask_ref, self.finish, self.table, self.even, self.odd = ask_ref, finish, table, even, odd
        self.send, self.to_ref, self.send_sem, self.recv_sem, self.own = send, to_ref, send_sem, recv_sem, own
        self.shards = send.shape[0]
        self.rows = send.shape[1] // REGIONS
        self.blocks = self.rows // PITCH
        self.me = lax.axis_index("gauss")

    def piece(self, ref, shard, part):
        return ref.at[shard, pl.ds(part * self.rows, self.rows)]

    def copy(self, part, to, by):
        return remote(
            self.piece(self.send, to, part),
            self.piece(self.to_ref, by, part),
            self.send_sem.at[part, to],
            self.recv_sem.at[part, by],
            to,
        )

    def kept(self, part):
        return pltpu.make_async_copy(
            self.piece(self.send, self.me, part), self.piece(self.to_ref, self.me, part), self.own.at[part]
        )

    def start(self, part):
        blocks = self.blocks

        def one(k, _):
            to, last = shifted(k), shifted(k + self.shards - 1)
            for c in range(blocks):
                now, past = (self.even, self.odd) if c % 2 == 0 else (self.odd, self.even)
                self.finish(past, *((to, part * blocks + c - 1) if c else (last, part * blocks + blocks - 1)))
                for u in range(BLOCK):
                    now[u : u + 1, :] = self.table[pl.ds(self.ask_ref[to, part * blocks + c, u], 1), :]
                if c == 0:
                    if self.own is not None:

                        @pl.when(k == 1)
                        def _():
                            self.kept(part).start()

                    @pl.when(k > 1)
                    def _():
                        self.copy(part, last, self.me).start()

            return 0

        lax.fori_loop(0, self.shards, one, 0)
        last = shifted(self.shards - 1)
        self.finish(self.odd, last, part * blocks + blocks - 1)
        self.copy(part, last, self.me).start()

    def wait(self, part, arrived=None):
        def end(k, _):
            by = shifted(k, True)
            self.copy(part, self.me, by).wait_recv()
            if arrived is not None:
                arrived(by)
            self.copy(part, shifted(k), self.me).wait_send()
            return 0

        lax.fori_loop(1, self.shards, end, 0)
        if self.own is not None:
            self.kept(part).wait()


def greet():
    shards = lax.axis_size("gauss")
    me = lax.axis_index("gauss")
    barrier = pltpu.get_barrier_semaphore()

    def hail(k, _):
        pl.semaphore_signal(
            barrier, inc=1, device_id={"gauss": lax.rem(me + k, shards)}, device_id_type=pl.DeviceIdType.MESH
        )
        return 0

    lax.fori_loop(1, shards, hail, 0)
    beside = 1 - lax.axis_index("view")
    pl.semaphore_signal(barrier, inc=1, device_id={"view": beside}, device_id_type=pl.DeviceIdType.MESH)
    pl.semaphore_wait(barrier, shards)


class Tile:
    def __init__(self, t, cot_ref, images_ref, grads, rows, earlier, later, scratch):
        self.t, self.cot_ref, self.images_ref, self.grads, self.rows = t, cot_ref, images_ref, grads, rows
        self.earlier, self.later = earlier, later
        self.turned, self.alpha, self.ratio, self.parts, self.sums, self.weight, self.high, self.low, self.pull = scratch
        self.length = rows.shape[0]
        self.half = self.length // 2

    def put(self, at, x):
        half = self.half
        high, low = split(x)
        high, low = high.astype(BF16), low.astype(BF16)
        self.parts[pl.ds(at, TILE_SIDE), 0:half] = high[:, 0:half]
        self.parts[pl.ds(at, TILE_SIDE), half : 2 * half] = low[:, 0:half]
        self.parts[pl.ds(at, TILE_SIDE), 2 * half : 3 * half] = high[:, half:]
        self.parts[pl.ds(at, TILE_SIDE), 3 * half : 4 * half] = low[:, half:]

    def turn(self):
        self.turned[...] = self.rows[...].T[0:WIRE]

    def shape(self):
        turned = self.turned
        self.x0, self.y0, r2, r3, r4, r5 = (turned[k : k + 1, :] for k in range(GEOM))
        self.conic_a = jnp.exp(r2)
        self.conic_c = jnp.exp(r4)
        self.skew = jnp.tanh(r3)
        self.middle = jnp.sqrt(self.conic_a * self.conic_c)
        self.conic_b = 0.9 * self.skew * self.middle
        self.opaque = 1.0 / (1.0 + jnp.exp(-r5))
        spot = iota((TILE_SIDE, self.length), 0).astype(F32) + 0.5
        self.dx = spot - self.x0
        self.dy = spot - self.y0
        scale = -0.5 * LOG2E
        self.part_x = (scale * self.conic_a) * self.dx * self.dx
        self.cross = (2.0 * scale * self.conic_b) * self.dx
        self.part_y = (scale * self.conic_c) * self.dy * self.dy + jnp.log2(0.99 * self.opaque)

    def alphas(self, py):
        at = py * TILE_SIDE
        a = jnp.exp2(self.part_x + (self.cross * self.dy[py : py + 1] + self.part_y[py : py + 1]))
        log = jnp.log2(1.0 - a)
        self.alpha[pl.ds(at, TILE_SIDE), :] = a
        self.ratio[pl.ds(at, TILE_SIDE), :] = a * jnp.exp2(-log)
        self.put(at, log)

    def prefix(self):
        half = self.half
        self.sums[:, 0:half] = dot(self.parts[:, 0 : 2 * half], self.earlier[...])
        self.sums[:, half:] = dot(self.parts[:, 2 * half :], self.earlier[...])

    def weights(self, py):
        at, half = py * TILE_SIDE, self.half
        b = self.sums[pl.ds(at, TILE_SIDE), :]
        last = (
            b[:, half - 1 : half]
            + self.parts[pl.ds(at, TILE_SIDE), half - 1 : half].astype(F32)
            + self.parts[pl.ds(at, TILE_SIDE), 2 * half - 1 : 2 * half].astype(F32)
        )
        b = jnp.concatenate([b[:, 0:half], b[:, half:] + last], axis=1)
        w = jnp.exp2(b) * self.alpha[pl.ds(at, TILE_SIDE), :]
        high, low = split(w)
        self.weight[pl.ds(at, TILE_SIDE), :] = w
        self.high[pl.ds(at, TILE_SIDE), :] = high.astype(BF16)
        self.low[pl.ds(at, TILE_SIDE), :] = low.astype(BF16)

    def products(self):
        channel = iota((WIRE, self.length), 0)
        colour = jnp.where((channel >= GEOM) & (channel < SENT), self.turned[...], 0.0)
        colour_hi, colour_lo = split(colour)
        cot = jnp.concatenate(
            [jnp.zeros((GEOM, PIXELS), F32), self.cot_ref[self.t], jnp.zeros((WIRE - SENT, PIXELS), F32)], axis=0
        )
        cot_hi, cot_lo = split(cot)
        fill = jnp.zeros((128 - 3 * WIRE, self.length), F32)
        fill_cot = jnp.zeros((128 - 3 * WIRE, PIXELS), F32)
        three = jnp.concatenate([cot_hi, cot_lo, cot_hi, fill_cot], axis=0).T.astype(BF16)
        other = jnp.concatenate([colour_hi, colour_hi, colour_lo, fill], axis=0).astype(BF16)
        self.pull[...] = dot(three, other)
        both = jnp.concatenate([colour_hi, colour_lo], axis=0).astype(BF16)
        image = dot(both, self.high[...], ((1,), (1,)))
        image_lo = dot(both[0:48], self.low[...], ((1,), (1,)))
        image = image[0:WIRE] + image[WIRE:] + image_lo[0:WIRE]
        self.images_ref[self.t] = image[GEOM:SENT]
        both = jnp.concatenate([cot_hi, cot_lo], axis=0).astype(BF16)
        grad = dot(both, self.high[...])
        grad_lo = dot(both[0:48], self.low[...])
        self.turned[...] = grad[0:WIRE] + grad[WIRE:] + grad_lo[0:WIRE]

    def terms(self, py):
        at = py * TILE_SIDE
        q = self.pull[pl.ds(at, TILE_SIDE), :] * self.weight[pl.ds(at, TILE_SIDE), :]
        self.pull[pl.ds(at, TILE_SIDE), :] = q
        self.put(at, q)

    def suffix(self):
        half = self.half
        self.sums[:, 0:half] = dot(self.parts[:, 0 : 2 * half], self.later[...])
        self.sums[:, half:] = dot(self.parts[:, 2 * half :], self.later[...])

    def moments(self, py):
        at, half = py * TILE_SIDE, self.half
        s = self.sums[pl.ds(at, TILE_SIDE), :]
        q = self.pull[pl.ds(at, TILE_SIDE), :]
        first = s[:, half : half + 1] + q[:, half : half + 1]
        s = jnp.concatenate([s[:, 0:half] + first, s[:, half:]], axis=1)
        h = q - s * self.ratio[pl.ds(at, TILE_SIDE), :]
        hy = h * self.dy[py : py + 1]
        hyy = hy * self.dy[py : py + 1]
        if py == 0:
            self.m0, self.m1, self.m2 = h, hy, hyy
        else:
            self.m0, self.m1, self.m2 = self.m0 + h, self.m1 + hy, self.m2 + hyy

    def close(self):
        def total(x):
            return jnp.sum(x, axis=0, keepdims=True)

        m0x = self.m0 * self.dx
        s0, sx, sy = total(self.m0), total(m0x), total(self.m1)
        sxx, sxy, syy = total(m0x * self.dx), total(self.m1 * self.dx), total(self.m2)
        shared = -0.5 * self.conic_b * sxy
        geometry = (
            self.conic_a * sx + self.conic_b * sy,
            self.conic_b * sx + self.conic_c * sy,
            shared - 0.5 * self.conic_a * sxx,
            -0.9 * (1.0 - self.skew * self.skew) * self.middle * sxy,
            shared - 0.5 * self.conic_c * syy,
            (1.0 - self.opaque) * s0,
        )
        grad = self.turned[...]
        channel = iota(grad.shape, 0)
        for k, value in enumerate(geometry):
            grad = jnp.where(channel == k, value, grad)
        at = pl.multiple_of(self.t * self.length, self.length)
        self.grads[pl.ds(at, self.length), 0:WIRE] = grad.T


def paint(slot_ref, cot_ref, images_ref, table, grads, rows, earlier, later, scratch, between):
    tiles = cot_ref.shape[0]
    length = rows[0].shape[0]
    blocks = length // BLOCK
    half = length // 2
    above = iota((2 * half, half), 0) % half
    beside = iota((2 * half, half), 1)
    earlier[...] = (above < beside).astype(F32).astype(BF16)
    later[...] = (above > beside).astype(F32).astype(BF16)

    def pick(into, t, start, count):
        for u in range(start, start + count):
            into[u : u + 1, :] = table[pl.ds(slot_ref[t * blocks + u // BLOCK, u % BLOCK], 1), :]

    pick(rows[0], 0, 0, length)
    pick(rows[1], 1, 0, length)

    def two(i, _):
        for share, read, step in between:

            @pl.when(i == int(tiles * share) // 2)
            def _(read=read, step=step):
                step()
                if read:

                    def again(j, _):
                        at = pl.multiple_of(j * BLOCK, BLOCK)
                        for k in range(2):
                            for u in range(BLOCK):
                                rows[k][pl.ds(at + u, 1), :] = table[
                                    pl.ds(slot_ref[(2 * i + k) * blocks + j, u], 1), :
                                ]
                        return 0

                    lax.fori_loop(0, blocks, again, 0)

        a, b = (
            Tile(2 * i + k, cot_ref, images_ref, grads, rows[k], earlier, later, scratch[k]) for k in range(2)
        )
        following = [jnp.minimum(2 * i + 2 + k, tiles - 1) for k in range(2)]
        todo = [(k, start) for start in range(0, length, PICKS) for k in range(2)]

        def more():
            if todo:
                k, start = todo.pop(0)
                pick(rows[k], following[k], start, PICKS)

        def sweep(step):
            for py in range(TILE_SIDE):
                step(py)
                more()

        a.turn()
        b.turn()
        a.shape()
        sweep(a.alphas)
        a.prefix()
        b.shape()
        sweep(b.alphas)
        b.prefix()
        sweep(a.weights)
        a.products()
        sweep(b.weights)
        b.products()
        sweep(a.terms)
        a.suffix()
        sweep(b.terms)
        b.suffix()
        sweep(a.moments)
        a.close()
        sweep(b.moments)
        b.close()
        while todo:
            more()
        return 0

    lax.fori_loop(0, tiles // 2, two, 0)


def paint_scratch(length):
    full = (PIXELS, length)
    one = [
        VMEM((WIRE, length), F32),
        VMEM(full, F32),
        VMEM(full, F32),
        VMEM((PIXELS, 2 * length), BF16),
        VMEM(full, F32),
        VMEM(full, F32),
        VMEM(full, BF16),
        VMEM(full, BF16),
        VMEM(full, F32),
    ]
    return [VMEM((length, 128), F32)] * 2 + [VMEM((length, length // 2), BF16)] * 2 + one + one


def render_kernel(
    slot_ref, entry_ref, ask_ref, used_ref, rows_ref, cot_ref,
    images_ref, back_ref, named_ref, cos_ref, clash_ref, void_ref,
    held, table, asked_ref, asked, ask_send, ask_recv, own_sem, even, odd, send, got,
    send_sem, recv_sem, back_send, back_recv, kept_sem, here, there, void_sem, grads, *scratch,
):
    width, columns = held.shape
    shards = send.shape[0]
    blocks = send.shape[1] // PITCH
    me = lax.axis_index("gauss")
    load = pltpu.make_async_copy(rows_ref, held, own_sem)
    load.start()
    greet()

    def copy(to, by):
        return remote(ask_ref.at[to], asked_ref.at[by], ask_send.at[to], ask_recv.at[by], to)

    def ask(k, _):
        copy(shifted(k), me).start()
        return 0

    lax.fori_loop(1, shards, ask, 0)
    load.wait()

    def turn(i, _):
        at = pl.multiple_of(i * 512, 512)
        table[pl.ds(at, 512), 0:width] = held[:, pl.ds(at, 512)].T
        return 0

    lax.fori_loop(0, columns // 512, turn, 0)
    asked_ref[me] = ask_ref[me]

    def end(k, _):
        copy(shifted(k), me).wait_send()
        copy(me, shifted(k, True)).wait_recv()
        return 0

    lax.fori_loop(1, shards, end, 0)
    for c in range(blocks):
        named_ref[:, c, :] = asked_ref[:, c, :]
    down = pltpu.make_async_copy(named_ref, asked, own_sem)
    down.start()
    void = jnp.zeros((1, 1), F32)
    for c in range(blocks):
        row = asked_ref[:, c, :]
        view = asked_ref[:, blocks + c, :]
        cos = jnp.zeros(view.shape, F32)
        for v, value in enumerate(view_cosines()):
            cos = jnp.where(view == v, value, cos)
        cos_ref[:, c, :] = cos
        void = jnp.maximum(void, jnp.max((view == VIEWS).astype(F32), axis=(0, 1), keepdims=True))
        lane = iota(row.shape, 1) % GROUP
        same = jnp.zeros(row.shape, F32)
        for d in range(1, GROUP):
            same = jnp.where((pltpu.roll(row, d, 1) == row) & (lane >= d), 1.0, same)
        clash_ref[:, c : c + 1] = jnp.max(same, axis=1, keepdims=True).astype(I32)
    here[...] = jnp.broadcast_to(void, here.shape)
    beside = 1 - lax.axis_index("view")
    tell = pltpu.make_async_remote_copy(
        src_ref=here,
        dst_ref=there,
        send_sem=void_sem.at[0],
        recv_sem=void_sem.at[1],
        device_id={"view": beside},
        device_id_type=pl.DeviceIdType.MESH,
    )
    tell.start()
    down.wait()

    def blend(rows, to, c):
        turned = rows[...].T
        second = jnp.concatenate([jnp.zeros((GEOM, BLOCK), F32), turned[SENT : SENT + CHANNELS]], axis=0)
        send[to, c * PITCH : c * PITCH + SENT, :] = turned[0:SENT] + cos_ref[to, c : c + 1, :] * second

    def unpack(source, by, part):
        for c in range(part * blocks // REGIONS, (part + 1) * blocks // REGIONS):
            at = pl.multiple_of((by * blocks + c) * BLOCK, BLOCK)
            table[pl.ds(at, BLOCK), 0:SENT] = source[by, c * PITCH : c * PITCH + SENT, :].T

    out = Exchange(asked, blend, table, even, odd, send, got, send_sem, recv_sem)

    def take(part):
        out.wait(part, lambda by: unpack(got, by, part))
        unpack(send, me, part)

    def mask(rows, to, c):
        used = used_ref[to, c : c + 1, :] > 0
        send[to, c * PITCH : c * PITCH + SENT, :] = jnp.where(used, rows[...].T[0:SENT], 0.0)

    back = Exchange(entry_ref, mask, grads, even, odd, send, back_ref, back_send, back_recv, kept_sem)
    out.start(0)
    out.start(1)
    take(0)
    between = ((FIRST, True, lambda: take(1)), (SECOND, False, lambda: back.start(0)))
    tiles = scratch[4:13], scratch[13:22]
    paint(slot_ref, cot_ref, images_ref, table, grads, scratch[0:2], scratch[2], scratch[3], tiles, between)
    back.start(1)
    back.wait(0)
    back.wait(1)
    tell.wait()
    void_ref[...] = jnp.maximum(here[...], there[...]).astype(I32)


def render(slot, entry, used, ask, gauss_rows, cot):
    shards = ask.shape[0]
    blocks = ask.shape[1] // 2
    width, columns = gauss_rows.shape
    tiles = cot.shape[0]
    length = slot.size // tiles
    wire = (shards, blocks * PITCH, BLOCK)
    sems = pltpu.SemaphoreType.DMA((shards,))
    pairs = pltpu.SemaphoreType.DMA((REGIONS, shards))
    return pl.pallas_call(
        render_kernel,
        out_shape=(
            jax.ShapeDtypeStruct((tiles, CHANNELS, PIXELS), F32),
            jax.ShapeDtypeStruct(wire, F32),
            jax.ShapeDtypeStruct(entry.shape, I32),
            jax.ShapeDtypeStruct(entry.shape, F32),
            jax.ShapeDtypeStruct((shards, 128), I32),
            jax.ShapeDtypeStruct((8, 128), I32),
        ),
        in_specs=[whole(SMEM), whole(SMEM), whole(VMEM), whole(VMEM), whole(pl.ANY), whole(VMEM)],
        out_specs=(whole(VMEM), whole(pl.ANY), whole(VMEM), whole(VMEM), whole(VMEM), whole(VMEM)),
        scratch_shapes=[
            VMEM((width, columns), F32),
            VMEM((columns, 128), F32),
            VMEM(ask.shape, I32),
            SMEM(entry.shape, I32),
            sems,
            sems,
            pltpu.SemaphoreType.DMA,
            VMEM((BLOCK, 128), F32),
            VMEM((BLOCK, 128), F32),
            VMEM(wire, F32),
            VMEM(wire, F32),
            pairs,
            pairs,
            pairs,
            pairs,
            pltpu.SemaphoreType.DMA((REGIONS,)),
            VMEM((8, 128), F32),
            VMEM((8, 128), F32),
            pltpu.SemaphoreType.DMA((2,)),
            VMEM((tiles * length, 128), F32),
        ]
        + paint_scratch(length),
        compiler_params=params(collective_id=0, has_side_effects=True),
        name="render",
    )(slot, entry, ask, used, gauss_rows, cot)


def collect_kernel(
    half_ref, ask_ref, clash_ref, cos_ref, wire_ref, keep_ref, send_ref, table, table2, even, odd, wide, sems
):
    step_id = pl.program_id(0)
    sources = wire_ref.shape[0]
    width, half = keep_ref.shape
    blocks = wire_ref.shape[1] // PITCH
    step = 512

    @pl.when(step_id == 0)
    def _():
        table[...] = jnp.zeros_like(table)
        table2[...] = jnp.zeros_like(table2)
        even[...] = jnp.zeros_like(even)
        odd[...] = jnp.zeros_like(odd)

    def turn(s, c, rows):
        back = wire_ref[s, c * PITCH : c * PITCH + SENT, :]
        scaled = cos_ref[s, c : c + 1, :] * back
        rows[:, 0:width] = jnp.concatenate([back, scaled[GEOM:SENT]], axis=0).T

    def add(at, c, rows):
        for g in range(BLOCK // GROUP):
            into = (table, table2)[g % 2]
            places = [ask_ref[at, c, g * GROUP + u] for u in range(GROUP)]
            sums = [into[pl.ds(r, 1), :] + rows[g * GROUP + u : g * GROUP + u + 1, :] for u, r in enumerate(places)]
            for r, value in zip(places, sums):
                into[pl.ds(r, 1), :] = value

    def add_slowly(at, c, rows):
        for u in range(BLOCK):
            into = (table, table2)[u % 2]
            into[pl.ds(ask_ref[at, c, u], 1), :] += rows[u : u + 1, :]

    def finish(at, c, rows, more):
        def quick():
            more()
            add(at, c, rows)

        def careful():
            more()
            add_slowly(at, c, rows)

        lax.cond(clash_ref[at, c] == 0, quick, careful)

    def one(s, _):
        source = step_id * sources + s
        for c in range(blocks):
            now, past = (even, odd) if c % 2 == 0 else (odd, even)
            at = source if c else jnp.maximum(source - 1, 0)
            finish(at, (c - 1) % blocks, past, functools.partial(turn, s, c, now))
        return 0

    lax.fori_loop(0, sources, one, 0)

    @pl.when(step_id == pl.num_programs(0) - 1)
    def _():
        finish(pl.num_programs(0) * sources - 1, blocks - 1, odd, lambda: None)
        copies = []
        for ref, base in ((send_ref, half - half_ref[0]), (keep_ref, half_ref[0])):
            for part in range(COPIES):
                length = half // COPIES
                held = wide.at[len(copies)]

                def back(i, _):
                    at = pl.multiple_of(i * step, step)
                    there = pl.multiple_of(base + part * length + at, step)
                    both = table[pl.ds(there, step), :] + table2[pl.ds(there, step), :]
                    held[:, pl.ds(at, step)] = both.T[0:width]
                    return 0

                lax.fori_loop(0, length // step, back, 0)
                into = ref.at[:, pl.ds(part * length, length)]
                copies.append(pltpu.make_async_copy(held, into, sems.at[len(copies)]))
                copies[-1].start()
        for copy in copies:
            copy.wait()


def collect(half, asked, clash, cos, wire, width, columns):
    shards, sent, _ = wire.shape
    part = jax.ShapeDtypeStruct((width, columns // 2), F32)
    return pl.pallas_call(
        collect_kernel,
        grid=(shards // SOURCES,),
        out_shape=(part, part),
        in_specs=[
            whole(SMEM),
            whole(SMEM),
            whole(SMEM),
            pl.BlockSpec((SOURCES,) + cos.shape[1:], lambda i: (i, 0, 0)),
            pl.BlockSpec((SOURCES, sent, BLOCK), lambda i: (i, 0, 0)),
        ],
        out_specs=(whole(pl.ANY), whole(pl.ANY)),
        scratch_shapes=[
            VMEM((columns, 128), F32),
            VMEM((columns, 128), F32),
            VMEM((BLOCK, 128), F32),
            VMEM((BLOCK, 128), F32),
            VMEM((2 * COPIES, width, columns // 2 // COPIES), F32),
            pltpu.SemaphoreType.DMA((2 * COPIES,)),
        ],
        compiler_params=params(),
        name="collect",
    )(half, asked, clash, cos, wire)


def plain_composite(entry_params, view_cos, cotangent):
    pixel = jnp.arange(PIXELS)
    across = (pixel % TILE_SIDE).astype(jnp.float32) + 0.5
    down = (pixel // TILE_SIDE).astype(jnp.float32) + 0.5

    def render(params):
        off_x = across[None, :] - params[:, 0][:, None]
        off_y = down[None, :] - params[:, 1][:, None]
        conic_a = jnp.exp(params[:, 2])
        conic_c = jnp.exp(params[:, 4])
        conic_b = 0.9 * jnp.tanh(params[:, 3]) * jnp.sqrt(conic_a * conic_c)
        power = -0.5 * (
            conic_a[:, None] * off_x * off_x
            + 2.0 * conic_b[:, None] * off_x * off_y
            + conic_c[:, None] * off_y * off_y
        )
        alpha = 0.99 * jax.nn.sigmoid(params[:, 5])[:, None] * jnp.exp(power)
        logs = jnp.log(1.0 - alpha)
        before = jnp.cumsum(logs, axis=0) - logs
        weight = jnp.exp(before) * alpha
        colour = params[:, 6 : 6 + CHANNELS] + view_cos * params[:, 6 + CHANNELS : 6 + 2 * CHANNELS]
        return lax.dot_general(
            colour, weight, (((0,), (0,)), ((), ())), precision=lax.Precision.HIGHEST
        )

    image, pull = jax.vjp(render, entry_params)
    grads = pull(cotangent)
    return (image, grads[0])


def plain(gauss_rows, vis_shard, vis_row, tile_index, cotangent):
    shards = lax.axis_size("gauss")
    tiles, length = vis_row.shape
    entries = tiles * length
    capacity = 2 * entries // shards
    width = gauss_rows.shape[0]
    own_cols = gauss_rows.shape[1]
    shard_of = vis_shard.reshape(entries)
    row_of = vis_row.reshape(entries)
    hits = (shard_of[:, None] == jnp.arange(shards, dtype=jnp.int32)[None, :]).astype(jnp.int32)
    place = jnp.sum((jnp.cumsum(hits, axis=0) - 1) * hits, axis=1)
    slot_of = shard_of * capacity + place
    requests = (
        jnp.zeros((shards * capacity,), jnp.int32).at[slot_of].set(row_of).reshape(shards, capacity)
    )
    row_major = jnp.transpose(gauss_rows)
    asked = lax.all_to_all(requests, "gauss", split_axis=0, concat_axis=0, tiled=True)
    fetched = jnp.take(row_major, asked.reshape(-1), axis=0).reshape(
        asked.shape[0], asked.shape[1], width
    )
    sent = lax.all_to_all(fetched, "gauss", split_axis=0, concat_axis=0, tiled=True)
    entry_rows = jnp.take(sent.reshape(shards * capacity, width), slot_of, axis=0)
    tile_rows = entry_rows.reshape(tiles, length, width)
    view_cos = jnp.cos(TWO_PI * (tile_index // SCREEN_TILES).astype(jnp.float32) / VIEWS)

    def one_tile(packed):
        return plain_composite(packed[0], packed[1], packed[2])

    images, grads = lax.map(one_tile, (tile_rows, view_cos, cotangent), batch_size=4)
    entry_grads = grads.reshape(entries, width)
    outgoing = (
        jnp.zeros((shards * capacity, width), jnp.float32)
        .at[slot_of]
        .set(entry_grads)
        .reshape(shards, capacity, width)
    )
    returned = lax.all_to_all(outgoing, "gauss", split_axis=0, concat_axis=0, tiled=True)
    row_totals = (
        jnp.zeros((own_cols, width), jnp.float32)
        .at[asked.reshape(-1)]
        .add(returned.reshape(shards * capacity, width))
    )
    totals = jnp.transpose(row_totals)
    half = own_cols // 2
    summed = lax.psum(totals, "view")
    gradient = lax.dynamic_slice_in_dim(summed, lax.axis_index("view") * half, half, 1)
    return (images, gradient)


def per_device(gauss_rows, vis_shard, vis_row, tile_index, cotangent):
    shards = lax.axis_size("gauss")
    width, columns = gauss_rows.shape
    ask, entry, used, slot = route(tile_index, vis_shard.reshape(-1, BLOCK), vis_row, shards)
    images, returned, named, cos, clash, void = render(slot, entry, used, ask, gauss_rows, cotangent)

    def quick():
        half = (lax.axis_index("view") * (columns // 2)).astype(I32).reshape(1)
        keep, send = collect(half, named, clash, cos, returned, width, columns)
        other = lax.ppermute(send, "view", [(0, 1), (1, 0)])
        return (images, keep + other)

    def careful():
        return plain(gauss_rows, vis_shard, vis_row, tile_index, cotangent)

    return lax.cond(void[0, 0] == 0, quick, careful)


def solution(mesh):
    placed = (
        P(None, "gauss"),
        P(("gauss", "view"), None, None),
        P(("gauss", "view"), None),
        P(("gauss", "view")),
        P(("gauss", "view"), None, None),
    )
    return jax.shard_map(
        per_device,
        mesh=mesh,
        in_specs=placed,
        out_specs=(P(("gauss", "view"), None, None), P(None, ("gauss", "view"))),
        check_vma=False,
    )
```

```python
import functools
import math

import jax
import jax.numpy as jnp
from jax import lax
from jax.experimental import pallas as pl
from jax.experimental.pallas import tpu as pltpu
from jax.sharding import PartitionSpec as P

CHANNELS = 29
TILE_SIDE = 16
PIXELS = 256
VIEWS = 8
SCREEN_TILES = 8160
GEOM = 6
SENT = 35
WIRE = 40
TWO_PI = 6.283185307179586
LOG2E = 1.4426950408889634
VMEM = pltpu.VMEM
SMEM = pltpu.SMEM
F32 = jnp.float32
BF16 = jnp.bfloat16
I32 = jnp.int32
GROUP = 8
BLOCK = 128
LEAVE = (3 / 8, 5 / 8, 7 / 8)
READ = 2
SOURCES = 8
COPIES = 4
PICKS = 8


def params(**more):
    return pltpu.CompilerParams(vmem_limit_bytes=60 * 2**20, **more)


def whole(space):
    return pl.BlockSpec(memory_space=space)


def iota(shape, dim):
    return lax.broadcasted_iota(I32, shape, dim)


def dot(a, b, contract=((1,), (0,))):
    return lax.dot_general(a, b, (contract, ((), ())), preferred_element_type=F32)


def view_cosines():
    return [math.cos(TWO_PI * v / VIEWS) for v in range(VIEWS)]


def split(x):
    high = x.astype(BF16).astype(F32)
    return high, x - high


def route_kernel(tile_ref, shard_ref, row_ref, ask_ref, entry_ref, used_ref, slot_ref, carry_ref, early_ref):
    shards = ask_ref.shape[0]
    tiles, length = row_ref.shape
    tile_blocks = length // BLOCK
    width = 256
    parts = length // width
    capacity = 2 * tiles * length // shards
    blocks = capacity // BLOCK
    leave = [int(tiles * share) // 2 for share in LEAVE]
    before = (iota((width, width), 0) < iota((width, width), 1)).astype(F32).astype(BF16)
    lane = iota((1, width), 1).astype(F32)

    def some(i, state):
        total = state
        carry = carry_ref[...]
        early_ref[...] = jnp.maximum(early_ref[...], carry * jnp.where(i == leave[0], 1.0, 0.0))
        least = sum(jnp.where(i == pair, float((n + 1) * BLOCK), 0.0) for n, pair in enumerate(leave))
        carry = jnp.maximum(carry, least)
        spots = [(2 * i + u // parts, u % parts) for u in range(2 * parts)]
        shard = [
            jnp.concatenate(
                [shard_ref[pl.ds(t * tile_blocks + h * (width // BLOCK) + b, 1), :] for b in range(width // BLOCK)],
                axis=1,
            )
            for t, h in spots
        ]
        hot = [(iota((shards, width), 0) == one).astype(F32) for one in shard]
        seen = dot(jnp.concatenate(hot, axis=0).astype(BF16), before)
        at, values = [], []
        for u, (t, h) in enumerate(spots):
            place = jnp.sum(hot[u] * (seen[shards * u : shards * (u + 1)] + carry), axis=0, keepdims=True)
            carry = carry + jnp.broadcast_to(jnp.sum(hot[u], axis=1, keepdims=True), hot[u].shape)
            place = place.astype(I32)
            slot = shard[u] * capacity + jnp.minimum(place, capacity - 1)
            for b in range(width // BLOCK):
                slot_ref[pl.ds(t * tile_blocks + h * (width // BLOCK) + b, 1), :] = slot[
                    :, b * BLOCK : (b + 1) * BLOCK
                ]
            at.append((iota((capacity, width), 0) == place).astype(F32).astype(BF16))
            row = row_ref[pl.ds(t, 1), h * width : (h + 1) * width]
            parts_of = (
                (row & 255).astype(F32),
                (row >> 8).astype(F32),
                sum(
                    (jnp.full((1, width), tile_ref[t], I32) >= SCREEN_TILES * v).astype(F32) for v in range(VIEWS)
                ),
                lane,
                jnp.full((1, width), t * parts + h, I32).astype(F32),
            )
            values.append(jnp.concatenate([hot[u] * part for part in parts_of], axis=0).astype(BF16))
        at = jnp.concatenate(at, axis=1)
        values = jnp.concatenate(values, axis=1)
        carry_ref[...] = carry
        return total + dot(values, at, ((1,), (1,)))

    carry_ref[...] = jnp.zeros_like(carry_ref)
    early_ref[...] = jnp.zeros_like(early_ref)
    total = lax.fori_loop(0, tiles // 2, some, jnp.zeros((5 * shards, capacity), F32))
    over = (early_ref[...] > float(READ * BLOCK)) | (carry_ref[...] > float(capacity))
    over = jnp.max(over.astype(F32), axis=(0, 1), keepdims=True)
    low, high, view, lane, chunk = (total[shards * k : shards * (k + 1)].astype(I32) for k in range(5))
    used = view > 0
    row = jnp.where(used, low + 256 * high, iota((shards, capacity), 1))
    view = jnp.where(over > 0.0, VIEWS, jnp.where(used, view - 1, 0))
    entry = lane + width * chunk
    used = used.astype(I32)
    for c in range(blocks):
        lanes = slice(c * BLOCK, (c + 1) * BLOCK)
        ask_ref[:, c, :] = row[:, lanes]
        ask_ref[:, blocks + c, :] = view[:, lanes]
        entry_ref[:, c, :] = entry[:, lanes]
        used_ref[:, c, :] = used[:, lanes]


def route(tile, shard, row, shards):
    tiles, length = row.shape
    blocks = 2 * tiles * length // shards // BLOCK
    lists = jax.ShapeDtypeStruct((shards, blocks, BLOCK), I32)
    return pl.pallas_call(
        route_kernel,
        out_shape=(
            jax.ShapeDtypeStruct((shards, 2 * blocks, BLOCK), I32),
            lists,
            lists,
            jax.ShapeDtypeStruct((tiles * length // BLOCK, BLOCK), I32),
        ),
        in_specs=[whole(SMEM), whole(VMEM), whole(VMEM)],
        out_specs=(whole(VMEM),) * 4,
        scratch_shapes=[VMEM((shards, 256), F32)] * 2,
        compiler_params=params(),
        name="route",
    )(tile, shard, row)


class Partners:
    def __init__(self):
        self.shards = lax.axis_size("gauss")
        self.side = round(self.shards ** (1 / 3))
        self.me = lax.axis_index("gauss")
        self.units = (self.side * self.side, self.side, 1)
        self.here = [lax.rem(lax.div(self.me, jnp.int32(unit)), self.side) + self.side for unit in self.units]
        self.sign = 1 - 2 * lax.axis_index("view")

    def __call__(self, k):
        step = lax.rem(37 * k, self.shards)
        to = 0
        for unit, here in zip(self.units, self.here):
            by = lax.div(step, jnp.int32(unit)) if unit > 1 else step
            by = lax.rem(by, self.side) if unit < self.side * self.side else by
            to = to + lax.rem(here + self.sign * by, self.side) * unit
        return to

    def any(self, k):
        return lax.rem(self.me + k, self.shards)


def remote(src, dst, send_sem, recv_sem, to):
    return pltpu.make_async_remote_copy(
        src_ref=src,
        dst_ref=dst,
        send_sem=send_sem,
        recv_sem=recv_sem,
        device_id={"gauss": to},
        device_id_type=pl.DeviceIdType.MESH,
    )


class Exchange:
    def __init__(self, ask_ref, finish, table, even, odd, send, to_ref, send_sem, recv_sem, blocks, own=None):
        self.ask_ref, self.finish, self.table, self.buffers = ask_ref, finish, table, (even, odd)
        self.send, self.to_ref, self.send_sem, self.recv_sem, self.own = send, to_ref, send_sem, recv_sem, own
        self.blocks = blocks
        self.partner = Partners()
        self.shards, self.me = self.partner.shards, self.partner.me

    def piece(self, ref, shard, part):
        return ref.at[shard] if part is None else ref.at[shard, pl.ds(part * self.blocks, self.blocks)]

    def copy(self, part, to, by):
        send_sem, recv_sem = self.send_sem, self.recv_sem
        if self.own is None:
            send_sem, recv_sem = send_sem.at[part], recv_sem.at[part]
        return remote(
            self.piece(self.send, to, part), self.piece(self.to_ref, by, part), send_sem.at[to], recv_sem.at[by], to
        )

    def kept(self, part):
        return pltpu.make_async_copy(
            self.piece(self.send, self.me, part), self.piece(self.to_ref, self.me, part), self.own
        )

    def leave(self, part, k, to):
        if self.own is not None:

            @pl.when(k == 0)
            def _():
                self.kept(part).start()

        @pl.when(k > 0)
        def _():
            self.copy(part, to, self.me).start()

    def start(self, part):
        blocks, base = self.blocks, part * self.blocks

        def some(i, last):
            for n in range(2):
                k, c = (2 * i + n, 0) if blocks == 1 else (i, n)
                to = self.partner(k) if c == 0 else to
                now, past = self.buffers[n], self.buffers[1 - n]
                self.finish(past, *((to, base + c - 1) if c else (last, base + blocks - 1)))
                for u in range(0, BLOCK, 8):
                    picked = [self.table[pl.ds(self.ask_ref[to, base + c, u + v], 1), :] for v in range(8)]
                    now[u : u + 8, :] = jnp.concatenate(picked, axis=0)
                if c == 0:
                    pl.when(k > 0)(functools.partial(self.leave, part, k - 1, last))
                if c == blocks - 1:
                    last = to
            return last

        last = lax.fori_loop(0, self.shards * blocks // 2, some, self.me)
        self.finish(self.buffers[1], last, base + blocks - 1)
        self.copy(part, last, self.me).start()

    def wait(self, part=None, arrived=None):
        def end(k, _):
            by = self.partner.any(k)
            self.copy(part, self.me, by).wait_recv()
            if arrived is not None:
                arrived(by)
            self.copy(part, by, self.me).wait_send()
            return 0

        lax.fori_loop(1, self.shards, end, 0)
        if self.own is not None:
            self.kept(part).wait()


def greet():
    shards = lax.axis_size("gauss")
    me = lax.axis_index("gauss")
    barrier = pltpu.get_barrier_semaphore()

    def hail(k, _):
        pl.semaphore_signal(
            barrier, inc=1, device_id={"gauss": lax.rem(me + k, shards)}, device_id_type=pl.DeviceIdType.MESH
        )
        return 0

    lax.fori_loop(1, shards, hail, 0)
    beside = 1 - lax.axis_index("view")
    pl.semaphore_signal(barrier, inc=1, device_id={"view": beside}, device_id_type=pl.DeviceIdType.MESH)
    pl.semaphore_wait(barrier, shards)


class Tile:
    def __init__(self, t, cot_ref, images_ref, grads, rows, earlier, later, scratch):
        self.t, self.cot_ref, self.images_ref, self.grads, self.rows = t, cot_ref, images_ref, grads, rows
        self.earlier, self.later = earlier, later
        self.turned, self.alpha, self.ratio, self.parts, self.sums, self.weight, self.high, self.low, self.pull = scratch
        self.length = rows.shape[0]
        self.half = self.length // 2

    def put(self, at, x):
        half = self.half
        high, low = split(x)
        high, low = high.astype(BF16), low.astype(BF16)
        self.parts[pl.ds(at, TILE_SIDE), 0:half] = high[:, 0:half]
        self.parts[pl.ds(at, TILE_SIDE), half : 2 * half] = low[:, 0:half]
        self.parts[pl.ds(at, TILE_SIDE), 2 * half : 3 * half] = high[:, half:]
        self.parts[pl.ds(at, TILE_SIDE), 3 * half : 4 * half] = low[:, half:]

    def turn(self):
        self.turned[...] = self.rows[...].T[0:WIRE]

    def shape(self):
        turned = self.turned
        self.x0, self.y0, r2, r3, r4, r5 = (turned[k : k + 1, :] for k in range(GEOM))
        self.conic_a = jnp.exp(r2)
        self.conic_c = jnp.exp(r4)
        self.skew = jnp.tanh(r3)
        self.middle = jnp.sqrt(self.conic_a * self.conic_c)
        self.conic_b = 0.9 * self.skew * self.middle
        self.opaque = 1.0 / (1.0 + jnp.exp(-r5))
        spot = iota((TILE_SIDE, self.length), 0).astype(F32) + 0.5
        self.dx = spot - self.x0
        self.dy = spot - self.y0
        scale = -0.5 * LOG2E
        self.part_x = (scale * self.conic_a) * self.dx * self.dx
        self.cross = (2.0 * scale * self.conic_b) * self.dx
        self.part_y = (scale * self.conic_c) * self.dy * self.dy + jnp.log2(0.99 * self.opaque)

    def alphas(self, py):
        at = py * TILE_SIDE
        a = jnp.exp2(self.part_x + (self.cross * self.dy[py : py + 1] + self.part_y[py : py + 1]))
        log = jnp.log2(1.0 - a)
        self.alpha[pl.ds(at, TILE_SIDE), :] = a
        self.ratio[pl.ds(at, TILE_SIDE), :] = a * jnp.exp2(-log)
        self.put(at, log)

    def prefix(self):
        half = self.half
        self.sums[:, 0:half] = dot(self.parts[:, 0 : 2 * half], self.earlier[...])
        self.sums[:, half:] = dot(self.parts[:, 2 * half :], self.earlier[...])

    def weights(self, py):
        at, half = py * TILE_SIDE, self.half
        b = self.sums[pl.ds(at, TILE_SIDE), :]
        last = (
            b[:, half - 1 : half]
            + self.parts[pl.ds(at, TILE_SIDE), half - 1 : half].astype(F32)
            + self.parts[pl.ds(at, TILE_SIDE), 2 * half - 1 : 2 * half].astype(F32)
        )
        b = jnp.concatenate([b[:, 0:half], b[:, half:] + last], axis=1)
        w = jnp.exp2(b) * self.alpha[pl.ds(at, TILE_SIDE), :]
        high, low = split(w)
        self.weight[pl.ds(at, TILE_SIDE), :] = w
        self.high[pl.ds(at, TILE_SIDE), :] = high.astype(BF16)
        self.low[pl.ds(at, TILE_SIDE), :] = low.astype(BF16)

    def products(self):
        channel = iota((WIRE, self.length), 0)
        colour = jnp.where((channel >= GEOM) & (channel < SENT), self.turned[...], 0.0)
        colour_hi, colour_lo = split(colour)
        cot = jnp.concatenate(
            [jnp.zeros((GEOM, PIXELS), F32), self.cot_ref[self.t], jnp.zeros((WIRE - SENT, PIXELS), F32)], axis=0
        )
        cot_hi, cot_lo = split(cot)
        fill = jnp.zeros((128 - 3 * WIRE, self.length), F32)
        fill_cot = jnp.zeros((128 - 3 * WIRE, PIXELS), F32)
        three = jnp.concatenate([cot_hi, cot_lo, cot_hi, fill_cot], axis=0).T.astype(BF16)
        other = jnp.concatenate([colour_hi, colour_hi, colour_lo, fill], axis=0).astype(BF16)
        self.pull[...] = dot(three, other)
        both = jnp.concatenate([colour_hi, colour_lo], axis=0).astype(BF16)
        image = dot(both, self.high[...], ((1,), (1,)))
        image_lo = dot(both[0:48], self.low[...], ((1,), (1,)))
        image = image[0:WIRE] + image[WIRE:] + image_lo[0:WIRE]
        self.images_ref[self.t] = image[GEOM:SENT]
        both = jnp.concatenate([cot_hi, cot_lo], axis=0).astype(BF16)
        grad = dot(both, self.high[...])
        grad_lo = dot(both[0:48], self.low[...])
        self.turned[...] = grad[0:WIRE] + grad[WIRE:] + grad_lo[0:WIRE]

    def terms(self, py):
        at = py * TILE_SIDE
        q = self.pull[pl.ds(at, TILE_SIDE), :] * self.weight[pl.ds(at, TILE_SIDE), :]
        self.pull[pl.ds(at, TILE_SIDE), :] = q
        self.put(at, q)

    def suffix(self):
        half = self.half
        self.sums[:, 0:half] = dot(self.parts[:, 0 : 2 * half], self.later[...])
        self.sums[:, half:] = dot(self.parts[:, 2 * half :], self.later[...])

    def moments(self, py):
        at, half = py * TILE_SIDE, self.half
        s = self.sums[pl.ds(at, TILE_SIDE), :]
        q = self.pull[pl.ds(at, TILE_SIDE), :]
        first = s[:, half : half + 1] + q[:, half : half + 1]
        s = jnp.concatenate([s[:, 0:half] + first, s[:, half:]], axis=1)
        h = q - s * self.ratio[pl.ds(at, TILE_SIDE), :]
        hy = h * self.dy[py : py + 1]
        hyy = hy * self.dy[py : py + 1]
        if py == 0:
            self.m0, self.m1, self.m2 = h, hy, hyy
        else:
            self.m0, self.m1, self.m2 = self.m0 + h, self.m1 + hy, self.m2 + hyy

    def close(self):
        def total(x):
            return jnp.sum(x, axis=0, keepdims=True)

        m0x = self.m0 * self.dx
        s0, sx, sy = total(self.m0), total(m0x), total(self.m1)
        sxx, sxy, syy = total(m0x * self.dx), total(self.m1 * self.dx), total(self.m2)
        shared = -0.5 * self.conic_b * sxy
        geometry = (
            self.conic_a * sx + self.conic_b * sy,
            self.conic_b * sx + self.conic_c * sy,
            shared - 0.5 * self.conic_a * sxx,
            -0.9 * (1.0 - self.skew * self.skew) * self.middle * sxy,
            shared - 0.5 * self.conic_c * syy,
            (1.0 - self.opaque) * s0,
        )
        grad = self.turned[...]
        channel = iota(grad.shape, 0)
        for k, value in enumerate(geometry):
            grad = jnp.where(channel == k, value, grad)
        at = pl.multiple_of(self.t * self.length, self.length)
        self.grads[pl.ds(at, self.length), 0:WIRE] = grad.T


def paint(slot_ref, cot_ref, images_ref, table, grads, rows, earlier, later, scratch, between):
    tiles = cot_ref.shape[0]
    length = rows[0].shape[0]
    blocks = length // BLOCK
    half = length // 2
    above = iota((2 * half, half), 0) % half
    beside = iota((2 * half, half), 1)
    earlier[...] = (above < beside).astype(F32).astype(BF16)
    later[...] = (above > beside).astype(F32).astype(BF16)

    def pick(into, t, start, count):
        for u in range(start, start + count, 8):
            picked = [table[pl.ds(slot_ref[t * blocks + u // BLOCK, (u + v) % BLOCK], 1), :] for v in range(8)]
            into[u : u + 8, :] = jnp.concatenate(picked, axis=0)

    pick(rows[0], 0, 0, length)
    pick(rows[1], 1, 0, length)

    def two(i, _):
        for share, read, step in between:

            @pl.when(i == int(tiles * share) // 2)
            def _(read=read, step=step):
                step()
                if read:

                    def again(j, _):
                        at = pl.multiple_of(j * BLOCK, BLOCK)
                        for k in range(2):
                            for u in range(0, BLOCK, 8):
                                picked = [
                                    table[pl.ds(slot_ref[(2 * i + k) * blocks + j, u + v], 1), :] for v in range(8)
                                ]
                                rows[k][pl.ds(at + u, 8), :] = jnp.concatenate(picked, axis=0)
                        return 0

                    lax.fori_loop(0, blocks, again, 0)

        a, b = (
            Tile(2 * i + k, cot_ref, images_ref, grads, rows[k], earlier, later, scratch[k]) for k in range(2)
        )
        following = [jnp.minimum(2 * i + 2 + k, tiles - 1) for k in range(2)]
        todo = [(k, start) for start in range(0, length, PICKS) for k in range(2)]

        def more():
            if todo:
                k, start = todo.pop(0)
                pick(rows[k], following[k], start, PICKS)

        def sweep(step):
            for py in range(TILE_SIDE):
                step(py)
                more()

        a.turn()
        b.turn()
        a.shape()
        sweep(a.alphas)
        a.prefix()
        b.shape()
        sweep(b.alphas)
        b.prefix()
        sweep(a.weights)
        a.products()
        sweep(b.weights)
        b.products()
        sweep(a.terms)
        a.suffix()
        sweep(b.terms)
        b.suffix()
        sweep(a.moments)
        a.close()
        sweep(b.moments)
        b.close()
        while todo:
            more()
        return 0

    lax.fori_loop(0, tiles // 2, two, 0)


def paint_scratch(length):
    full = (PIXELS, length)
    one = [
        VMEM((WIRE, length), F32),
        VMEM(full, F32),
        VMEM(full, F32),
        VMEM((PIXELS, 2 * length), BF16),
        VMEM(full, F32),
        VMEM(full, F32),
        VMEM(full, BF16),
        VMEM(full, BF16),
        VMEM(full, F32),
    ]
    return [VMEM((length, 128), F32)] * 2 + [VMEM((length, length // 2), BF16)] * 2 + one + one


def render_kernel(
    slot_ref, entry_ref, ask_ref, used_ref, rows_ref, cot_ref,
    images_ref, back_ref, named_ref, cos_ref, clash_ref, void_ref,
    held, table, asked_ref, asked, ask_send, ask_recv, own_sem, even, odd, send, got,
    send_sem, recv_sem, back_send, back_recv, kept_sem, here, there, void_sem, grads, *scratch,
):
    width, columns = held.shape
    shards = send.shape[0]
    blocks = send.shape[1]
    me = lax.axis_index("gauss")
    load = pltpu.make_async_copy(rows_ref, held, own_sem)
    load.start()
    greet()

    partner = Partners()

    def copy(to, by):
        return remote(ask_ref.at[to], asked_ref.at[by], ask_send.at[to], ask_recv.at[by], to)

    def ask(k, _):
        copy(partner(k), me).start()
        return 0

    lax.fori_loop(1, shards, ask, 0)
    load.wait()

    def turn(i, _):
        at = pl.multiple_of(i * 512, 512)
        table[pl.ds(at, 512), 0:width] = held[:, pl.ds(at, 512)].T
        return 0

    lax.fori_loop(0, columns // 512, turn, 0)
    asked_ref[me] = ask_ref[me]

    def end(k, _):
        by = partner.any(k)
        copy(me, by).wait_recv()
        copy(by, me).wait_send()
        return 0

    lax.fori_loop(1, shards, end, 0)
    for c in range(blocks):
        named_ref[:, c, :] = asked_ref[:, c, :]
    down = pltpu.make_async_copy(named_ref, asked, own_sem)
    down.start()
    void = jnp.zeros((1, 1), F32)
    for c in range(blocks):
        row = asked_ref[:, c, :]
        view = asked_ref[:, blocks + c, :]
        cos = jnp.zeros(view.shape, F32)
        for v, value in enumerate(view_cosines()):
            cos = jnp.where(view == v, value, cos)
        cos_ref[:, c, :] = cos
        void = jnp.maximum(void, jnp.max((view == VIEWS).astype(F32), axis=(0, 1), keepdims=True))
        lane = iota(row.shape, 1) % GROUP
        same = jnp.zeros(row.shape, F32)
        for d in range(1, GROUP):
            same = jnp.where((pltpu.roll(row, d, 1) == row) & (lane >= d), 1.0, same)
        clash_ref[:, c : c + 1] = jnp.max(same, axis=1, keepdims=True).astype(I32)
    here[...] = jnp.broadcast_to(void, here.shape)
    beside = 1 - lax.axis_index("view")
    tell = pltpu.make_async_remote_copy(
        src_ref=here,
        dst_ref=there,
        send_sem=void_sem.at[0],
        recv_sem=void_sem.at[1],
        device_id={"view": beside},
        device_id_type=pl.DeviceIdType.MESH,
    )
    tell.start()
    down.wait()

    def blend(rows, to, c):
        turned = rows[...].T
        second = jnp.concatenate([jnp.zeros((GEOM, BLOCK), F32), turned[SENT : SENT + CHANNELS]], axis=0)
        send[to, c] = turned[0:SENT] + cos_ref[to, c : c + 1, :] * second

    def unpack(source, by, part):
        for c in range(part * READ, (part + 1) * READ):
            at = pl.multiple_of((by * blocks + c) * BLOCK, BLOCK)
            table[pl.ds(at, BLOCK), 0:SENT] = source[by, c].T

    out = Exchange(asked, blend, table, even, odd, send, got, send_sem, recv_sem, READ)

    def take(part):
        out.wait(part, lambda by: unpack(got, by, part))
        unpack(send, me, part)

    def mask(rows, to, c):
        used = used_ref[to, c : c + 1, :] > 0
        send[to, c] = jnp.where(used, rows[...].T[0:SENT], 0.0)

    back = Exchange(entry_ref, mask, grads, even, odd, send, back_ref, back_send, back_recv, 1, kept_sem.at[0])
    parts = blocks // READ
    for part in range(parts):
        out.start(part)
    take(0)

    def first():
        back.start(0)
        for part in range(1, parts):
            take(part)

    between = [(LEAVE[0], True, first)]
    for n in range(1, blocks - 1):
        between.append((LEAVE[n], False, functools.partial(back.start, n)))
    tiles = scratch[4:13], scratch[13:22]
    paint(slot_ref, cot_ref, images_ref, table, grads, scratch[0:2], scratch[2], scratch[3], tiles, between)
    back.start(blocks - 1)
    back.wait()
    tell.wait()
    void_ref[...] = jnp.maximum(here[...], there[...]).astype(I32)


def render(slot, entry, used, ask, gauss_rows, cot):
    shards = ask.shape[0]
    blocks = ask.shape[1] // 2
    width, columns = gauss_rows.shape
    tiles = cot.shape[0]
    length = slot.size // tiles
    wire = (shards, blocks, SENT, BLOCK)
    sems = pltpu.SemaphoreType.DMA((shards,))
    some = pltpu.SemaphoreType.DMA((blocks // READ, shards))
    return pl.pallas_call(
        render_kernel,
        out_shape=(
            jax.ShapeDtypeStruct((tiles, CHANNELS, PIXELS), F32),
            jax.ShapeDtypeStruct(wire, F32),
            jax.ShapeDtypeStruct(entry.shape, I32),
            jax.ShapeDtypeStruct(entry.shape, F32),
            jax.ShapeDtypeStruct((shards, 128), I32),
            jax.ShapeDtypeStruct((8, 128), I32),
        ),
        in_specs=[whole(SMEM), whole(SMEM), whole(VMEM), whole(VMEM), whole(pl.ANY), whole(VMEM)],
        out_specs=(whole(VMEM), whole(pl.ANY), whole(VMEM), whole(VMEM), whole(VMEM), whole(VMEM)),
        scratch_shapes=[
            VMEM((width, columns), F32),
            VMEM((columns, 128), F32),
            VMEM(ask.shape, I32),
            SMEM(entry.shape, I32),
            sems,
            sems,
            pltpu.SemaphoreType.DMA,
            VMEM((BLOCK, 128), F32),
            VMEM((BLOCK, 128), F32),
            VMEM(wire, F32),
            VMEM(wire, F32),
            some,
            some,
            sems,
            sems,
            pltpu.SemaphoreType.DMA((1,)),
            VMEM((8, 128), F32),
            VMEM((8, 128), F32),
            pltpu.SemaphoreType.DMA((2,)),
            VMEM((tiles * length, 128), F32),
        ]
        + paint_scratch(length),
        compiler_params=params(collective_id=0, has_side_effects=True),
        name="render",
    )(slot, entry, ask, used, gauss_rows, cot)


def collect_kernel(
    half_ref, ask_ref, clash_ref, cos_ref, wire_ref, keep_ref, send_ref, table, table2, even, odd, wide, sems
):
    step_id = pl.program_id(0)
    sources = wire_ref.shape[0]
    width, half = keep_ref.shape
    blocks = wire_ref.shape[1]
    step = 512

    @pl.when(step_id == 0)
    def _():
        table[...] = jnp.zeros_like(table)
        table2[...] = jnp.zeros_like(table2)
        even[...] = jnp.zeros_like(even)
        odd[...] = jnp.zeros_like(odd)

    def turn(s, c, rows):
        back = wire_ref[s, c]
        scaled = cos_ref[s, c : c + 1, :] * back
        rows[:, 0:width] = jnp.concatenate([back, scaled[GEOM:SENT]], axis=0).T

    def add(at, c, rows):
        for g in range(BLOCK // GROUP):
            into = (table, table2)[g % 2]
            places = [ask_ref[at, c, g * GROUP + u] for u in range(GROUP)]
            sums = [into[pl.ds(r, 1), :] + rows[g * GROUP + u : g * GROUP + u + 1, :] for u, r in enumerate(places)]
            for r, value in zip(places, sums):
                into[pl.ds(r, 1), :] = value

    def add_slowly(at, c, rows):
        for u in range(BLOCK):
            into = (table, table2)[u % 2]
            into[pl.ds(ask_ref[at, c, u], 1), :] += rows[u : u + 1, :]

    def finish(at, c, rows, more):
        def quick():
            more()
            add(at, c, rows)

        def careful():
            more()
            add_slowly(at, c, rows)

        lax.cond(clash_ref[at, c] == 0, quick, careful)

    def one(s, _):
        source = step_id * sources + s
        for c in range(blocks):
            now, past = (even, odd) if c % 2 == 0 else (odd, even)
            at = source if c else jnp.maximum(source - 1, 0)
            finish(at, (c - 1) % blocks, past, functools.partial(turn, s, c, now))
        return 0

    lax.fori_loop(0, sources, one, 0)

    @pl.when(step_id == pl.num_programs(0) - 1)
    def _():
        finish(pl.num_programs(0) * sources - 1, blocks - 1, odd, lambda: None)
        copies = []
        for ref, base in ((send_ref, half - half_ref[0]), (keep_ref, half_ref[0])):
            for part in range(COPIES):
                length = half // COPIES
                held = wide.at[len(copies)]

                def back(i, _):
                    at = pl.multiple_of(i * step, step)
                    there = pl.multiple_of(base + part * length + at, step)
                    both = table[pl.ds(there, step), :] + table2[pl.ds(there, step), :]
                    held[:, pl.ds(at, step)] = both.T[0:width]
                    return 0

                lax.fori_loop(0, length // step, back, 0)
                into = ref.at[:, pl.ds(part * length, length)]
                copies.append(pltpu.make_async_copy(held, into, sems.at[len(copies)]))
                copies[-1].start()
        for copy in copies:
            copy.wait()


def collect(half, asked, clash, cos, wire, width, columns):
    shards = wire.shape[0]
    part = jax.ShapeDtypeStruct((width, columns // 2), F32)
    return pl.pallas_call(
        collect_kernel,
        grid=(shards // SOURCES,),
        out_shape=(part, part),
        in_specs=[
            whole(SMEM),
            whole(SMEM),
            whole(SMEM),
            pl.BlockSpec((SOURCES,) + cos.shape[1:], lambda i: (i, 0, 0)),
            pl.BlockSpec((SOURCES,) + wire.shape[1:], lambda i: (i, 0, 0, 0)),
        ],
        out_specs=(whole(pl.ANY), whole(pl.ANY)),
        scratch_shapes=[
            VMEM((columns, 128), F32),
            VMEM((columns, 128), F32),
            VMEM((BLOCK, 128), F32),
            VMEM((BLOCK, 128), F32),
            VMEM((2 * COPIES, width, columns // 2 // COPIES), F32),
            pltpu.SemaphoreType.DMA((2 * COPIES,)),
        ],
        compiler_params=params(),
        name="collect",
    )(half, asked, clash, cos, wire)


def plain_composite(entry_params, view_cos, cotangent):
    pixel = jnp.arange(PIXELS)
    across = (pixel % TILE_SIDE).astype(jnp.float32) + 0.5
    down = (pixel // TILE_SIDE).astype(jnp.float32) + 0.5

    def render(params):
        off_x = across[None, :] - params[:, 0][:, None]
        off_y = down[None, :] - params[:, 1][:, None]
        conic_a = jnp.exp(params[:, 2])
        conic_c = jnp.exp(params[:, 4])
        conic_b = 0.9 * jnp.tanh(params[:, 3]) * jnp.sqrt(conic_a * conic_c)
        power = -0.5 * (
            conic_a[:, None] * off_x * off_x
            + 2.0 * conic_b[:, None] * off_x * off_y
            + conic_c[:, None] * off_y * off_y
        )
        alpha = 0.99 * jax.nn.sigmoid(params[:, 5])[:, None] * jnp.exp(power)
        logs = jnp.log(1.0 - alpha)
        before = jnp.cumsum(logs, axis=0) - logs
        weight = jnp.exp(before) * alpha
        colour = params[:, 6 : 6 + CHANNELS] + view_cos * params[:, 6 + CHANNELS : 6 + 2 * CHANNELS]
        return lax.dot_general(
            colour, weight, (((0,), (0,)), ((), ())), precision=lax.Precision.HIGHEST
        )

    image, pull = jax.vjp(render, entry_params)
    grads = pull(cotangent)
    return (image, grads[0])


def plain(gauss_rows, vis_shard, vis_row, tile_index, cotangent):
    shards = lax.axis_size("gauss")
    tiles, length = vis_row.shape
    entries = tiles * length
    capacity = 2 * entries // shards
    width = gauss_rows.shape[0]
    own_cols = gauss_rows.shape[1]
    shard_of = vis_shard.reshape(entries)
    row_of = vis_row.reshape(entries)
    hits = (shard_of[:, None] == jnp.arange(shards, dtype=jnp.int32)[None, :]).astype(jnp.int32)
    place = jnp.sum((jnp.cumsum(hits, axis=0) - 1) * hits, axis=1)
    slot_of = shard_of * capacity + place
    requests = (
        jnp.zeros((shards * capacity,), jnp.int32).at[slot_of].set(row_of).reshape(shards, capacity)
    )
    row_major = jnp.transpose(gauss_rows)
    asked = lax.all_to_all(requests, "gauss", split_axis=0, concat_axis=0, tiled=True)
    fetched = jnp.take(row_major, asked.reshape(-1), axis=0).reshape(
        asked.shape[0], asked.shape[1], width
    )
    sent = lax.all_to_all(fetched, "gauss", split_axis=0, concat_axis=0, tiled=True)
    entry_rows = jnp.take(sent.reshape(shards * capacity, width), slot_of, axis=0)
    tile_rows = entry_rows.reshape(tiles, length, width)
    view_cos = jnp.cos(TWO_PI * (tile_index // SCREEN_TILES).astype(jnp.float32) / VIEWS)

    def one_tile(packed):
        return plain_composite(packed[0], packed[1], packed[2])

    images, grads = lax.map(one_tile, (tile_rows, view_cos, cotangent), batch_size=4)
    entry_grads = grads.reshape(entries, width)
    outgoing = (
        jnp.zeros((shards * capacity, width), jnp.float32)
        .at[slot_of]
        .set(entry_grads)
        .reshape(shards, capacity, width)
    )
    returned = lax.all_to_all(outgoing, "gauss", split_axis=0, concat_axis=0, tiled=True)
    row_totals = (
        jnp.zeros((own_cols, width), jnp.float32)
        .at[asked.reshape(-1)]
        .add(returned.reshape(shards * capacity, width))
    )
    totals = jnp.transpose(row_totals)
    half = own_cols // 2
    summed = lax.psum(totals, "view")
    gradient = lax.dynamic_slice_in_dim(summed, lax.axis_index("view") * half, half, 1)
    return (images, gradient)


def per_device(gauss_rows, vis_shard, vis_row, tile_index, cotangent):
    shards = lax.axis_size("gauss")
    width, columns = gauss_rows.shape
    ask, entry, used, slot = route(tile_index, vis_shard.reshape(-1, BLOCK), vis_row, shards)
    images, returned, named, cos, clash, void = render(slot, entry, used, ask, gauss_rows, cotangent)

    def quick():
        half = (lax.axis_index("view") * (columns // 2)).astype(I32).reshape(1)
        keep, send = collect(half, named, clash, cos, returned, width, columns)
        other = lax.ppermute(send, "view", [(0, 1), (1, 0)])
        return (images, keep + other)

    def careful():
        return plain(gauss_rows, vis_shard, vis_row, tile_index, cotangent)

    return lax.cond(void[0, 0] == 0, quick, careful)


def solution(mesh):
    placed = (
        P(None, "gauss"),
        P(("gauss", "view"), None, None),
        P(("gauss", "view"), None),
        P(("gauss", "view")),
        P(("gauss", "view"), None, None),
    )
    return jax.shard_map(
        per_device,
        mesh=mesh,
        in_specs=placed,
        out_specs=(P(("gauss", "view"), None, None), P(None, ("gauss", "view"))),
        check_vma=False,
    )
```

```python
import functools
import math

import jax
import jax.numpy as jnp
from jax import lax
from jax.experimental import pallas as pl
from jax.experimental.pallas import tpu as pltpu
from jax.sharding import PartitionSpec as P

CHANNELS = 29
TILE_SIDE = 16
PIXELS = 256
VIEWS = 8
SCREEN_TILES = 8160
GEOM = 6
SENT = 35
WIRE = 40
TWO_PI = 6.283185307179586
LOG2E = 1.4426950408889634
VMEM = pltpu.VMEM
SMEM = pltpu.SMEM
F32 = jnp.float32
BF16 = jnp.bfloat16
I32 = jnp.int32
GROUP = 8
BLOCK = 128
LEAVE = (3 / 8, 5 / 8, 7 / 8)
READ = 2
SOURCES = 8
COPIES = 4
PICKS = 8


def params(**more):
    return pltpu.CompilerParams(vmem_limit_bytes=60 * 2**20, **more)


def whole(space):
    return pl.BlockSpec(memory_space=space)


def iota(shape, dim):
    return lax.broadcasted_iota(I32, shape, dim)


def dot(a, b, contract=((1,), (0,))):
    return lax.dot_general(a, b, (contract, ((), ())), preferred_element_type=F32)


def view_cosines():
    return [math.cos(TWO_PI * v / VIEWS) for v in range(VIEWS)]


def split(x):
    high = x.astype(BF16).astype(F32)
    return high, x - high


def route_kernel(tile_ref, shard_ref, row_ref, ask_ref, entry_ref, used_ref, slot_ref, carry_ref, early_ref):
    shards = ask_ref.shape[0]
    tiles, length = row_ref.shape
    tile_blocks = length // BLOCK
    width = 256
    parts = length // width
    capacity = 2 * tiles * length // shards
    blocks = capacity // BLOCK
    leave = [int(tiles * share) // 2 for share in LEAVE]
    before = (iota((width, width), 0) < iota((width, width), 1)).astype(F32).astype(BF16)
    lane = iota((1, width), 1).astype(F32)

    def some(i, state):
        total = state
        carry = carry_ref[...]
        early_ref[...] = jnp.maximum(early_ref[...], carry * jnp.where(i == leave[0], 1.0, 0.0))
        least = sum(jnp.where(i == pair, float((n + 1) * BLOCK), 0.0) for n, pair in enumerate(leave))
        carry = jnp.maximum(carry, least)
        spots = [(2 * i + u // parts, u % parts) for u in range(2 * parts)]
        shard = [
            jnp.concatenate(
                [shard_ref[pl.ds(t * tile_blocks + h * (width // BLOCK) + b, 1), :] for b in range(width // BLOCK)],
                axis=1,
            )
            for t, h in spots
        ]
        hot = [(iota((shards, width), 0) == one).astype(F32) for one in shard]
        seen = dot(jnp.concatenate(hot, axis=0).astype(BF16), before)
        at, values = [], []
        for u, (t, h) in enumerate(spots):
            place = jnp.sum(hot[u] * (seen[shards * u : shards * (u + 1)] + carry), axis=0, keepdims=True)
            carry = carry + jnp.broadcast_to(jnp.sum(hot[u], axis=1, keepdims=True), hot[u].shape)
            place = place.astype(I32)
            slot = shard[u] * capacity + jnp.minimum(place, capacity - 1)
            for b in range(width // BLOCK):
                slot_ref[pl.ds(t * tile_blocks + h * (width // BLOCK) + b, 1), :] = slot[
                    :, b * BLOCK : (b + 1) * BLOCK
                ]
            at.append((iota((capacity, width), 0) == place).astype(F32).astype(BF16))
            row = row_ref[pl.ds(t, 1), h * width : (h + 1) * width]
            parts_of = (
                (row & 255).astype(F32),
                (row >> 8).astype(F32),
                sum(
                    (jnp.full((1, width), tile_ref[t], I32) >= SCREEN_TILES * v).astype(F32) for v in range(VIEWS)
                ),
                lane,
                jnp.full((1, width), t * parts + h, I32).astype(F32),
            )
            values.append(jnp.concatenate([hot[u] * part for part in parts_of], axis=0).astype(BF16))
        at = jnp.concatenate(at, axis=1)
        values = jnp.concatenate(values, axis=1)
        carry_ref[...] = carry
        return total + dot(values, at, ((1,), (1,)))

    carry_ref[...] = jnp.zeros_like(carry_ref)
    early_ref[...] = jnp.zeros_like(early_ref)
    total = lax.fori_loop(0, tiles // 2, some, jnp.zeros((5 * shards, capacity), F32))
    over = (early_ref[...] > float(READ * BLOCK)) | (carry_ref[...] > float(capacity))
    over = jnp.max(over.astype(F32), axis=(0, 1), keepdims=True)
    low, high, view, lane, chunk = (total[shards * k : shards * (k + 1)].astype(I32) for k in range(5))
    used = view > 0
    row = jnp.where(used, low + 256 * high, iota((shards, capacity), 1))
    view = jnp.where(over > 0.0, VIEWS, jnp.where(used, view - 1, 0))
    entry = lane + width * chunk
    used = used.astype(I32)
    for c in range(blocks):
        lanes = slice(c * BLOCK, (c + 1) * BLOCK)
        ask_ref[:, c, :] = row[:, lanes]
        ask_ref[:, blocks + c, :] = view[:, lanes]
        entry_ref[:, c, :] = entry[:, lanes]
        used_ref[:, c, :] = used[:, lanes]


def route(tile, shard, row, shards):
    tiles, length = row.shape
    blocks = 2 * tiles * length // shards // BLOCK
    lists = jax.ShapeDtypeStruct((shards, blocks, BLOCK), I32)
    return pl.pallas_call(
        route_kernel,
        out_shape=(
            jax.ShapeDtypeStruct((shards, 2 * blocks, BLOCK), I32),
            lists,
            lists,
            jax.ShapeDtypeStruct((tiles * length // BLOCK, BLOCK), I32),
        ),
        in_specs=[whole(SMEM), whole(VMEM), whole(VMEM)],
        out_specs=(whole(VMEM),) * 4,
        scratch_shapes=[VMEM((shards, 256), F32)] * 2,
        compiler_params=params(),
        name="route",
    )(tile, shard, row)


class Partners:
    def __init__(self):
        self.shards = lax.axis_size("gauss")
        self.side = round(self.shards ** (1 / 3))
        self.me = lax.axis_index("gauss")
        self.units = (self.side * self.side, self.side, 1)
        self.here = [lax.rem(lax.div(self.me, jnp.int32(unit)), self.side) + self.side for unit in self.units]
        self.sign = 1 - 2 * lax.axis_index("view")

    def __call__(self, k):
        step = lax.rem(37 * k, self.shards)
        to = 0
        for unit, here in zip(self.units, self.here):
            by = lax.div(step, jnp.int32(unit)) if unit > 1 else step
            by = lax.rem(by, self.side) if unit < self.side * self.side else by
            to = to + lax.rem(here + self.sign * by, self.side) * unit
        return to

    def any(self, k):
        return lax.rem(self.me + k, self.shards)


def remote(src, dst, send_sem, recv_sem, to):
    return pltpu.make_async_remote_copy(
        src_ref=src,
        dst_ref=dst,
        send_sem=send_sem,
        recv_sem=recv_sem,
        device_id={"gauss": to},
        device_id_type=pl.DeviceIdType.MESH,
    )


class Exchange:
    def __init__(self, ask_ref, finish, table, even, odd, send, to_ref, send_sem, recv_sem, blocks, own=None):
        self.ask_ref, self.finish, self.table, self.buffers = ask_ref, finish, table, (even, odd)
        self.send, self.to_ref, self.send_sem, self.recv_sem, self.own = send, to_ref, send_sem, recv_sem, own
        self.blocks = blocks
        self.partner = Partners()
        self.shards, self.me = self.partner.shards, self.partner.me

    def piece(self, ref, shard, part):
        return ref.at[shard] if part is None else ref.at[shard, pl.ds(part * self.blocks, self.blocks)]

    def copy(self, part, to, by):
        send_sem, recv_sem = self.send_sem, self.recv_sem
        if self.own is None:
            send_sem, recv_sem = send_sem.at[part], recv_sem.at[part]
        return remote(
            self.piece(self.send, to, part), self.piece(self.to_ref, by, part), send_sem.at[to], recv_sem.at[by], to
        )

    def kept(self, part):
        return pltpu.make_async_copy(
            self.piece(self.send, self.me, part), self.piece(self.to_ref, self.me, part), self.own
        )

    def gather(self, to, block, into):
        for u in range(0, BLOCK, 8):
            picked = [self.table[pl.ds(self.ask_ref[to, block, u + v], 1), :] for v in range(8)]
            into[u : u + 8, :] = jnp.concatenate(picked, axis=0)

    def start(self, part):
        blocks, base, me = self.blocks, part * self.blocks, self.me
        even, odd = self.buffers
        first = self.partner(1)
        self.gather(me, base, even)
        if blocks == 1:
            self.gather(first, base, odd)
            self.finish(even, me, base)
        else:
            self.gather(me, base + 1, odd)
            self.finish(even, me, base)
            self.gather(first, base, even)
            self.finish(odd, me, base + 1)
            self.gather(first, base + 1, odd)
            self.finish(even, first, base)
        if self.own is not None:
            self.kept(part).start()

        def some(i, last):
            for n in range(2):
                k, c = (2 * i + n + 2, 0) if blocks == 1 else (i + 2, n)
                to = self.partner(k) if c == 0 else to
                now, past = self.buffers[n], self.buffers[1 - n]
                self.finish(past, *((to, base + c - 1) if c else (last, base + blocks - 1)))
                self.gather(to, base + c, now)
                if c == 0:
                    self.copy(part, last, me).start()
                if c == blocks - 1:
                    last = to
            return last

        last = lax.fori_loop(0, (self.shards - 2) * blocks // 2, some, first)
        self.finish(odd, last, base + blocks - 1)
        self.copy(part, last, me).start()

    def wait(self, part=None, arrived=None):
        def end(k, _):
            by = self.partner.any(k)
            self.copy(part, self.me, by).wait_recv()
            if arrived is not None:
                arrived(by)
            self.copy(part, by, self.me).wait_send()
            return 0

        lax.fori_loop(1, self.shards, end, 0)
        if self.own is not None:
            self.kept(part).wait()


def greet():
    shards = lax.axis_size("gauss")
    me = lax.axis_index("gauss")
    barrier = pltpu.get_barrier_semaphore()

    def hail(k, _):
        pl.semaphore_signal(
            barrier, inc=1, device_id={"gauss": lax.rem(me + k, shards)}, device_id_type=pl.DeviceIdType.MESH
        )
        return 0

    lax.fori_loop(1, shards, hail, 0)
    beside = 1 - lax.axis_index("view")
    pl.semaphore_signal(barrier, inc=1, device_id={"view": beside}, device_id_type=pl.DeviceIdType.MESH)
    pl.semaphore_wait(barrier, shards)


class Tile:
    def __init__(self, t, cot_ref, images_ref, grads, rows, earlier, later, scratch):
        self.t, self.cot_ref, self.images_ref, self.grads, self.rows = t, cot_ref, images_ref, grads, rows
        self.earlier, self.later = earlier, later
        self.turned, self.alpha, self.ratio, self.parts, self.sums, self.weight, self.high, self.low, self.pull = scratch
        self.length = rows.shape[0]
        self.half = self.length // 2

    def put(self, at, x):
        half = self.half
        high, low = split(x)
        high, low = high.astype(BF16), low.astype(BF16)
        self.parts[pl.ds(at, TILE_SIDE), 0:half] = high[:, 0:half]
        self.parts[pl.ds(at, TILE_SIDE), half : 2 * half] = low[:, 0:half]
        self.parts[pl.ds(at, TILE_SIDE), 2 * half : 3 * half] = high[:, half:]
        self.parts[pl.ds(at, TILE_SIDE), 3 * half : 4 * half] = low[:, half:]

    def turn(self):
        self.turned[...] = self.rows[...].T[0:WIRE]

    def shape(self):
        turned = self.turned
        self.x0, self.y0, r2, r3, r4, r5 = (turned[k : k + 1, :] for k in range(GEOM))
        self.conic_a = jnp.exp(r2)
        self.conic_c = jnp.exp(r4)
        self.skew = jnp.tanh(r3)
        self.middle = jnp.sqrt(self.conic_a * self.conic_c)
        self.conic_b = 0.9 * self.skew * self.middle
        self.opaque = 1.0 / (1.0 + jnp.exp(-r5))
        spot = iota((TILE_SIDE, self.length), 0).astype(F32) + 0.5
        self.dx = spot - self.x0
        self.dy = spot - self.y0
        scale = -0.5 * LOG2E
        self.part_x = (scale * self.conic_a) * self.dx * self.dx
        self.cross = (2.0 * scale * self.conic_b) * self.dx
        self.part_y = (scale * self.conic_c) * self.dy * self.dy + jnp.log2(0.99 * self.opaque)

    def alphas(self, py):
        at = py * TILE_SIDE
        a = jnp.exp2(self.part_x + (self.cross * self.dy[py : py + 1] + self.part_y[py : py + 1]))
        log = jnp.log2(1.0 - a)
        self.alpha[pl.ds(at, TILE_SIDE), :] = a
        self.ratio[pl.ds(at, TILE_SIDE), :] = a * jnp.exp2(-log)
        self.put(at, log)

    def prefix(self):
        half = self.half
        self.sums[:, 0:half] = dot(self.parts[:, 0 : 2 * half], self.earlier[...])
        self.sums[:, half:] = dot(self.parts[:, 2 * half :], self.earlier[...])

    def weights(self, py):
        at, half = py * TILE_SIDE, self.half
        b = self.sums[pl.ds(at, TILE_SIDE), :]
        last = (
            b[:, half - 1 : half]
            + self.parts[pl.ds(at, TILE_SIDE), half - 1 : half].astype(F32)
            + self.parts[pl.ds(at, TILE_SIDE), 2 * half - 1 : 2 * half].astype(F32)
        )
        b = jnp.concatenate([b[:, 0:half], b[:, half:] + last], axis=1)
        w = jnp.exp2(b) * self.alpha[pl.ds(at, TILE_SIDE), :]
        high, low = split(w)
        self.weight[pl.ds(at, TILE_SIDE), :] = w
        self.high[pl.ds(at, TILE_SIDE), :] = high.astype(BF16)
        self.low[pl.ds(at, TILE_SIDE), :] = low.astype(BF16)

    def products(self):
        channel = iota((WIRE, self.length), 0)
        colour = jnp.where((channel >= GEOM) & (channel < SENT), self.turned[...], 0.0)
        colour_hi, colour_lo = split(colour)
        cot = jnp.concatenate(
            [jnp.zeros((GEOM, PIXELS), F32), self.cot_ref[self.t], jnp.zeros((WIRE - SENT, PIXELS), F32)], axis=0
        )
        cot_hi, cot_lo = split(cot)
        fill = jnp.zeros((128 - 3 * WIRE, self.length), F32)
        fill_cot = jnp.zeros((128 - 3 * WIRE, PIXELS), F32)
        three = jnp.concatenate([cot_hi, cot_lo, cot_hi, fill_cot], axis=0).T.astype(BF16)
        other = jnp.concatenate([colour_hi, colour_hi, colour_lo, fill], axis=0).astype(BF16)
        self.pull[...] = dot(three, other)
        both = jnp.concatenate([colour_hi, colour_lo], axis=0).astype(BF16)
        image = dot(both, self.high[...], ((1,), (1,)))
        image_lo = dot(both[0:48], self.low[...], ((1,), (1,)))
        image = image[0:WIRE] + image[WIRE:] + image_lo[0:WIRE]
        self.images_ref[self.t] = image[GEOM:SENT]
        both = jnp.concatenate([cot_hi, cot_lo], axis=0).astype(BF16)
        grad = dot(both, self.high[...])
        grad_lo = dot(both[0:48], self.low[...])
        self.turned[...] = grad[0:WIRE] + grad[WIRE:] + grad_lo[0:WIRE]

    def terms(self, py):
        at = py * TILE_SIDE
        q = self.pull[pl.ds(at, TILE_SIDE), :] * self.weight[pl.ds(at, TILE_SIDE), :]
        self.pull[pl.ds(at, TILE_SIDE), :] = q
        self.put(at, q)

    def suffix(self):
        half = self.half
        self.sums[:, 0:half] = dot(self.parts[:, 0 : 2 * half], self.later[...])
        self.sums[:, half:] = dot(self.parts[:, 2 * half :], self.later[...])

    def moments(self, py):
        at, half = py * TILE_SIDE, self.half
        s = self.sums[pl.ds(at, TILE_SIDE), :]
        q = self.pull[pl.ds(at, TILE_SIDE), :]
        first = s[:, half : half + 1] + q[:, half : half + 1]
        s = jnp.concatenate([s[:, 0:half] + first, s[:, half:]], axis=1)
        h = q - s * self.ratio[pl.ds(at, TILE_SIDE), :]
        hy = h * self.dy[py : py + 1]
        hyy = hy * self.dy[py : py + 1]
        if py == 0:
            self.m0, self.m1, self.m2 = h, hy, hyy
        else:
            self.m0, self.m1, self.m2 = self.m0 + h, self.m1 + hy, self.m2 + hyy

    def close(self):
        def total(x):
            return jnp.sum(x, axis=0, keepdims=True)

        m0x = self.m0 * self.dx
        s0, sx, sy = total(self.m0), total(m0x), total(self.m1)
        sxx, sxy, syy = total(m0x * self.dx), total(self.m1 * self.dx), total(self.m2)
        shared = -0.5 * self.conic_b * sxy
        geometry = (
            self.conic_a * sx + self.conic_b * sy,
            self.conic_b * sx + self.conic_c * sy,
            shared - 0.5 * self.conic_a * sxx,
            -0.9 * (1.0 - self.skew * self.skew) * self.middle * sxy,
            shared - 0.5 * self.conic_c * syy,
            (1.0 - self.opaque) * s0,
        )
        grad = self.turned[...]
        channel = iota(grad.shape, 0)
        for k, value in enumerate(geometry):
            grad = jnp.where(channel == k, value, grad)
        at = pl.multiple_of(self.t * self.length, self.length)
        self.grads[pl.ds(at, self.length), 0:WIRE] = grad.T


def paint(slot_ref, cot_ref, images_ref, table, grads, rows, earlier, later, scratch, between):
    tiles = cot_ref.shape[0]
    length = rows[0].shape[0]
    blocks = length // BLOCK
    half = length // 2
    above = iota((2 * half, half), 0) % half
    beside = iota((2 * half, half), 1)
    earlier[...] = (above < beside).astype(F32).astype(BF16)
    later[...] = (above > beside).astype(F32).astype(BF16)

    def pick(into, t, start, count):
        for u in range(start, start + count, 8):
            picked = [table[pl.ds(slot_ref[t * blocks + u // BLOCK, (u + v) % BLOCK], 1), :] for v in range(8)]
            into[u : u + 8, :] = jnp.concatenate(picked, axis=0)

    pick(rows[0], 0, 0, length)
    pick(rows[1], 1, 0, length)

    def two(i, _):
        for share, read, step in between:

            @pl.when(i == int(tiles * share) // 2)
            def _(read=read, step=step):
                step()
                if read:

                    def again(j, _):
                        at = pl.multiple_of(j * BLOCK, BLOCK)
                        for k in range(2):
                            for u in range(0, BLOCK, 8):
                                picked = [
                                    table[pl.ds(slot_ref[(2 * i + k) * blocks + j, u + v], 1), :] for v in range(8)
                                ]
                                rows[k][pl.ds(at + u, 8), :] = jnp.concatenate(picked, axis=0)
                        return 0

                    lax.fori_loop(0, blocks, again, 0)

        a, b = (
            Tile(2 * i + k, cot_ref, images_ref, grads, rows[k], earlier, later, scratch[k]) for k in range(2)
        )
        following = [jnp.minimum(2 * i + 2 + k, tiles - 1) for k in range(2)]
        todo = [(k, start) for start in range(0, length, PICKS) for k in range(2)]

        def more():
            if todo:
                k, start = todo.pop(0)
                pick(rows[k], following[k], start, PICKS)

        def sweep(step):
            for py in range(TILE_SIDE):
                step(py)
                more()

        a.turn()
        b.turn()
        a.shape()
        sweep(a.alphas)
        a.prefix()
        b.shape()
        sweep(b.alphas)
        b.prefix()
        sweep(a.weights)
        a.products()
        sweep(b.weights)
        b.products()
        sweep(a.terms)
        a.suffix()
        sweep(b.terms)
        b.suffix()
        sweep(a.moments)
        a.close()
        sweep(b.moments)
        b.close()
        while todo:
            more()
        return 0

    lax.fori_loop(0, tiles // 2, two, 0)


def paint_scratch(length):
    full = (PIXELS, length)
    one = [
        VMEM((WIRE, length), F32),
        VMEM(full, F32),
        VMEM(full, F32),
        VMEM((PIXELS, 2 * length), BF16),
        VMEM(full, F32),
        VMEM(full, F32),
        VMEM(full, BF16),
        VMEM(full, BF16),
        VMEM(full, F32),
    ]
    return [VMEM((length, 128), F32)] * 2 + [VMEM((length, length // 2), BF16)] * 2 + one + one


def render_kernel(
    slots_ref, entries_ref, ask_ref, used_ref, rows_ref, cots_ref,
    images_ref, back_ref, named_ref, cos_ref, clash_ref, void_ref,
    held, table, asked_ref, asked, ask_send, ask_recv, own_sem, even, odd, send, got,
    send_sem, recv_sem, back_send, back_recv, kept_sem, here, there, void_sem, slot_ref, entry_ref, cot_ref, late_sem, grads, *scratch,
):
    width, columns = held.shape
    shards = send.shape[0]
    blocks = send.shape[1]
    me = lax.axis_index("gauss")
    load = pltpu.make_async_copy(rows_ref, held, own_sem)
    load.start()
    late = [
        pltpu.make_async_copy(source, into, late_sem.at[n])
        for n, (source, into) in enumerate(((slots_ref, slot_ref), (entries_ref, entry_ref), (cots_ref, cot_ref)))
    ]
    for one in late:
        one.start()
    greet()

    partner = Partners()

    def copy(to, by):
        return remote(ask_ref.at[to], asked_ref.at[by], ask_send.at[to], ask_recv.at[by], to)

    def ask(k, _):
        copy(partner(k), me).start()
        return 0

    lax.fori_loop(1, shards, ask, 0)
    load.wait()

    def turn(i, _):
        at = pl.multiple_of(i * 512, 512)
        table[pl.ds(at, 512), 0:width] = held[:, pl.ds(at, 512)].T
        return 0

    lax.fori_loop(0, columns // 512, turn, 0)
    asked_ref[me] = ask_ref[me]

    def end(k, _):
        by = partner.any(k)
        copy(me, by).wait_recv()
        copy(by, me).wait_send()
        return 0

    lax.fori_loop(1, shards, end, 0)
    for c in range(blocks):
        named_ref[:, c, :] = asked_ref[:, c, :]
    down = pltpu.make_async_copy(named_ref, asked, own_sem)
    down.start()
    void = jnp.zeros((1, 1), F32)
    for c in range(blocks):
        row = asked_ref[:, c, :]
        view = asked_ref[:, blocks + c, :]
        cos = jnp.zeros(view.shape, F32)
        for v, value in enumerate(view_cosines()):
            cos = jnp.where(view == v, value, cos)
        cos_ref[:, c, :] = cos
        void = jnp.maximum(void, jnp.max((view == VIEWS).astype(F32), axis=(0, 1), keepdims=True))
        lane = iota(row.shape, 1) % GROUP
        same = jnp.zeros(row.shape, F32)
        for d in range(1, GROUP):
            same = jnp.where((pltpu.roll(row, d, 1) == row) & (lane >= d), 1.0, same)
        clash_ref[:, c : c + 1] = jnp.max(same, axis=1, keepdims=True).astype(I32)
    here[...] = jnp.broadcast_to(void, here.shape)
    beside = 1 - lax.axis_index("view")
    tell = pltpu.make_async_remote_copy(
        src_ref=here,
        dst_ref=there,
        send_sem=void_sem.at[0],
        recv_sem=void_sem.at[1],
        device_id={"view": beside},
        device_id_type=pl.DeviceIdType.MESH,
    )
    tell.start()
    down.wait()

    def blend(rows, to, c):
        turned = rows[...].T
        second = jnp.concatenate([jnp.zeros((GEOM, BLOCK), F32), turned[SENT : SENT + CHANNELS]], axis=0)
        send[to, c] = turned[0:SENT] + cos_ref[to, c : c + 1, :] * second

    def unpack(source, by, part):
        for c in range(part * READ, (part + 1) * READ):
            at = pl.multiple_of((by * blocks + c) * BLOCK, BLOCK)
            table[pl.ds(at, BLOCK), 0:SENT] = source[by, c].T

    out = Exchange(asked, blend, table, even, odd, send, got, send_sem, recv_sem, READ)

    def take(part):
        out.wait(part, lambda by: unpack(got, by, part))
        unpack(send, me, part)

    def mask(rows, to, c):
        used = used_ref[to, c : c + 1, :] > 0
        send[to, c] = jnp.where(used, rows[...].T[0:SENT], 0.0)

    back = Exchange(entry_ref, mask, grads, even, odd, send, back_ref, back_send, back_recv, 1, kept_sem.at[0])
    parts = blocks // READ
    for part in range(parts):
        out.start(part)
    take(0)
    for one in late:
        one.wait()

    def first():
        back.start(0)
        for part in range(1, parts):
            take(part)

    between = [(LEAVE[0], True, first)]
    for n in range(1, blocks - 1):
        between.append((LEAVE[n], False, functools.partial(back.start, n)))
    tiles = scratch[4:13], scratch[13:22]
    paint(slot_ref, cot_ref, images_ref, table, grads, scratch[0:2], scratch[2], scratch[3], tiles, between)
    back.start(blocks - 1)
    back.wait()
    tell.wait()
    void_ref[...] = jnp.maximum(here[...], there[...]).astype(I32)


def render(slot, entry, used, ask, gauss_rows, cot):
    shards = ask.shape[0]
    blocks = ask.shape[1] // 2
    width, columns = gauss_rows.shape
    tiles = cot.shape[0]
    length = slot.size // tiles
    wire = (shards, blocks, SENT, BLOCK)
    sems = pltpu.SemaphoreType.DMA((shards,))
    some = pltpu.SemaphoreType.DMA((blocks // READ, shards))
    return pl.pallas_call(
        render_kernel,
        out_shape=(
            jax.ShapeDtypeStruct((tiles, CHANNELS, PIXELS), F32),
            jax.ShapeDtypeStruct(wire, F32),
            jax.ShapeDtypeStruct(entry.shape, I32),
            jax.ShapeDtypeStruct(entry.shape, F32),
            jax.ShapeDtypeStruct((shards, 128), I32),
            jax.ShapeDtypeStruct((8, 128), I32),
        ),
        in_specs=[whole(pl.ANY), whole(pl.ANY), whole(VMEM), whole(VMEM), whole(pl.ANY), whole(pl.ANY)],
        out_specs=(whole(VMEM), whole(pl.ANY), whole(VMEM), whole(VMEM), whole(VMEM), whole(VMEM)),
        scratch_shapes=[
            VMEM((width, columns), F32),
            VMEM((columns, 128), F32),
            VMEM(ask.shape, I32),
            SMEM(entry.shape, I32),
            sems,
            sems,
            pltpu.SemaphoreType.DMA,
            VMEM((BLOCK, 128), F32),
            VMEM((BLOCK, 128), F32),
            VMEM(wire, F32),
            VMEM(wire, F32),
            some,
            some,
            sems,
            sems,
            pltpu.SemaphoreType.DMA((1,)),
            VMEM((8, 128), F32),
            VMEM((8, 128), F32),
            pltpu.SemaphoreType.DMA((2,)),
            SMEM(slot.shape, I32),
            SMEM(entry.shape, I32),
            VMEM(cot.shape, F32),
            pltpu.SemaphoreType.DMA((3,)),
            VMEM((tiles * length, 128), F32),
        ]
        + paint_scratch(length),
        compiler_params=params(collective_id=0, has_side_effects=True),
        name="render",
    )(slot, entry, ask, used, gauss_rows, cot)


def collect_kernel(
    half_ref, names_ref, clashes_ref, cos_ref, wire_ref, keep_ref, send_ref,
    table, table2, even, odd, wide, sems, ask_ref, clash_ref, load_sem,
):
    step_id = pl.program_id(0)
    sources = wire_ref.shape[0]
    width, half = keep_ref.shape
    blocks = wire_ref.shape[1]
    step = 512

    @pl.when(step_id == 0)
    def _():
        loads = [
            pltpu.make_async_copy(names_ref, ask_ref, load_sem.at[0]),
            pltpu.make_async_copy(clashes_ref, clash_ref, load_sem.at[1]),
        ]
        for load in loads:
            load.start()
        table[...] = jnp.zeros_like(table)
        table2[...] = jnp.zeros_like(table2)
        even[...] = jnp.zeros_like(even)
        odd[...] = jnp.zeros_like(odd)
        for load in loads:
            load.wait()

    def turn(s, c, rows):
        back = wire_ref[s, c]
        scaled = cos_ref[s, c : c + 1, :] * back
        rows[:, 0:width] = jnp.concatenate([back, scaled[GEOM:SENT]], axis=0).T

    def add(at, c, rows):
        for g in range(BLOCK // GROUP):
            into = (table, table2)[g % 2]
            places = [ask_ref[at, c, g * GROUP + u] for u in range(GROUP)]
            sums = [into[pl.ds(r, 1), :] + rows[g * GROUP + u : g * GROUP + u + 1, :] for u, r in enumerate(places)]
            for r, value in zip(places, sums):
                into[pl.ds(r, 1), :] = value

    def add_slowly(at, c, rows):
        for u in range(BLOCK):
            into = (table, table2)[u % 2]
            into[pl.ds(ask_ref[at, c, u], 1), :] += rows[u : u + 1, :]

    def finish(at, c, rows, more):
        def quick():
            more()
            add(at, c, rows)

        def careful():
            more()
            add_slowly(at, c, rows)

        lax.cond(clash_ref[at, c] == 0, quick, careful)

    def one(s, _):
        source = step_id * sources + s
        for c in range(blocks):
            now, past = (even, odd) if c % 2 == 0 else (odd, even)
            at = source if c else jnp.maximum(source - 1, 0)
            finish(at, (c - 1) % blocks, past, functools.partial(turn, s, c, now))
        return 0

    lax.fori_loop(0, sources, one, 0)

    @pl.when(step_id == pl.num_programs(0) - 1)
    def _():
        finish(pl.num_programs(0) * sources - 1, blocks - 1, odd, lambda: None)
        copies = []
        for ref, base in ((send_ref, half - half_ref[0]), (keep_ref, half_ref[0])):
            for part in range(COPIES):
                length = half // COPIES
                held = wide.at[len(copies)]

                def back(i, _):
                    at = pl.multiple_of(i * step, step)
                    there = pl.multiple_of(base + part * length + at, step)
                    both = table[pl.ds(there, step), :] + table2[pl.ds(there, step), :]
                    held[:, pl.ds(at, step)] = both.T[0:width]
                    return 0

                lax.fori_loop(0, length // step, back, 0)
                into = ref.at[:, pl.ds(part * length, length)]
                copies.append(pltpu.make_async_copy(held, into, sems.at[len(copies)]))
                copies[-1].start()
        for copy in copies:
            copy.wait()


def collect(half, asked, clash, cos, wire, width, columns):
    shards = wire.shape[0]
    part = jax.ShapeDtypeStruct((width, columns // 2), F32)
    return pl.pallas_call(
        collect_kernel,
        grid=(shards // SOURCES,),
        out_shape=(part, part),
        in_specs=[
            whole(SMEM),
            whole(pl.ANY),
            whole(pl.ANY),
            pl.BlockSpec((SOURCES,) + cos.shape[1:], lambda i: (i, 0, 0)),
            pl.BlockSpec((SOURCES,) + wire.shape[1:], lambda i: (i, 0, 0, 0)),
        ],
        out_specs=(whole(pl.ANY), whole(pl.ANY)),
        scratch_shapes=[
            VMEM((columns, 128), F32),
            VMEM((columns, 128), F32),
            VMEM((BLOCK, 128), F32),
            VMEM((BLOCK, 128), F32),
            VMEM((2 * COPIES, width, columns // 2 // COPIES), F32),
            pltpu.SemaphoreType.DMA((2 * COPIES,)),
            SMEM(asked.shape, I32),
            SMEM(clash.shape, I32),
            pltpu.SemaphoreType.DMA((2,)),
        ],
        compiler_params=params(),
        name="collect",
    )(half, asked, clash, cos, wire)


def plain_composite(entry_params, view_cos, cotangent):
    pixel = jnp.arange(PIXELS)
    across = (pixel % TILE_SIDE).astype(jnp.float32) + 0.5
    down = (pixel // TILE_SIDE).astype(jnp.float32) + 0.5

    def render(params):
        off_x = across[None, :] - params[:, 0][:, None]
        off_y = down[None, :] - params[:, 1][:, None]
        conic_a = jnp.exp(params[:, 2])
        conic_c = jnp.exp(params[:, 4])
        conic_b = 0.9 * jnp.tanh(params[:, 3]) * jnp.sqrt(conic_a * conic_c)
        power = -0.5 * (
            conic_a[:, None] * off_x * off_x
            + 2.0 * conic_b[:, None] * off_x * off_y
            + conic_c[:, None] * off_y * off_y
        )
        alpha = 0.99 * jax.nn.sigmoid(params[:, 5])[:, None] * jnp.exp(power)
        logs = jnp.log(1.0 - alpha)
        before = jnp.cumsum(logs, axis=0) - logs
        weight = jnp.exp(before) * alpha
        colour = params[:, 6 : 6 + CHANNELS] + view_cos * params[:, 6 + CHANNELS : 6 + 2 * CHANNELS]
        return lax.dot_general(
            colour, weight, (((0,), (0,)), ((), ())), precision=lax.Precision.HIGHEST
        )

    image, pull = jax.vjp(render, entry_params)
    grads = pull(cotangent)
    return (image, grads[0])


def plain(gauss_rows, vis_shard, vis_row, tile_index, cotangent):
    shards = lax.axis_size("gauss")
    tiles, length = vis_row.shape
    entries = tiles * length
    capacity = 2 * entries // shards
    width = gauss_rows.shape[0]
    own_cols = gauss_rows.shape[1]
    shard_of = vis_shard.reshape(entries)
    row_of = vis_row.reshape(entries)
    hits = (shard_of[:, None] == jnp.arange(shards, dtype=jnp.int32)[None, :]).astype(jnp.int32)
    place = jnp.sum((jnp.cumsum(hits, axis=0) - 1) * hits, axis=1)
    slot_of = shard_of * capacity + place
    requests = (
        jnp.zeros((shards * capacity,), jnp.int32).at[slot_of].set(row_of).reshape(shards, capacity)
    )
    row_major = jnp.transpose(gauss_rows)
    asked = lax.all_to_all(requests, "gauss", split_axis=0, concat_axis=0, tiled=True)
    fetched = jnp.take(row_major, asked.reshape(-1), axis=0).reshape(
        asked.shape[0], asked.shape[1], width
    )
    sent = lax.all_to_all(fetched, "gauss", split_axis=0, concat_axis=0, tiled=True)
    entry_rows = jnp.take(sent.reshape(shards * capacity, width), slot_of, axis=0)
    tile_rows = entry_rows.reshape(tiles, length, width)
    view_cos = jnp.cos(TWO_PI * (tile_index // SCREEN_TILES).astype(jnp.float32) / VIEWS)

    def one_tile(packed):
        return plain_composite(packed[0], packed[1], packed[2])

    images, grads = lax.map(one_tile, (tile_rows, view_cos, cotangent), batch_size=4)
    entry_grads = grads.reshape(entries, width)
    outgoing = (
        jnp.zeros((shards * capacity, width), jnp.float32)
        .at[slot_of]
        .set(entry_grads)
        .reshape(shards, capacity, width)
    )
    returned = lax.all_to_all(outgoing, "gauss", split_axis=0, concat_axis=0, tiled=True)
    row_totals = (
        jnp.zeros((own_cols, width), jnp.float32)
        .at[asked.reshape(-1)]
        .add(returned.reshape(shards * capacity, width))
    )
    totals = jnp.transpose(row_totals)
    half = own_cols // 2
    summed = lax.psum(totals, "view")
    gradient = lax.dynamic_slice_in_dim(summed, lax.axis_index("view") * half, half, 1)
    return (images, gradient)


def per_device(gauss_rows, vis_shard, vis_row, tile_index, cotangent):
    shards = lax.axis_size("gauss")
    width, columns = gauss_rows.shape
    ask, entry, used, slot = route(tile_index, vis_shard.reshape(-1, BLOCK), vis_row, shards)
    images, returned, named, cos, clash, void = render(slot, entry, used, ask, gauss_rows, cotangent)

    def quick():
        half = (lax.axis_index("view") * (columns // 2)).astype(I32).reshape(1)
        keep, send = collect(half, named, clash, cos, returned, width, columns)
        other = lax.ppermute(send, "view", [(0, 1), (1, 0)])
        return (images, keep + other)

    def careful():
        return plain(gauss_rows, vis_shard, vis_row, tile_index, cotangent)

    return lax.cond(void[0, 0] == 0, quick, careful)


def solution(mesh):
    placed = (
        P(None, "gauss"),
        P(("gauss", "view"), None, None),
        P(("gauss", "view"), None),
        P(("gauss", "view")),
        P(("gauss", "view"), None, None),
    )
    return jax.shard_map(
        per_device,
        mesh=mesh,
        in_specs=placed,
        out_specs=(P(("gauss", "view"), None, None), P(None, ("gauss", "view"))),
        check_vma=False,
    )
```
